32 devices in a mesh: dp: 8 (over z, x), head: 4 (over y, core).
Axes of the slice: x: 2, y: 2, z: 4, core: 2. Of those that a mesh axis runs over, the one named last changes fastest.
Arguments:
- tokens: bfloat16 [16, 1280, 768], P('dp', 'head'), may hold values from -6 to 6
- passes: int32 [16], P('dp'), may hold values from 2 to 5, as said below
- first_gain: float32 [768], replicated, may hold values from 0.1 to 1.9
- first_shift: float32 [768], replicated, may hold values from -1.75 to 1.75
- heads_weight: bfloat16 [768, 12, 192], replicated, may hold values from -0.21875 to 0.21875
- query_bias: float32 [768], replicated, may hold values from -1.75 to 1.75
- value_bias: float32 [768], replicated, may hold values from -1.75 to 1.75
- output_weight: bfloat16 [768, 768], replicated, may hold values from -0.875 to 0.875
- output_bias: float32 [768], replicated, may hold values from -1.75 to 1.75
- second_gain: float32 [768], replicated, may hold values from 0.1 to 1.9
- second_shift: float32 [768], replicated, may hold values from -1.75 to 1.75
- upward_weight: bfloat16 [768, 3072], replicated, may hold values from -0.21875 to 0.21875
- upward_bias: float32 [3072], replicated, may hold values from -1.75 to 1.75
- downward_weight: bfloat16 [3072, 768], replicated, may hold values from -0.109375 to 0.109375
- downward_bias: float32 [768], replicated, may hold values from -1.75 to 1.75
- pass_embed: float32 [5, 768], replicated, may hold values from -3 to 3
- cotangent: bfloat16 [16, 1280, 768], P('dp', 'head'), may hold values from -6 to 6
Outputs:
- layer_output: bfloat16 [16, 1280, 768], P('dp', 'head')
- tokens_grad: float32 [16, 1280, 768], P('dp', 'head')
- first_gain_grad: float32 [768], P('dp')
- first_shift_grad: float32 [768], P('dp')
- heads_weight_grad: float32 [768, 12, 192], P('dp')
- query_bias_grad: float32 [768], P('dp')
- value_bias_grad: float32 [768], P('dp')
- output_weight_grad: float32 [768, 768], P('dp')
- output_bias_grad: float32 [768], P('dp')
- second_gain_grad: float32 [768], P('dp')
- second_shift_grad: float32 [768], P('dp')
- upward_weight_grad: float32 [768, 3072], P('dp')
- upward_bias_grad: float32 [3072], P('dp')
- downward_weight_grad: float32 [3072, 768], P('dp')
- downward_bias_grad: float32 [768], P('dp')
- pass_embed_grad: float32 [5, 768], P(None, 'dp')
The draws below stay inside these ranges and needn't reach their ends.
Inputs may be any that keep to these rules, and one draw needn't show every extreme that they name: Among the 2 sequences of each index of dp, one has 5 passes.
All inputs are finite; a program needn't handle non-finite values.
Results may differ from the reference program's by a relative error of at most 0.0095.
Values may be sent and summed in bfloat16 or wider, within the bound.
A program may use at most 192 MiB of HBM per device.

```python
import jax
import jax.numpy as jnp
from jax import lax

D = 768
HEADS = 12
HEAD = 64
FF = 3072
BASE = 256
PASSES = 5
SEQ_GRP = 2
MAXLEN = 1280
SEQS = 16


def draw_passes(key, part):
    key = jax.random.fold_in(key, 11)
    count_key, pick_key = jax.random.split(key)
    counts = jax.random.randint(count_key, (SEQS,), 2, PASSES + 1)
    picks = jax.random.randint(pick_key, (SEQS // SEQ_GRP,), 0, SEQ_GRP)
    places = jnp.arange(SEQS, dtype=jnp.int32)
    chosen = places % SEQ_GRP == picks[places // SEQ_GRP]
    return jnp.where(chosen, PASSES, counts).astype(jnp.int32)


def shard_levels(own_key, shape, cuts, least, largest):
    def one(dim, blocks):
        draws = jax.random.uniform(jax.random.fold_in(jax.random.fold_in(own_key, 6), dim), (blocks,), jnp.float32, least / len(cuts), largest / len(cuts))
        return jnp.repeat(jnp.exp(draws), shape[dim] // blocks).reshape((-1,) + (1,) * (len(shape) - dim - 1))

    gain = one(*cuts[0])
    for cut in cuts[1:]:
        gain = gain * one(*cut)
    return gain


def bell_draw(key, shape, scale, limit, shards=(), held_as=jnp.bfloat16):
    values = jax.random.normal(key, shape, jnp.float32) * scale
    if len(shards) > 0:
        values = shard_levels(key, shape, shards, -0.22, 0.18) * values
    return jnp.clip(values, min=-limit, max=limit).astype(held_as)


def setup_inputs(seed: int = 0) -> dict:
    key_of = jax.random.split(jax.random.key(seed), 18)
    return {
        "tokens": bell_draw(key_of[0], (SEQS, MAXLEN, D), 1.0, 6.0, ((0, 8), (1, 4))),
        "passes": draw_passes(jax.random.fold_in(key_of[17], 71), 0),
        "first_gain": jnp.clip(1.0 + 0.18 * jax.random.normal(key_of[2], (D,), jnp.float32), 0.1, 1.9),
        "first_shift": bell_draw(key_of[3], (D,), 0.3, 1.75, (), jnp.float32),
        "heads_weight": bell_draw(key_of[4], (D, HEADS, 3 * HEAD), D ** -0.5, 0.21875),
        "query_bias": bell_draw(key_of[5], (D,), 0.3, 1.75, (), jnp.float32),
        "value_bias": bell_draw(key_of[6], (D,), 0.3, 1.75, (), jnp.float32),
        "output_weight": bell_draw(key_of[7], (D, D), (D // 16) ** -0.5, 0.875),
        "output_bias": bell_draw(key_of[8], (D,), 0.3, 1.75, (), jnp.float32),
        "second_gain": jnp.clip(1.0 + 0.18 * jax.random.normal(key_of[9], (D,), jnp.float32), 0.1, 1.9),
        "second_shift": bell_draw(key_of[10], (D,), 0.3, 1.75, (), jnp.float32),
        "upward_weight": bell_draw(key_of[11], (D, FF), D ** -0.5, 0.21875),
        "upward_bias": bell_draw(key_of[12], (FF,), 0.3, 1.75, (), jnp.float32),
        "downward_weight": bell_draw(key_of[13], (FF, D), FF ** -0.5, 0.109375),
        "downward_bias": bell_draw(key_of[14], (D,), 0.3, 1.75, (), jnp.float32),
        "pass_embed": bell_draw(key_of[15], (PASSES, D), 0.5, 3.0, (), jnp.float32),
        "cotangent": bell_draw(key_of[16], (SEQS, MAXLEN, D), 1.0, 6.0, ((0, 8), (1, 4))),
    }


NEG_FILL = -1e+30
EPSILON = 1e-05

@jax.custom_vjp
def low(v):
    return lax.optimization_barrier(v.astype(jnp.bfloat16)).astype(jnp.float32)

@jax.custom_vjp
def low_back(v):
    return v

def low_keep(v):
    return (low(v), None)

def low_pass(kept, grad):
    return (grad,)

def back_keep(v):
    return (v, None)

def back_low(kept, grad):
    return (low(grad),)
low.defvjp(low_keep, low_pass)
low_back.defvjp(back_keep, back_low)

def highest(left, right):
    return jnp.dot(left, right, precision=lax.Precision.HIGHEST)

def layer_norm(hidden, gain_vec, shift_vec):
    centre = hidden - lax.optimization_barrier(jnp.mean(hidden, axis=-1, keepdims=True))
    spread = lax.optimization_barrier(jnp.mean(centre * centre, axis=-1, keepdims=True))
    return centre * lax.rsqrt(spread + EPSILON) * gain_vec + shift_vec

def gelu_tanh(inner):
    return jax.nn.gelu(inner, approximate=True)

def sequence_forward(row_tokens, pass_count, params):
    first_gain, first_shift, heads_weight, query_bias, value_bias, output_weight, output_bias, second_gain, second_shift, upward_weight, upward_bias, downward_weight, downward_bias, pass_embed = params
    places = jnp.arange(MAXLEN, dtype=jnp.int32)
    length = pass_count * BASE
    section = places % pass_count
    valid = (places < length).astype(row_tokens.dtype)[:, None]
    table = jnp.zeros_like(row_tokens)
    for section_id in range(PASSES):
        table = table + jnp.where((section == section_id)[:, None], pass_embed[section_id][None, :], 0.0)
    embedded = row_tokens + table
    first_normed = low(layer_norm(embedded, first_gain, first_shift))
    packed = highest(first_normed, heads_weight.reshape(D, 3 * D)).reshape(MAXLEN, HEADS, 3 * HEAD)
    bias_table = jnp.concatenate([query_bias.reshape(HEADS, HEAD), jnp.zeros((HEADS, HEAD), query_bias.dtype), value_bias.reshape(HEADS, HEAD)], axis=1)
    packed = low_back(low(packed + bias_table))
    visible = (places[None, :] <= places[:, None]) & (places[None, :] < length)
    scale_factor = HEAD ** (-0.5)

    def one_head(block):
        queries = block[:, :HEAD]
        keys_in = block[:, HEAD:2 * HEAD]
        values_in = block[:, 2 * HEAD:]
        scores = low_back(highest(queries, keys_in.T) * scale_factor)
        scores = jnp.where(visible, scores, NEG_FILL)
        row_max = lax.optimization_barrier(jnp.max(scores, axis=-1, keepdims=True))
        raised = jnp.exp(scores - row_max)
        weights = raised / lax.optimization_barrier(jnp.sum(raised, axis=-1, keepdims=True))
        return highest(low(weights), values_in)
    per_head = lax.map(jax.checkpoint(one_head), packed.transpose(1, 0, 2))
    mixed = low_back(low(per_head.transpose(1, 0, 2).reshape(MAXLEN, D)))
    attended = low_back(highest(mixed, output_weight) + output_bias)
    middle = embedded + attended
    second_normed = low(layer_norm(middle, second_gain, second_shift))
    upward = low_back(highest(second_normed, upward_weight) + upward_bias)
    activated = low(gelu_tanh(upward))
    branch = low_back(highest(activated, downward_weight) + downward_bias)
    return (middle + branch) * valid

def reference(tokens, passes, first_gain, first_shift, heads_weight, query_bias, value_bias, output_weight, output_bias, second_gain, second_shift, upward_weight, upward_bias, downward_weight, downward_bias, pass_embed, cotangent):
    params = (first_gain.astype(jnp.float32), first_shift.astype(jnp.float32), heads_weight.astype(jnp.float32), query_bias.astype(jnp.float32), value_bias.astype(jnp.float32), output_weight.astype(jnp.float32), output_bias.astype(jnp.float32), second_gain.astype(jnp.float32), second_shift.astype(jnp.float32), upward_weight.astype(jnp.float32), upward_bias.astype(jnp.float32), downward_weight.astype(jnp.float32), downward_bias.astype(jnp.float32), pass_embed.astype(jnp.float32))

    def one_sequence(totals, sliced):
        row_tokens, pass_count, row_cotangent = sliced

        def forward(inputs, weights_all):
            return sequence_forward(inputs, pass_count, weights_all)
        result, pull = jax.vjp(forward, row_tokens.astype(jnp.float32), params)
        input_grad, weight_grads = pull(row_cotangent.astype(jnp.float32))
        totals = jax.tree.map(jnp.add, totals, weight_grads)
        return (totals, (result.astype(jnp.bfloat16), input_grad))
    start = tuple((jnp.zeros_like(member) for member in params))
    totals, outputs = lax.scan(one_sequence, start, (tokens, passes, cotangent))
    return (outputs[0], outputs[1], totals[0], totals[1], totals[2], totals[3], totals[4], totals[5], totals[6], totals[7], totals[8], totals[9], totals[10], totals[11], totals[12], totals[13])
```

```python
import functools

import jax
import jax.numpy as jnp
from jax import lax
from jax.experimental import pallas as pl
from jax.experimental.pallas import tpu as pltpu
from jax.sharding import PartitionSpec as P

HEADS = 12
HEAD = 64
BASE = 256
PASSES = 5
NEG_FILL = -1e30
EPSILON = 1e-05
TANH_IN = 0.7978845608028654
TANH_CUBE = 0.044715
F32 = jnp.float32
BF16 = jnp.bfloat16
VMEM_LIMIT = 60 * 2**20


def dot(left, right):
    return jnp.dot(left, right, preferred_element_type=F32)


def dot_nt(left, right):
    return lax.dot_general(
        left, right, (((1,), (1,)), ((), ())), preferred_element_type=F32
    )


def dot_tn(left, right):
    return lax.dot_general(
        left, right, (((0,), (0,)), ((), ())), preferred_element_type=F32
    )


def row_mean(block):
    return jnp.mean(block, axis=1, keepdims=True)


def col_sum(block):
    return jnp.sum(block, axis=0, keepdims=True)


def normalize(block):
    centre = block - row_mean(block)
    scale = lax.rsqrt(row_mean(centre * centre) + EPSILON)
    return centre * scale, scale


def places_of(block_id, core, half, rows):
    start = (block_id * half + core) * rows
    return start + lax.broadcasted_iota(jnp.int32, (rows, 1), 0)


def embed_kernel(scalars, kept, came, table, gain, shift, embedded, normed):
    core, seq, count = scalars[0], scalars[1], scalars[2]
    rows = kept.shape[0]
    for block_id in range(2):
        section = lax.rem(places_of(block_id, core, 2, rows), count)
        mine = kept[...].astype(F32)
        other = came[...].astype(F32)
        hidden = jnp.where(seq == block_id, mine, other)
        added = jnp.zeros_like(hidden)
        for section_id in range(PASSES):
            added = jnp.where(section == section_id, table[section_id : section_id + 1, :], added)
        hidden = hidden + added
        span = pl.ds(block_id * rows, rows)
        embedded[span, :] = hidden
        unit, _ = normalize(hidden)
        normed[span, :] = (unit * gain[...] + shift[...]).astype(BF16)


def gather_rows(core, kept, came, whole):
    rows = kept.shape[0] // 2
    for block_id in range(2):
        span = slice(block_id * rows, (block_id + 1) * rows)
        whole[pl.ds(pl.multiple_of((block_id * 2 + core) * rows, 64), rows), :] = kept[span, :]
        whole[pl.ds(pl.multiple_of((block_id * 2 + 1 - core) * rows, 64), rows), :] = came[span, :]


def split_rows(core, whole, kept, away):
    rows = kept.shape[0] // 2
    for block_id in range(2):
        span = slice(block_id * rows, (block_id + 1) * rows)
        kept[span, :] = whole[
            pl.ds(pl.multiple_of((block_id * 2 + core) * rows, 64), rows), :
        ].astype(kept.dtype)
        away[span, :] = whole[
            pl.ds(pl.multiple_of((block_id * 2 + 1 - core) * rows, 64), rows), :
        ].astype(away.dtype)


def head_parts(block, which):
    start = 3 * HEAD * which
    queries = block[:, start : start + HEAD] * jnp.asarray(HEAD**-0.5, BF16)
    keys = block[:, start + HEAD : start + 2 * HEAD]
    values = block[:, start + 2 * HEAD : start + 3 * HEAD]
    return queries, keys, values


def causal_block(size):
    key_place = lax.broadcasted_iota(jnp.int32, (size, size), 0)
    query_place = lax.broadcasted_iota(jnp.int32, (size, size), 1)
    return key_place <= query_place


def forward_kernel(
    scalars, kept, came, weight, bias, whole, packed, mixed, mixed_kept, mixed_away, log_total
):
    core = scalars[0]
    full = whole.shape[0]
    gather_rows(core, kept, came, whole)
    for start in range(0, full, BASE):
        span = pl.ds(start, BASE)
        packed[span, :] = (dot_nt(whole[span, :], weight[...]) + bias[...]).astype(BF16)
    visible = causal_block(BASE)

    def pair(index, carry):
        block = packed[:, pl.ds(pl.multiple_of(index * 6 * HEAD, 128), 6 * HEAD)]
        results, logs = [], []
        for which in range(2):
            queries, keys, values = head_parts(block, which)
            values_ext = jnp.concatenate([values.T, jnp.ones((16, full), BF16)], axis=0)
            outs, totals = [], []
            for start in range(0, full, BASE):
                end = start + BASE
                scores = dot_nt(keys[:end], queries[start:end])
                last = jnp.where(visible, scores[start:], NEG_FILL)
                scores = last if start == 0 else jnp.concatenate([scores[:start], last], axis=0)
                top = jnp.max(scores, axis=0, keepdims=True)
                raised = jnp.exp(scores - top).astype(BF16)
                grown = dot(values_ext[:, :end], raised)
                total = grown[HEAD : HEAD + 1]
                outs.append(grown[:HEAD] / total)
                totals.append(top + jnp.log(total))
            results.append(jnp.concatenate(outs, axis=1))
            logs.append(jnp.concatenate(totals, axis=1))
        mixed[:, pl.ds(pl.multiple_of(index * 2 * HEAD, 128), 2 * HEAD)] = jnp.concatenate(
            results, axis=0
        ).T.astype(BF16)
        log_total[index] = jnp.concatenate(logs, axis=0)
        return carry

    lax.fori_loop(0, HEADS // 4, pair, 0)
    split_rows(core, mixed, mixed_kept, mixed_away)


def feed_kernel(
    scalars,
    mixed_kept,
    mixed_came,
    embedded,
    cot_kept,
    cot_came,
    out_weight,
    out_bias,
    gain,
    shift,
    up_weight,
    up_bias,
    down_weight,
    down_bias,
    out_kept,
    out_away,
    middle_grad,
    mixed_grad_kept,
    mixed_grad_away,
    grads,
    row_sums,
    up_sums,
    mixed,
    middle,
    normed,
    normed_t,
    out_grad,
    branch,
    normed_grad,
):
    core, seq, count = scalars[0], scalars[1], scalars[2]
    total_rows, width = middle.shape
    rows = total_rows // 2
    half = width // 2
    hidden = up_weight.shape[1]
    owners = grads.shape[1]
    up_rows = width // owners
    down_rows = hidden // owners
    mixed[:, pl.ds(pl.multiple_of(core * half, 128), half)] = mixed_kept[...]
    mixed[:, pl.ds(pl.multiple_of((1 - core) * half, 128), half)] = mixed_came[...]
    valid = []
    for block_id in range(2):
        span = slice(block_id * rows, (block_id + 1) * rows)
        value = embedded[span, :] + dot(mixed[span, :], out_weight[...]) + out_bias[...]
        middle[span, :] = value
        unit, _ = normalize(value)
        normed[span, :] = (unit * gain[...] + shift[...]).astype(BF16)
        keep = places_of(block_id, core, 2, rows) < count * BASE
        valid.append(keep)
        cot = jnp.where(seq == block_id, cot_kept[...].astype(F32), cot_came[...].astype(F32))
        out_grad[span, :] = jnp.where(keep, cot, 0.0).astype(BF16)
    normed_t[...] = normed[...].T
    branch[...] = jnp.zeros_like(branch)
    normed_grad[...] = jnp.zeros_like(normed_grad)
    tile = 2 * half
    for step in range(hidden // tile):
        cols = pl.ds(step * tile, tile)
        value = dot(normed[...], up_weight[:, cols]) + up_bias[:, cols]
        square = value * value
        tanh = jnp.tanh(value * (TANH_IN + TANH_IN * TANH_CUBE * square))
        gate = 0.5 + 0.5 * tanh
        activated = (value * gate).astype(BF16)
        slope = gate + (0.5 * value) * (1.0 - tanh * tanh) * (
            TANH_IN + 3.0 * TANH_IN * TANH_CUBE * square
        )
        up_grad = (dot_nt(out_grad[...], down_weight[cols, :]) * slope).astype(BF16)
        branch[...] += dot(activated, down_weight[cols, :])
        normed_grad[...] += dot_nt(up_grad, up_weight[:, cols])
        up_sums[:, cols] = col_sum(up_grad.astype(F32))
        up_part = dot(normed_t[...], up_grad).astype(BF16)
        down_part = dot_tn(activated, out_grad[...]).astype(BF16)
        for sub in range(2):
            slot = (step * 2 + sub) % 4
            side = (step * 2 + sub) // 4
            for owner in range(owners):
                grads[side, owner, slot * up_rows : (slot + 1) * up_rows, :] = up_part[
                    owner * up_rows : (owner + 1) * up_rows, sub * half : (sub + 1) * half
                ]
        for owner in range(owners):
            first = max(owner * down_rows, step * tile)
            last = min((owner + 1) * down_rows, (step + 1) * tile)
            if first < last:
                place = 4 * up_rows + first - owner * down_rows
                for side in range(2):
                    grads[side, owner, place : place + last - first, :] = down_part[
                        first - step * tile : last - step * tile, side * half : (side + 1) * half
                    ]
    sums = [0.0] * 4
    for block_id in range(2):
        span = slice(block_id * rows, (block_id + 1) * rows)
        value = middle[span, :]
        unit, scale = normalize(value)
        inner = normed_grad[span, :]
        scaled = inner * gain[...]
        cot = out_grad[span, :].astype(F32)
        grad = cot + scale * (scaled - row_mean(scaled) - unit * row_mean(scaled * unit))
        middle_grad[span, :] = grad
        low = grad.astype(BF16)
        normed[span, :] = low
        result = jnp.where(
            valid[block_id], value + branch[span, :] + down_bias[...], 0.0
        ).astype(BF16)

        @pl.when(seq == block_id)
        def _():
            out_kept[...] = result

        @pl.when(seq != block_id)
        def _():
            out_away[...] = result

        mixed_grad_kept[span, :] = dot_nt(
            low, out_weight[pl.ds(pl.multiple_of(core * half, 128), half), :]
        ).astype(BF16)
        mixed_grad_away[span, :] = dot_nt(
            low, out_weight[pl.ds(pl.multiple_of((1 - core) * half, 128), half), :]
        ).astype(BF16)
        terms = (inner * unit, inner, low.astype(F32), cot)
        sums = [have + col_sum(term) for have, term in zip(sums, terms)]
    row_sums[...] = jnp.concatenate(sums + [jnp.zeros((4, width), F32)], axis=0)
    out_part = dot_tn(mixed[...], normed[...]).astype(BF16)
    base_row = 4 * up_rows + down_rows
    for owner in range(owners):
        for side in range(2):
            grads[side, owner, base_row : base_row + up_rows, :] = out_part[
                owner * up_rows : (owner + 1) * up_rows, side * half : (side + 1) * half
            ]


def backward_kernel(
    scalars,
    packed,
    log_total,
    mixed_kept,
    mixed_away,
    grad_kept,
    grad_came,
    whole,
    weight,
    inner_kept,
    inner_away,
    heads_grad,
    bias_sums,
    mixed,
    mixed_grad,
    packed_grad,
    inner,
    value_key_sum,
):
    core = scalars[0]
    full = whole.shape[0]
    owners = heads_grad.shape[0]
    own_rows = heads_grad.shape[1] // 3
    gather_rows(core, mixed_kept, mixed_away, mixed)
    gather_rows(core, grad_kept, grad_came, mixed_grad)
    visible = causal_block(BASE)

    def pair(index, carry):
        base = pl.multiple_of(index * 6 * HEAD, 128)
        block = packed[:, pl.ds(base, 6 * HEAD)]
        lanes = pl.ds(pl.multiple_of(index * 2 * HEAD, 128), 2 * HEAD)
        both_grad = mixed_grad[:, lanes]
        overlap = both_grad.astype(F32) * mixed[:, lanes].astype(F32)
        parts = []
        for which in range(2):
            queries, keys, values = head_parts(block, which)
            grad = both_grad[:, HEAD * which : HEAD * (which + 1)]
            delta = jnp.sum(
                overlap[:, HEAD * which : HEAD * (which + 1)], axis=1, keepdims=True
            ).T
            logs = log_total[index][which : which + 1]
            keys_t = keys.T
            blank = jnp.zeros_like(queries)
            grad_ext = jnp.concatenate([blank, grad], axis=1)
            queries_ext = jnp.concatenate([queries, blank], axis=1)
            query_parts = []
            for start in range(0, full, BASE):
                end = start + BASE
                span = slice(start, end)
                weights = jnp.exp(dot_nt(keys[:end], queries[span]) - logs[:, span])
                last = jnp.where(visible, weights[start:], 0.0)
                weights = (
                    last if start == 0 else jnp.concatenate([weights[:start], last], axis=0)
                )
                weight_grad = dot_nt(values[:end], grad[span])
                score_grad = (weights * (weight_grad - delta[:, span])).astype(BF16)
                added = dot(weights.astype(BF16), grad_ext[span]) + dot(
                    score_grad, queries_ext[span]
                )
                if start > 0:
                    value_key_sum[which, :start, :] += added[:start]
                value_key_sum[which, start:end, :] = added[start:]
                query_parts.append(dot(keys_t[:, :end], score_grad) * HEAD**-0.5)
            parts += [jnp.concatenate(query_parts, axis=1).T, value_key_sum[which]]
        packed_grad[:, pl.ds(base, 6 * HEAD)] = jnp.concatenate(parts, axis=1).astype(BF16)
        return carry

    lax.fori_loop(0, HEADS // 4, pair, 0)
    low = packed_grad[...]
    bias_sums[...] = col_sum(low.astype(F32))
    for start in range(0, full, BASE):
        inner[pl.ds(start, BASE), :] = dot(packed_grad[pl.ds(start, BASE), :], weight[...])
    split_rows(core, inner, inner_kept, inner_away)
    part = dot_tn(whole[...], low).astype(BF16)
    third = heads_grad.shape[2]
    for owner in range(owners):
        for group in range(3):
            heads_grad[owner, group * own_rows : (group + 1) * own_rows, :] = part[
                owner * own_rows : (owner + 1) * own_rows, group * third : (group + 1) * third
            ]


def input_kernel(
    scalars, inner_kept, inner_came, embedded, middle_grad, gain, grad_kept, grad_away, sums
):
    core, seq, count = scalars[0], scalars[1], scalars[2]
    total_rows, width = embedded.shape
    rows = total_rows // 2
    found = [0.0] * (2 + PASSES)
    for block_id in range(2):
        span = slice(block_id * rows, (block_id + 1) * rows)
        unit, scale = normalize(embedded[span, :])
        inner = inner_kept[span, :] + inner_came[span, :].astype(F32)
        scaled = inner * gain[...]
        grad = middle_grad[span, :] + scale * (
            scaled - row_mean(scaled) - unit * row_mean(scaled * unit)
        )

        @pl.when(seq == block_id)
        def _():
            grad_kept[...] = grad

        @pl.when(seq != block_id)
        def _():
            grad_away[...] = grad.astype(BF16)

        section = lax.rem(places_of(block_id, core, 2, rows), count)
        terms = [inner * unit, inner]
        for section_id in range(PASSES):
            terms.append(jnp.where(section == section_id, grad, 0.0))
        found = [have + col_sum(term) for have, term in zip(found, terms)]
    sums[...] = jnp.concatenate(found + [jnp.zeros((1, width), F32)], axis=0)


MESH = pl.DeviceIdType.MESH


def add_low(left, right):
    return (left.astype(F32) + right.astype(F32)).astype(BF16)


def main_kernel(
    count_ref,
    mixed_came,
    embedded,
    cot_kept,
    cot_came,
    out_bias,
    second_gain,
    second_shift,
    up_bias,
    down_bias,
    first_gain,
    log_total,
    out_weight_hbm,
    up_weight_hbm,
    down_weight_hbm,
    weight_hbm,
    packed_hbm,
    mixed_hbm,
    whole_hbm,
    out_hbm,
    tokens_hbm,
    up_hbm,
    down_hbm,
    square_hbm,
    heads_hbm,
    early_out,
    late_out,
    middle_grad,
    mixed_grad_kept,
    mixed_grad_away,
    mixed_grad_came,
    inner_away,
    inner_came,
    tokens_away,
    tokens_came,
    out_stage,
    up_parts,
    up_core,
    up_land,
    down_parts,
    down_core,
    down_land,
    square_parts,
    square_core,
    square_land,
    heads_parts,
    heads_land,
    up_final,
    down_final,
    square_final,
    heads_final,
    early,
    early_total,
    early_heads,
    early_owners,
    late,
    late_total,
    late_heads,
    late_owners,
    send_sems,
    recv_sems,
    local_sems,
):
    dp, head = lax.axis_index("dp"), lax.axis_index("head")
    core, seq = head % 2, head // 2
    bit0, bit1, bit2 = dp % 2, (dp // 2) % 2, dp // 4
    far_core, far_seq = 1 - core, 1 - seq
    far0, far1, far2 = 1 - bit0, 1 - bit1, 1 - bit2
    to_core = {"head": head + far_core - core}
    to_seq = {"head": head + 2 * (far_seq - seq)}
    to0 = {"dp": dp + far0 - bit0}
    to1 = {"dp": dp + 2 * (far1 - bit1)}
    to2 = {"dp": dp + 4 * (far2 - bit2)}
    head_peers = [lax.rem(head + step, 4) for step in range(1, 4)]
    dp_peers = [lax.rem(dp + step, 8) for step in range(1, 8)]
    own_half = pl.multiple_of(core * 384, 128)
    far_half = pl.multiple_of(far_core * 384, 128)
    own_starts = [pl.multiple_of((block * 2 + core) * 320, 64) for block in range(2)]
    far_starts = [pl.multiple_of((block * 2 + far_core) * 320, 64) for block in range(2)]
    late_blocks = [far_seq, seq]
    late_own = [pl.multiple_of((block * 2 + core) * 320, 64) for block in late_blocks]
    late_far = [pl.multiple_of((block * 2 + far_core) * 320, 64) for block in late_blocks]
    late_spans = [pl.multiple_of(block * 320, 64) for block in late_blocks]
    owner_base = core * 4
    own_weight = pl.multiple_of(core * 1152, 128)
    count = count_ref[0]
    length = count * BASE
    rows, total_rows, width, half, full, tile = 320, 640, 768, 384, 1280, 1024

    sent = []
    used = [0, 0]

    def view(place):
        if isinstance(place, tuple):
            return place[0].at[place[1:]]
        return place

    class Sent:
        def __init__(self, source, target, device):
            self.parts = (source, target, device, used[0])
            used[0] += 1

        def make(self):
            source, target, device, index = self.parts
            return pltpu.make_async_remote_copy(
                src_ref=view(source),
                dst_ref=view(target),
                send_sem=send_sems.at[index],
                recv_sem=recv_sems.at[index],
                device_id=device,
                device_id_type=MESH,
            )

        def wait_recv(self):
            self.make().wait_recv()

        def wait_send(self):
            self.make().wait_send()

    class Fetched:
        def __init__(self, source, target):
            self.parts = (source, target, used[1])
            used[1] += 1

        def make(self):
            source, target, index = self.parts
            return pltpu.make_async_copy(view(source), view(target), local_sems.at[index])

        def wait(self):
            self.make().wait()

    def send(source, target, device):
        copy = Sent(source, target, device)
        copy.make().start()
        sent.append(copy)
        return copy

    def fetch(source, target):
        copy = Fetched(source, target)
        copy.make().start()
        return copy

    every = slice(None)

    barrier = pltpu.get_barrier_semaphore()
    for peer in head_peers:
        pl.semaphore_signal(barrier, inc=1, device_id={"head": peer}, device_id_type=MESH)
    for peer in dp_peers:
        pl.semaphore_signal(barrier, inc=1, device_id={"dp": peer}, device_id_type=MESH)

    def first_step(parts, at, cored):
        if cored is None:
            return at
        copy = send((parts,) + at + (far_core,), (cored,) + at, to_core)
        yield
        copy.wait_recv()
        place = at + (core,)
        parts[place] = add_low(parts[place], cored[at] if at else cored[...])
        return place

    def halving(parts, lead, land, at, away, kept, device):
        copy = send((parts,) + lead + away, (land,) + at, device)
        yield
        copy.wait_recv()
        place = lead + kept
        parts[place] = add_low(parts[place], land[at] if at else land[...])

    def chain_x(parts, at, cored, land, final):
        lead = yield from first_step(parts, at, cored)
        yield from halving(
            parts, lead, land[0], at, (every, every, far0), (every, every, bit0), to0
        )
        yield from halving(parts, lead, land[1], at, (every, far1, bit0), (every, bit1, bit0), to1)
        yield from halving(parts, lead, land[2], at, (far2, bit1, bit0), (bit2, bit1, bit0), to2)
        place = lead + (bit2, bit1, bit0)
        copy = send((parts,) + place, (land[3],) + at, to_seq)
        yield
        copy.wait_recv()
        final[at + (core,)] = add_low(parts[place], land[3][at] if at else land[3][...])
        copy = send((final,) + at + (core,), (final,) + at + (core,), to_core)
        yield
        copy.wait_recv()
        yield

    def chain_y(parts, at, cored, land, final):
        lead = yield from first_step(parts, at, cored)
        yield from halving(
            parts, lead, land[0], at, (every, every, every, far_seq), (every, every, every, seq),
            to_seq,
        )
        yield from halving(
            parts, lead, land[1], at, (every, every, far0, seq), (every, every, bit0, seq), to0
        )
        yield from halving(
            parts, lead, land[2], at, (every, far1, bit0, seq), (every, bit1, bit0, seq), to1
        )
        copy = send((parts,) + lead + (far2, bit1, bit0, seq), (land[3],) + at, to2)
        yield
        copy.wait_recv()
        final[at + (core, seq)] = add_low(parts[lead + (bit2, bit1, bit0, seq)], land[3][at])
        place = (final,) + at + (core, seq)
        copy = send(place, place, to_seq)
        yield
        copy.wait_recv()
        place = (final,) + at + (core,)
        copy = send(place, place, to_core)
        yield
        copy.wait_recv()
        yield

    def vector_sum(parts, summed, by_head, by_owner, result):
        copies = [
            send(parts, (by_head, head), {"head": peer}) for peer in head_peers
        ]
        by_head[head] = parts[...]
        yield
        for copy in copies:
            copy.wait_recv()
        summed[...] = by_head[0] + by_head[1] + by_head[2] + by_head[3]
        copies = [
            send((summed, peer), (by_owner, dp), {"dp": peer}) for peer in dp_peers
        ]
        by_owner[dp] = summed[dp]
        yield
        for copy in copies:
            copy.wait_recv()
        found = by_owner[0]
        for place in range(1, 8):
            found = found + by_owner[place]
        result[...] = found
        yield

    class Chain:
        def __init__(self, name, length, steps):
            self.name, self.steps, self.length, self.taken = name, steps, length, 0

        def step(self):
            with jax.named_scope(f"{self.name}_{self.taken}"):
                self.taken += 1
                next(self.steps)

    ups = [
        Chain(f"up{t}", 7, chain_x(up_parts, (t,), up_core, up_land, up_final)) for t in range(3)
    ]
    downs = [
        Chain(f"down{t}", 8, chain_y(down_parts, (t,), down_core, down_land, down_final))
        for t in range(3)
    ]
    square = Chain("square", 7, chain_x(square_parts, (), square_core, square_land, square_final))
    heads = [
        Chain("heads0", 6, chain_x(heads_parts, (0,), None, heads_land, heads_final)),
        Chain(
            "heads1",
            7,
            chain_y(heads_parts, (1,), None, heads_land[:3] + heads_land[4:], heads_final),
        ),
        Chain("heads2", 6, chain_x(heads_parts, (2,), None, heads_land, heads_final)),
    ]
    early_sum = Chain(
        "early", 3, vector_sum(early, early_total, early_heads, early_owners, early_out)
    )
    late_sum = Chain("late", 3, vector_sum(late, late_total, late_heads, late_owners, late_out))

    def tick(*chains):
        for chain in chains:
            chain.step()

    def feed_phase(
        out_weight, up_weight, down_weight, mixed, middle, normed, normed_t, out_grad, branch,
        active, up_grads,
    ):
        fetched = [
            fetch(
                (mixed_hbm, pl.ds(own_starts[block], rows)),
                (mixed_grad_kept, pl.ds(block * rows, rows)),
            )
            for block in range(2)
        ]
        out_fetch = fetch(out_weight_hbm, out_weight)

        def load(step):
            slot = step % 2
            copies = []
            for group in range(8):
                cols = pl.ds(group * half + step * 128, 128)
                into = pl.ds(group * 128, 128)
                copies.append(fetch((up_weight_hbm, every, cols), (up_weight, slot, every, into)))
                copies.append(fetch((down_weight_hbm, cols), (down_weight, slot, into)))
            return copies

        loads = [load(0), load(1)]
        with jax.named_scope("barrier"):
            pl.semaphore_wait(barrier, 10)
        for copy in fetched:
            copy.wait()
        with jax.named_scope("project"):
            mixed[:, pl.ds(own_half, half)] = mixed_grad_kept[...]
            mixed[:, pl.ds(far_half, half)] = mixed_came[...]
            out_fetch.wait()
            valid = []
            for block in range(2):
                span = slice(block * rows, (block + 1) * rows)
                value = embedded[span, :] + dot(mixed[span, :], out_weight[...]) + out_bias[...]
                middle[span, :] = value
                unit, _ = normalize(value)
                normed[span, :] = (unit * second_gain[...] + second_shift[...]).astype(BF16)
                keep = places_of(block, core, 2, rows) < length
                valid.append(keep)
                cot = jnp.where(seq == block, cot_kept[...].astype(F32), cot_came[...].astype(F32))
                out_grad[span, :] = jnp.where(keep, cot, 0.0).astype(BF16)
        normed_t[...] = normed[...].T
        branch[...] = jnp.zeros_like(branch)
        middle_grad[...] = jnp.zeros_like(middle_grad)
        early[...] = jnp.zeros_like(early)
        late[...] = jnp.zeros_like(late)
        plan = (
            ((), (), (), ()),
            ((), (ups[0], downs[0]), (), ()),
            ((), (ups[0], downs[0], ups[1], downs[1]), (), ()),
        )
        for step in range(3):
            slot = step % 2
            for copy in loads[step]:
                copy.wait()
            for block in range(2):
                span = slice(block * rows, (block + 1) * rows)
                with jax.named_scope("hidden"):
                    value = dot(normed[span, :], up_weight[slot]) + up_bias[step]
                    square_of = value * value
                    tanh = jnp.tanh(value * (TANH_IN + TANH_IN * TANH_CUBE * square_of))
                    gate = 0.5 + 0.5 * tanh
                    act = (value * gate).astype(BF16)
                    slope = gate + (0.5 * value) * (1.0 - tanh * tanh) * (
                        TANH_IN + 3.0 * TANH_IN * TANH_CUBE * square_of
                    )
                    up_grad = (dot_nt(out_grad[span, :], down_weight[slot]) * slope).astype(BF16)
                    active[span, :] = act
                    up_grads[span, :] = up_grad
                    branch[span, :] += dot(act, down_weight[slot])
                    middle_grad[span, :] += dot_nt(up_grad, up_weight[slot])
                tick(*plan[step][block])
            if step == 0:
                loads.append(None)
            sums = col_sum(up_grads[...].astype(F32))
            for group in range(8):
                early[group, 4 + step : 5 + step, :] = sums[:, group * 128 : (group + 1) * 128]
            with jax.named_scope("up_weight"):
                for side in range(2):
                    up_parts[step, side] = (
                        dot(normed_t[...], up_grads[:, side * 512 : (side + 1) * 512])
                        .astype(BF16)
                        .reshape(2, 2, 2, 2, 48, 512)
                    )
            tick(ups[step])
            with jax.named_scope("down_weight"):
                for side in range(2):
                    down_parts[step, side] = (
                        dot_tn(active[...], out_grad[:, side * half : (side + 1) * half])
                        .astype(BF16)
                        .reshape(2, 2, 2, 2, 64, half)
                    )
            tick(downs[step])
            if step == 0:
                loads[2] = load(2)
        sums = [0.0] * 4
        with jax.named_scope("middle_grad"):
            for block in range(2):
                span = slice(block * rows, (block + 1) * rows)
                value = middle[span, :]
                unit, scale = normalize(value)
                inner = middle_grad[span, :]
                scaled = inner * second_gain[...]
                cot = out_grad[span, :].astype(F32)
                grad = cot + scale * (scaled - row_mean(scaled) - unit * row_mean(scaled * unit))
                middle_grad[span, :] = grad
                low = grad.astype(BF16)
                normed[span, :] = low
                out_stage[block] = jnp.where(
                    valid[block], value + branch[span, :] + down_bias[...], 0.0
                ).astype(BF16)
                mixed_grad_away[span, :] = dot_nt(low, out_weight[pl.ds(far_half, half), :]).astype(
                    BF16
                )
                terms = (inner * unit, inner, low.astype(F32), cot)
                sums = [have + col_sum(term) for have, term in zip(sums, terms)]
        exchange = send(mixed_grad_away, mixed_grad_came, to_core)
        with jax.named_scope("output_weight"):
            for block in range(2):
                span = slice(block * rows, (block + 1) * rows)
                mixed_grad_kept[span, :] = dot_nt(
                    normed[span, :], out_weight[pl.ds(own_half, half), :]
                ).astype(BF16)
            for side in range(2):
                square_parts[side] = (
                    dot_tn(mixed[...], normed[:, side * half : (side + 1) * half])
                    .astype(BF16)
                    .reshape(2, 2, 2, 2, 48, half)
                )
        for line, found in enumerate(sums):
            for group in range(8):
                early[group, line : line + 1, :96] = found[:, group * 96 : (group + 1) * 96]
        return exchange

    exchange = pl.run_scoped(
        lambda *refs: (feed_phase(*refs), None)[1],
        pltpu.VMEM((width, width), BF16),
        pltpu.VMEM((2, width, tile), BF16),
        pltpu.VMEM((2, tile, width), BF16),
        pltpu.VMEM((total_rows, width), BF16),
        pltpu.VMEM((total_rows, width), F32),
        pltpu.VMEM((total_rows, width), BF16),
        pltpu.VMEM((width, total_rows), BF16),
        pltpu.VMEM((total_rows, width), BF16),
        pltpu.VMEM((total_rows, width), F32),
        pltpu.VMEM((total_rows, tile), BF16),
        pltpu.VMEM((total_rows, tile), BF16),
    )
    exchange = sent[-1]
    tick(square, early_sum)
    out_sent = send((out_stage, far_seq), (out_hbm, seq), to_seq)
    out_kept = fetch((out_stage, seq), (out_hbm, seq))

    def back_phase(
        packed, mixed, whole, weight, mixed_grad, packed_grad, inner_kept, value_key_sum,
        up_stage, down_stage, square_stage, heads_stage, tokens_stage,
    ):
        packed_fetch = fetch(packed_hbm, packed)
        mixed_fetch = fetch(mixed_hbm, mixed)
        whole_fetch = fetch(whole_hbm, whole)
        weight_fetch = fetch((weight_hbm, pl.ds(own_weight, 1152)), weight)
        for block in range(2):
            span = slice(block * rows, (block + 1) * rows)
            mixed_grad[pl.ds(own_starts[block], rows), :] = mixed_grad_kept[span, :]
        with jax.named_scope("mixed_grad"):
            exchange.wait_recv()
            for block in range(2):
                span = slice(block * rows, (block + 1) * rows)
                mixed_grad[pl.ds(far_starts[block], rows), :] = mixed_grad_came[span, :]
        visible = causal_block(BASE)
        with jax.named_scope("fetch"):
            packed_fetch.wait()
            mixed_fetch.wait()
        tick(ups[2], downs[2])
        plan = (
            (downs[0], ups[1], square, early_sum),
            (ups[0], downs[1], early_sum),
            (downs[0], ups[2], downs[2]),
            (ups[1], square, downs[1]),
            (ups[0], downs[0], heads[0]),
            (ups[1], ups[2], downs[2]),
        )
        for index in range(3):
            block = packed[:, index * 384 : (index + 1) * 384]
            both_grad = mixed_grad[:, index * 128 : (index + 1) * 128]
            overlap = both_grad.astype(F32) * mixed[:, index * 128 : (index + 1) * 128].astype(F32)
            parts = []
            for which in range(2):
                with jax.named_scope("attend"):
                    queries, keys, values = head_parts(block, which)
                    grad = both_grad[:, HEAD * which : HEAD * (which + 1)]
                    delta = jnp.sum(
                        overlap[:, HEAD * which : HEAD * (which + 1)], axis=1, keepdims=True
                    ).T
                    logs = log_total[index][which : which + 1]
                    keys_t = keys.T
                    blank = jnp.zeros_like(queries)
                    grad_ext = jnp.concatenate([blank, grad], axis=1)
                    queries_ext = jnp.concatenate([queries, blank], axis=1)
                    query_parts = []
                    for start in range(0, full, BASE):
                        end = start + BASE
                        span = slice(start, end)
                        weights = jnp.exp(dot_nt(keys[:end], queries[span]) - logs[:, span])
                        last = jnp.where(visible, weights[start:], 0.0)
                        weights = (
                            last if start == 0 else jnp.concatenate([weights[:start], last], axis=0)
                        )
                        weight_grad = dot_nt(values[:end], grad[span])
                        score_grad = (weights * (weight_grad - delta[:, span])).astype(BF16)
                        added = dot(weights.astype(BF16), grad_ext[span]) + dot(
                            score_grad, queries_ext[span]
                        )
                        if start > 0:
                            value_key_sum[which, :start, :] += added[:start]
                        value_key_sum[which, start:end, :] = added[start:]
                        query_parts.append(dot(keys_t[:, :end], score_grad) * HEAD**-0.5)
                    parts += [jnp.concatenate(query_parts, axis=1).T, value_key_sum[which]]
                tick(*plan[index * 2 + which])
            low = jnp.concatenate(parts, axis=1).astype(BF16)
            packed_grad[:, index * 384 : (index + 1) * 384] = low
            sums = col_sum(low.astype(F32))
            for which in range(2):
                for line in range(2):
                    first = 192 * which + 128 * line
                    piece = sums[:, first : first + 64]
                    place = (index * 2 + which) * 64
                    while place < (index * 2 + which + 1) * 64:
                        group = place // 96
                        stop = min((group + 1) * 96, (index * 2 + which + 1) * 64)
                        offset = place - (index * 2 + which) * 64
                        late[
                            owner_base + group,
                            7 + line : 8 + line,
                            place - group * 96 : stop - group * 96,
                        ] = piece[:, offset : offset + stop - place]
                        place = stop
            if index == 0:
                whole_fetch.wait()
            with jax.named_scope("heads_weight"):
                heads_parts[index] = (
                    dot_tn(whole[...], low).astype(BF16).reshape(2, 2, 2, 2, 48, half)
                )
            tick(heads[index])
        weight_fetch.wait()
        found = [0.0] * (2 + PASSES)
        ends = (
            ((square, downs[1], downs[0]), (ups[2], heads[0], heads[1])),
            ((ups[0], downs[2], heads[2]), (ups[1], square, heads[0], heads[1])),
        )
        copies = []
        for order in range(2):
            with jax.named_scope("inner"):
                inner_away[order] = dot(
                    packed_grad[pl.ds(late_far[order], rows), :], weight[...]
                ).astype(BF16)
                copies.append(send((inner_away, order), (inner_came, order), to_core))
                inner_kept[order] = dot(packed_grad[pl.ds(late_own[order], rows), :], weight[...])
            tick(*ends[order][0])
        for order in range(2):
            span = pl.ds(late_spans[order], rows)
            with jax.named_scope("input"):
                unit, scale = normalize(embedded[span, :])
                copies[order].wait_recv()
                inner = inner_kept[order] + inner_came[order].astype(F32)
                scaled = inner * first_gain[...]
                grad = middle_grad[span, :] + scale * (
                    scaled - row_mean(scaled) - unit * row_mean(scaled * unit)
                )
                if order == 0:
                    tokens_away[...] = grad.astype(BF16)
                    tokens_sent = send(tokens_away, tokens_came, to_seq)
                else:
                    tokens_stage[0] = grad
                    tokens_kept = fetch((tokens_stage, 0), (tokens_hbm, seq))
                section = lax.rem(places_of(late_blocks[order], core, 2, rows), count)
                terms = [inner * unit, inner]
                for section_id in range(PASSES):
                    terms.append(jnp.where(section == section_id, grad, 0.0))
                found = [have + col_sum(term) for have, term in zip(found, terms)]
            tick(*ends[order][1])
        for line, value in enumerate(found):
            for group in range(8):
                late[group, line : line + 1, :96] = value[:, group * 96 : (group + 1) * 96]
        tick(late_sum)

        def drain(chain):
            while chain.taken < chain.length:
                chain.step()

        writes = []
        for chain in downs + ups + [square, early_sum]:
            drain(chain)
        for side in range(2):
            for step in range(3):
                for group in range(4):
                    first = (side * 4 + group) * half + step * 128
                    for part in range(2):
                        up_stage[part * 48 : (part + 1) * 48, first : first + 128] = up_final[
                            step, side, part, :, group * 128 : (group + 1) * 128
                        ].astype(F32)
                for part in range(2):
                    first = step * 128 + part * 64
                    down_stage[first : first + 64, side * half : (side + 1) * half] = down_final[
                        step, side, part
                    ].astype(F32)
            for part in range(2):
                square_stage[part * 48 : (part + 1) * 48, side * half : (side + 1) * half] = (
                    square_final[side, part].astype(F32)
                )
        writes.append(fetch(up_stage, up_hbm))
        writes.append(fetch(down_stage, down_hbm))
        writes.append(fetch(square_stage, square_hbm))
        tick(late_sum)
        for chain in (heads[0], heads[1], heads[2], late_sum):
            drain(chain)
        for index in range(3):
            for side in range(2):
                for part in range(2):
                    for which in range(2):
                        heads_stage[
                            side * 6 + index * 2 + which, part * 48 : (part + 1) * 48, :
                        ] = heads_final[
                            index, side, part, :, which * 192 : (which + 1) * 192
                        ].astype(F32)
        writes.append(fetch(heads_stage, heads_hbm))
        with jax.named_scope("tokens"):
            tokens_sent.wait_recv()
            tokens_stage[1] = tokens_came[...].astype(F32)
            writes.append(fetch((tokens_stage, 1), (tokens_hbm, far_seq)))
        tokens_kept.wait()
        for copy in writes:
            copy.wait()

    pl.run_scoped(
        back_phase,
        pltpu.VMEM((full, 1152), BF16),
        pltpu.VMEM((full, half), BF16),
        pltpu.VMEM((full, width), BF16),
        pltpu.VMEM((1152, width), BF16),
        pltpu.VMEM((full, half), BF16),
        pltpu.VMEM((full, 1152), BF16),
        pltpu.VMEM((2, rows, width), F32),
        pltpu.VMEM((2, full, 2 * HEAD), F32),
        pltpu.VMEM((96, 3072), F32),
        pltpu.VMEM((384, width), F32),
        pltpu.VMEM((96, width), F32),
        pltpu.VMEM((HEADS, 96, 192), F32),
        pltpu.VMEM((2, rows, width), F32),
    )
    out_kept.wait()
    out_sent.wait_recv()
    for copy in sent:
        copy.wait_send()


def swap(value, axis, bit):
    count = lax.axis_size(axis)
    return lax.ppermute(value, axis, [(place, place ^ bit) for place in range(count)])


def call(kernel, out_shapes, args, scratch=(), flops=0, moved=0):
    specs = [pl.BlockSpec(memory_space=pltpu.SMEM)] + [
        pl.BlockSpec(memory_space=pltpu.VMEM) for _ in args[1:]
    ]
    return pl.pallas_call(
        kernel,
        out_shape=tuple(jax.ShapeDtypeStruct(*item) for item in out_shapes),
        in_specs=specs,
        scratch_shapes=[pltpu.VMEM(*item) for item in scratch],
        compiler_params=pltpu.CompilerParams(vmem_limit_bytes=VMEM_LIMIT),
        cost_estimate=pl.CostEstimate(flops=flops, bytes_accessed=moved, transcendentals=0),
    )(*args)


def fused_tail(
    count, mixed_came, embedded, cot_kept, cot_came, out_bias, second_gain, second_shift,
    up_bias, down_bias, first_gain, log_total, out_weight, up_weight, down_weight, weight_t,
    packed, mixed, whole,
):
    rows, width, half, full = 320, 768, 384, 1280
    row = lambda vector: vector.reshape(1, -1)
    up_bias = up_bias.reshape(8, 3, 128).swapaxes(0, 1).reshape(3, 1, 1024)

    def lands(lead, count, wide, last):
        return (
            pltpu.VMEM(lead + (2, 2, 2, count, wide), BF16),
            pltpu.VMEM(lead + (2, 2, count, wide), BF16),
            pltpu.VMEM(lead + (2, count, wide), BF16),
            pltpu.VMEM(lead + last + (count, wide), BF16),
        )

    def sums(lines):
        return (
            pltpu.VMEM((8, lines, 128), F32),
            pltpu.VMEM((8, lines, 128), F32),
            pltpu.VMEM((4, 8, lines, 128), F32),
            pltpu.VMEM((8, lines, 128), F32),
        )

    scratch = (
        pltpu.VMEM((2 * rows, width), F32),
        pltpu.VMEM((2 * rows, half), BF16),
        pltpu.VMEM((2 * rows, half), BF16),
        pltpu.VMEM((2 * rows, half), BF16),
        pltpu.VMEM((2, rows, width), BF16),
        pltpu.VMEM((2, rows, width), BF16),
        pltpu.VMEM((rows, width), BF16),
        pltpu.VMEM((rows, width), BF16),
        pltpu.VMEM((2, rows, width), BF16),
        pltpu.VMEM((3, 2, 2, 2, 2, 2, 48, 512), BF16),
        pltpu.VMEM((3, 2, 2, 2, 2, 48, 512), BF16),
        lands((3,), 48, 512, (2,)),
        pltpu.VMEM((3, 2, 2, 2, 2, 2, 64, half), BF16),
        pltpu.VMEM((3, 2, 2, 2, 2, 64, half), BF16),
        lands((3,), 64, half, ()),
        pltpu.VMEM((2, 2, 2, 2, 2, 48, half), BF16),
        pltpu.VMEM((2, 2, 2, 2, 48, half), BF16),
        lands((), 48, half, (2,)),
        pltpu.VMEM((3, 2, 2, 2, 2, 48, half), BF16),
        lands((3,), 48, half, (2,)) + (pltpu.VMEM((3, 48, half), BF16),),
        pltpu.VMEM((3, 2, 2, 48, 512), BF16),
        pltpu.VMEM((3, 2, 2, 64, half), BF16),
        pltpu.VMEM((2, 2, 48, half), BF16),
        pltpu.VMEM((3, 2, 2, 48, half), BF16),
        *sums(8),
        *sums(16),
        pltpu.SemaphoreType.DMA((96,)),
        pltpu.SemaphoreType.DMA((96,)),
        pltpu.SemaphoreType.DMA((80,)),
    )
    any_space = pl.BlockSpec(memory_space=pl.ANY)
    vmem = pl.BlockSpec(memory_space=pltpu.VMEM)
    out_shape = (
        jax.ShapeDtypeStruct((2, rows, width), BF16),
        jax.ShapeDtypeStruct((2, rows, width), F32),
        jax.ShapeDtypeStruct((96, 3072), F32),
        jax.ShapeDtypeStruct((384, width), F32),
        jax.ShapeDtypeStruct((96, width), F32),
        jax.ShapeDtypeStruct((HEADS, 96, 192), F32),
        jax.ShapeDtypeStruct((8, 128), F32),
        jax.ShapeDtypeStruct((16, 128), F32),
    )
    out, tokens, up, down, square, heads, early, late = pl.pallas_call(
        main_kernel,
        out_shape=out_shape,
        in_specs=[pl.BlockSpec(memory_space=pltpu.SMEM)] + [vmem] * 11 + [any_space] * 7,
        out_specs=(any_space,) * 6 + (vmem,) * 2,
        scratch_shapes=scratch,
        compiler_params=pltpu.CompilerParams(
            vmem_limit_bytes=64 * 2**20, collective_id=0, has_side_effects=True
        ),
    )(
        count.reshape(1).astype(jnp.int32), mixed_came, embedded, cot_kept, cot_came,
        row(out_bias), row(second_gain), row(second_shift), up_bias, row(down_bias),
        row(first_gain), log_total, out_weight, up_weight, down_weight,
        weight_t.reshape(-1, width), packed, mixed, whole,
    )
    return (
        out,
        tokens,
        late[0, :96],
        late[1, :96],
        heads.transpose(1, 0, 2),
        late[7, :96],
        late[8, :96],
        square,
        early[2, :96],
        early[0, :96],
        early[1, :96],
        up,
        early[4:7].reshape(-1),
        down,
        early[3, :96],
        late[2:7, :96],
    )


def both(left, right):
    return (left.astype(F32) + right.astype(F32)).astype(BF16)


def halve(value, axis, bit):
    mine = (lax.axis_index(axis) // bit) % 2
    pairs = value.reshape((value.shape[0] // 2, 2) + value.shape[1:])
    kept = lax.dynamic_index_in_dim(pairs, mine, 1, keepdims=False)
    away = lax.dynamic_index_in_dim(pairs, 1 - mine, 1, keepdims=False)
    return both(kept, swap(away, axis, bit))


def over_owners(value):
    bit = 1
    while bit < lax.axis_size("dp"):
        value = halve(value, "dp", bit)
        bit *= 2
    return value[0]


def total_share(value):
    count = value.shape[1] // 2
    seq = lax.axis_index("head") // 2
    first = over_owners(value[:, :count])
    first = both(first, swap(first, "head", 2))
    second = jnp.swapaxes(value[:, count:].reshape(value.shape[0], 2, -1, value.shape[2]), 0, 1)
    kept = lax.dynamic_index_in_dim(second, seq, 0, keepdims=False)
    away = lax.dynamic_index_in_dim(second, 1 - seq, 0, keepdims=False)
    second = over_owners(both(kept, swap(away, "head", 2)))
    other = swap(second, "head", 2)
    low_part = jnp.where(seq == 0, second, other)
    high_part = jnp.where(seq == 0, other, second)
    return jnp.concatenate([first, low_part, high_part], axis=0)


def on_device(
    tokens,
    passes,
    first_gain,
    first_shift,
    heads_weight,
    query_bias,
    value_bias,
    output_weight,
    output_bias,
    second_gain,
    second_shift,
    upward_weight,
    upward_bias,
    downward_weight,
    downward_bias,
    pass_embed,
    cotangent,
):
    owners = lax.axis_size("dp")
    _, rows, width = tokens.shape
    hidden = upward_weight.shape[1]
    half = width // 2
    full = 4 * rows
    place = lax.axis_index("head")
    core, seq = place % 2, place // 2
    count = lax.dynamic_index_in_dim(passes, seq, 0, keepdims=False)
    scalars = jnp.stack([core, seq, count]).astype(jnp.int32)

    def pick(array, index, axis=0):
        return lax.dynamic_index_in_dim(array, index, axis, keepdims=False)

    tokens_came = swap(pick(tokens, 1 - seq), "head", 2)
    cot_came = swap(pick(cotangent, 1 - seq), "head", 2)
    row = lambda vector: vector.reshape(1, -1)
    weight_t = heads_weight.transpose(1, 2, 0).reshape(2, 3 * half, width)
    weight_own = pick(weight_t, core)
    bias_table = jnp.concatenate(
        [
            query_bias.reshape(HEADS, HEAD),
            jnp.zeros((HEADS, HEAD), F32),
            value_bias.reshape(HEADS, HEAD),
        ],
        axis=1,
    ).reshape(2, 1, 3 * half)
    bias_own = pick(bias_table, core)

    embedded, normed = call(
        embed_kernel,
        [((2 * rows, width), F32), ((2 * rows, width), BF16)],
        (
            scalars,
            pick(tokens, seq),
            tokens_came,
            pass_embed,
            row(first_gain),
            row(first_shift),
        ),
        moved=10 * 2**20,
    )
    normed_came = swap(normed, "head", 1)
    whole, packed, mixed, mixed_kept, mixed_away, log_total = call(
        forward_kernel,
        [
            ((full, width), BF16),
            ((full, 3 * half), BF16),
            ((full, half), BF16),
            ((2 * rows, half), BF16),
            ((2 * rows, half), BF16),
            ((HEADS // 4, 2, full), F32),
        ],
        (scalars, normed, normed_came, weight_own, bias_own),
        moved=70 * 2**20,
    )
    mixed_came = swap(mixed_away, "head", 1)
    if owners == 8 and (rows, width, hidden) == (320, 768, 3072):
        return fused_tail(
            count, mixed_came, embedded, pick(cotangent, seq), cot_came, output_bias,
            second_gain, second_shift, upward_bias, downward_bias, first_gain, log_total,
            output_weight, upward_weight, downward_weight, weight_t, packed, mixed, whole,
        )
    up_rows, down_rows = width // owners, hidden // owners
    out_kept, out_away, middle_grad, mg_kept, mg_away, grads, row_sums, up_sums = call(
        feed_kernel,
        [
            ((rows, width), BF16),
            ((rows, width), BF16),
            ((2 * rows, width), F32),
            ((2 * rows, half), BF16),
            ((2 * rows, half), BF16),
            ((2, owners, 5 * up_rows + down_rows, half), BF16),
            ((8, width), F32),
            ((1, hidden), F32),
        ],
        (
            scalars,
            mixed_kept,
            mixed_came,
            embedded,
            pick(cotangent, seq),
            cot_came,
            output_weight,
            row(output_bias),
            row(second_gain),
            row(second_shift),
            upward_weight,
            row(upward_bias),
            downward_weight,
            row(downward_bias),
        ),
        scratch=[
            ((2 * rows, width), BF16),
            ((2 * rows, width), F32),
            ((2 * rows, width), BF16),
            ((width, 2 * rows), BF16),
            ((2 * rows, width), BF16),
            ((2 * rows, width), F32),
            ((2 * rows, width), F32),
        ],
        moved=120 * 2**20,
    )
    mg_came = swap(mg_away, "head", 1)
    out_came = swap(out_away, "head", 2)
    share = both(pick(grads, core), swap(pick(grads, 1 - core), "head", 1))
    inner_kept, inner_away, heads_grad, bias_sums = call(
        backward_kernel,
        [
            ((2 * rows, width), F32),
            ((2 * rows, width), BF16),
            ((owners, 3 * up_rows, half), BF16),
            ((1, 3 * half), F32),
        ],
        (
            scalars,
            packed,
            log_total,
            mixed_kept,
            mixed_away,
            mg_kept,
            mg_came,
            whole,
            weight_own,
        ),
        scratch=[
            ((full, half), BF16),
            ((full, half), BF16),
            ((full, 3 * half), BF16),
            ((full, width), F32),
            ((2, full, 2 * HEAD), F32),
        ],
        moved=100 * 2**20,
    )
    inner_came = swap(inner_away, "head", 1)
    grad_kept, grad_away, sums = call(
        input_kernel,
        [((rows, width), F32), ((rows, width), BF16), ((8, width), F32)],
        (scalars, inner_kept, inner_came, embedded, middle_grad, row(first_gain)),
        moved=10 * 2**20,
    )
    grad_came = swap(grad_away, "head", 2).astype(F32)

    def place_rows(kept, came):
        return jnp.stack([jnp.where(seq == 0, kept, came), jnp.where(seq == 0, came, kept)])

    bias_parts = jnp.where(
        (jnp.arange(2) == core)[:, None], bias_sums, 0.0
    ).reshape(HEADS, 3, HEAD)
    vectors = jnp.concatenate(
        [
            sums[:7],
            row_sums[:4],
            bias_parts[:, 0].reshape(1, width),
            bias_parts[:, 2].reshape(1, width),
            up_sums.reshape(-1, width // owners, owners).reshape(-1, width),
        ],
        axis=0,
    )
    vectors = lax.psum(vectors, ("dp", "head"))
    owner = lax.axis_index("dp")
    mine = lax.dynamic_slice_in_dim(vectors[:13], owner * up_rows, up_rows, 1)
    up_mine = lax.dynamic_slice_in_dim(vectors[13:].reshape(-1), owner * down_rows, down_rows, 0)

    share = total_share(share)
    share = jnp.stack([share, swap(share, "head", 1)])
    heads_share = total_share(heads_grad)
    heads_share = jnp.stack([heads_share, swap(heads_share, "head", 1)])
    share = jnp.where(core == 0, share, share[::-1]).astype(F32)
    heads_share = jnp.where(core == 0, heads_share, heads_share[::-1]).astype(F32)
    up_share = share[:, : 4 * up_rows].reshape(8, up_rows, half)
    up_share = up_share.transpose(1, 0, 2).reshape(up_rows, hidden)
    down_share = share[:, 4 * up_rows : 4 * up_rows + down_rows]
    down_share = down_share.transpose(1, 0, 2).reshape(down_rows, width)
    out_share = share[:, 4 * up_rows + down_rows :].transpose(1, 0, 2).reshape(up_rows, width)
    heads_share = heads_share.reshape(6, up_rows, half).transpose(1, 0, 2)
    heads_share = heads_share.reshape(up_rows, HEADS, 3 * HEAD)
    return (
        place_rows(out_kept, out_came),
        place_rows(grad_kept, grad_came),
        mine[0],
        mine[1],
        heads_share,
        mine[11],
        mine[12],
        out_share,
        mine[9],
        mine[7],
        mine[8],
        up_share,
        up_mine,
        down_share,
        mine[10],
        mine[2:7],
    )


def solution(mesh):
    rows_spec = P("dp", "head", None)
    in_specs = (rows_spec, P("dp")) + (P(),) * 14 + (rows_spec,)
    out_specs = (
        rows_spec,
        rows_spec,
        P("dp"),
        P("dp"),
        P("dp", None, None),
        P("dp"),
        P("dp"),
        P("dp", None),
        P("dp"),
        P("dp"),
        P("dp"),
        P("dp", None),
        P("dp"),
        P("dp", None),
        P("dp"),
        P(None, "dp"),
    )
    return jax.shard_map(
        on_device, mesh=mesh, in_specs=in_specs, out_specs=out_specs, check_vma=False
    )
```

```python
import functools

import jax
import jax.numpy as jnp
from jax import lax
from jax.experimental import pallas as pl
from jax.experimental.pallas import tpu as pltpu
from jax.sharding import PartitionSpec as P

HEADS = 12
HEAD = 64
BASE = 256
PASSES = 5
NEG_FILL = -1e30
EPSILON = 1e-05
TANH_IN = 0.7978845608028654
TANH_CUBE = 0.044715
F32 = jnp.float32
BF16 = jnp.bfloat16
VMEM_LIMIT = 60 * 2**20


def dot(left, right):
    return jnp.dot(left, right, preferred_element_type=F32)


def dot_nt(left, right):
    return lax.dot_general(
        left, right, (((1,), (1,)), ((), ())), preferred_element_type=F32
    )


def dot_tn(left, right):
    return lax.dot_general(
        left, right, (((0,), (0,)), ((), ())), preferred_element_type=F32
    )


def row_mean(block):
    return jnp.mean(block, axis=1, keepdims=True)


def col_sum(block):
    return jnp.sum(block, axis=0, keepdims=True)


def normalize(block):
    centre = block - row_mean(block)
    scale = lax.rsqrt(row_mean(centre * centre) + EPSILON)
    return centre * scale, scale


def places_of(block_id, core, half, rows):
    start = (block_id * half + core) * rows
    return start + lax.broadcasted_iota(jnp.int32, (rows, 1), 0)


def embed_kernel(scalars, kept, came, table, gain, shift, embedded, normed):
    core, seq, count = scalars[0], scalars[1], scalars[2]
    rows = kept.shape[0]
    for block_id in range(2):
        section = lax.rem(places_of(block_id, core, 2, rows), count)
        mine = kept[...].astype(F32)
        other = came[...].astype(F32)
        hidden = jnp.where(seq == block_id, mine, other)
        added = jnp.zeros_like(hidden)
        for section_id in range(PASSES):
            added = jnp.where(section == section_id, table[section_id : section_id + 1, :], added)
        hidden = hidden + added
        span = pl.ds(block_id * rows, rows)
        embedded[span, :] = hidden
        unit, _ = normalize(hidden)
        normed[span, :] = (unit * gain[...] + shift[...]).astype(BF16)


def gather_rows(core, kept, came, whole):
    rows = kept.shape[0] // 2
    for block_id in range(2):
        span = slice(block_id * rows, (block_id + 1) * rows)
        whole[pl.ds(pl.multiple_of((block_id * 2 + core) * rows, 64), rows), :] = kept[span, :]
        whole[pl.ds(pl.multiple_of((block_id * 2 + 1 - core) * rows, 64), rows), :] = came[span, :]


def split_rows(core, whole, kept, away):
    rows = kept.shape[0] // 2
    for block_id in range(2):
        span = slice(block_id * rows, (block_id + 1) * rows)
        kept[span, :] = whole[
            pl.ds(pl.multiple_of((block_id * 2 + core) * rows, 64), rows), :
        ].astype(kept.dtype)
        away[span, :] = whole[
            pl.ds(pl.multiple_of((block_id * 2 + 1 - core) * rows, 64), rows), :
        ].astype(away.dtype)


def head_parts(block, which):
    start = 3 * HEAD * which
    queries = block[:, start : start + HEAD] * jnp.asarray(HEAD**-0.5, BF16)
    keys = block[:, start + HEAD : start + 2 * HEAD]
    values = block[:, start + 2 * HEAD : start + 3 * HEAD]
    return queries, keys, values


def causal_block(size):
    key_place = lax.broadcasted_iota(jnp.int32, (size, size), 0)
    query_place = lax.broadcasted_iota(jnp.int32, (size, size), 1)
    return key_place <= query_place


def forward_kernel(
    scalars, kept, came, weight, bias, whole, packed, mixed, mixed_kept, mixed_away, log_total
):
    core = scalars[0]
    full = whole.shape[0]
    gather_rows(core, kept, came, whole)
    for start in range(0, full, BASE):
        span = pl.ds(start, BASE)
        packed[span, :] = (dot_nt(whole[span, :], weight[...]) + bias[...]).astype(BF16)
    visible = causal_block(BASE)

    def pair(index, carry):
        block = packed[:, pl.ds(pl.multiple_of(index * 6 * HEAD, 128), 6 * HEAD)]
        results, logs = [], []
        for which in range(2):
            queries, keys, values = head_parts(block, which)
            values_ext = jnp.concatenate([values.T, jnp.ones((16, full), BF16)], axis=0)
            outs, totals = [], []
            for start in range(0, full, BASE):
                end = start + BASE
                scores = dot_nt(keys[:end], queries[start:end])
                last = jnp.where(visible, scores[start:], NEG_FILL)
                scores = last if start == 0 else jnp.concatenate([scores[:start], last], axis=0)
                top = jnp.max(scores, axis=0, keepdims=True)
                raised = jnp.exp(scores - top).astype(BF16)
                grown = dot(values_ext[:, :end], raised)
                total = grown[HEAD : HEAD + 1]
                outs.append(grown[:HEAD] / total)
                totals.append(top + jnp.log(total))
            results.append(jnp.concatenate(outs, axis=1))
            logs.append(jnp.concatenate(totals, axis=1))
        mixed[:, pl.ds(pl.multiple_of(index * 2 * HEAD, 128), 2 * HEAD)] = jnp.concatenate(
            results, axis=0
        ).T.astype(BF16)
        log_total[index] = jnp.concatenate(logs, axis=0)
        return carry

    lax.fori_loop(0, HEADS // 4, pair, 0)
    split_rows(core, mixed, mixed_kept, mixed_away)


def feed_kernel(
    scalars,
    mixed_kept,
    mixed_came,
    embedded,
    cot_kept,
    cot_came,
    out_weight,
    out_bias,
    gain,
    shift,
    up_weight,
    up_bias,
    down_weight,
    down_bias,
    out_kept,
    out_away,
    middle_grad,
    mixed_grad_kept,
    mixed_grad_away,
    grads,
    row_sums,
    up_sums,
    mixed,
    middle,
    normed,
    normed_t,
    out_grad,
    branch,
    normed_grad,
):
    core, seq, count = scalars[0], scalars[1], scalars[2]
    total_rows, width = middle.shape
    rows = total_rows // 2
    half = width // 2
    hidden = up_weight.shape[1]
    owners = grads.shape[1]
    up_rows = width // owners
    down_rows = hidden // owners
    mixed[:, pl.ds(pl.multiple_of(core * half, 128), half)] = mixed_kept[...]
    mixed[:, pl.ds(pl.multiple_of((1 - core) * half, 128), half)] = mixed_came[...]
    valid = []
    for block_id in range(2):
        span = slice(block_id * rows, (block_id + 1) * rows)
        value = embedded[span, :] + dot(mixed[span, :], out_weight[...]) + out_bias[...]
        middle[span, :] = value
        unit, _ = normalize(value)
        normed[span, :] = (unit * gain[...] + shift[...]).astype(BF16)
        keep = places_of(block_id, core, 2, rows) < count * BASE
        valid.append(keep)
        cot = jnp.where(seq == block_id, cot_kept[...].astype(F32), cot_came[...].astype(F32))
        out_grad[span, :] = jnp.where(keep, cot, 0.0).astype(BF16)
    normed_t[...] = normed[...].T
    branch[...] = jnp.zeros_like(branch)
    normed_grad[...] = jnp.zeros_like(normed_grad)
    tile = 2 * half
    for step in range(hidden // tile):
        cols = pl.ds(step * tile, tile)
        value = dot(normed[...], up_weight[:, cols]) + up_bias[:, cols]
        square = value * value
        tanh = jnp.tanh(value * (TANH_IN + TANH_IN * TANH_CUBE * square))
        gate = 0.5 + 0.5 * tanh
        activated = (value * gate).astype(BF16)
        slope = gate + (0.5 * value) * (1.0 - tanh * tanh) * (
            TANH_IN + 3.0 * TANH_IN * TANH_CUBE * square
        )
        up_grad = (dot_nt(out_grad[...], down_weight[cols, :]) * slope).astype(BF16)
        branch[...] += dot(activated, down_weight[cols, :])
        normed_grad[...] += dot_nt(up_grad, up_weight[:, cols])
        up_sums[:, cols] = col_sum(up_grad.astype(F32))
        up_part = dot(normed_t[...], up_grad).astype(BF16)
        down_part = dot_tn(activated, out_grad[...]).astype(BF16)
        for sub in range(2):
            slot = (step * 2 + sub) % 4
            side = (step * 2 + sub) // 4
            for owner in range(owners):
                grads[side, owner, slot * up_rows : (slot + 1) * up_rows, :] = up_part[
                    owner * up_rows : (owner + 1) * up_rows, sub * half : (sub + 1) * half
                ]
        for owner in range(owners):
            first = max(owner * down_rows, step * tile)
            last = min((owner + 1) * down_rows, (step + 1) * tile)
            if first < last:
                place = 4 * up_rows + first - owner * down_rows
                for side in range(2):
                    grads[side, owner, place : place + last - first, :] = down_part[
                        first - step * tile : last - step * tile, side * half : (side + 1) * half
                    ]
    sums = [0.0] * 4
    for block_id in range(2):
        span = slice(block_id * rows, (block_id + 1) * rows)
        value = middle[span, :]
        unit, scale = normalize(value)
        inner = normed_grad[span, :]
        scaled = inner * gain[...]
        cot = out_grad[span, :].astype(F32)
        grad = cot + scale * (scaled - row_mean(scaled) - unit * row_mean(scaled * unit))
        middle_grad[span, :] = grad
        low = grad.astype(BF16)
        normed[span, :] = low
        result = jnp.where(
            valid[block_id], value + branch[span, :] + down_bias[...], 0.0
        ).astype(BF16)

        @pl.when(seq == block_id)
        def _():
            out_kept[...] = result

        @pl.when(seq != block_id)
        def _():
            out_away[...] = result

        mixed_grad_kept[span, :] = dot_nt(
            low, out_weight[pl.ds(pl.multiple_of(core * half, 128), half), :]
        ).astype(BF16)
        mixed_grad_away[span, :] = dot_nt(
            low, out_weight[pl.ds(pl.multiple_of((1 - core) * half, 128), half), :]
        ).astype(BF16)
        terms = (inner * unit, inner, low.astype(F32), cot)
        sums = [have + col_sum(term) for have, term in zip(sums, terms)]
    row_sums[...] = jnp.concatenate(sums + [jnp.zeros((4, width), F32)], axis=0)
    out_part = dot_tn(mixed[...], normed[...]).astype(BF16)
    base_row = 4 * up_rows + down_rows
    for owner in range(owners):
        for side in range(2):
            grads[side, owner, base_row : base_row + up_rows, :] = out_part[
                owner * up_rows : (owner + 1) * up_rows, side * half : (side + 1) * half
            ]


def backward_kernel(
    scalars,
    packed,
    log_total,
    mixed_kept,
    mixed_away,
    grad_kept,
    grad_came,
    whole,
    weight,
    inner_kept,
    inner_away,
    heads_grad,
    bias_sums,
    mixed,
    mixed_grad,
    packed_grad,
    inner,
    value_key_sum,
):
    core = scalars[0]
    full = whole.shape[0]
    owners = heads_grad.shape[0]
    own_rows = heads_grad.shape[1] // 3
    gather_rows(core, mixed_kept, mixed_away, mixed)
    gather_rows(core, grad_kept, grad_came, mixed_grad)
    visible = causal_block(BASE)

    def pair(index, carry):
        base = pl.multiple_of(index * 6 * HEAD, 128)
        block = packed[:, pl.ds(base, 6 * HEAD)]
        lanes = pl.ds(pl.multiple_of(index * 2 * HEAD, 128), 2 * HEAD)
        both_grad = mixed_grad[:, lanes]
        overlap = both_grad.astype(F32) * mixed[:, lanes].astype(F32)
        parts = []
        for which in range(2):
            queries, keys, values = head_parts(block, which)
            grad = both_grad[:, HEAD * which : HEAD * (which + 1)]
            delta = jnp.sum(
                overlap[:, HEAD * which : HEAD * (which + 1)], axis=1, keepdims=True
            ).T
            logs = log_total[index][which : which + 1]
            keys_t = keys.T
            blank = jnp.zeros_like(queries)
            grad_ext = jnp.concatenate([blank, grad], axis=1)
            queries_ext = jnp.concatenate([queries, blank], axis=1)
            query_parts = []
            for start in range(0, full, BASE):
                end = start + BASE
                span = slice(start, end)
                weights = jnp.exp(dot_nt(keys[:end], queries[span]) - logs[:, span])
                last = jnp.where(visible, weights[start:], 0.0)
                weights = (
                    last if start == 0 else jnp.concatenate([weights[:start], last], axis=0)
                )
                weight_grad = dot_nt(values[:end], grad[span])
                score_grad = (weights * (weight_grad - delta[:, span])).astype(BF16)
                added = dot(weights.astype(BF16), grad_ext[span]) + dot(
                    score_grad, queries_ext[span]
                )
                if start > 0:
                    value_key_sum[which, :start, :] += added[:start]
                value_key_sum[which, start:end, :] = added[start:]
                query_parts.append(dot(keys_t[:, :end], score_grad) * HEAD**-0.5)
            parts += [jnp.concatenate(query_parts, axis=1).T, value_key_sum[which]]
        packed_grad[:, pl.ds(base, 6 * HEAD)] = jnp.concatenate(parts, axis=1).astype(BF16)
        return carry

    lax.fori_loop(0, HEADS // 4, pair, 0)
    low = packed_grad[...]
    bias_sums[...] = col_sum(low.astype(F32))
    for start in range(0, full, BASE):
        inner[pl.ds(start, BASE), :] = dot(packed_grad[pl.ds(start, BASE), :], weight[...])
    split_rows(core, inner, inner_kept, inner_away)
    part = dot_tn(whole[...], low).astype(BF16)
    third = heads_grad.shape[2]
    for owner in range(owners):
        for group in range(3):
            heads_grad[owner, group * own_rows : (group + 1) * own_rows, :] = part[
                owner * own_rows : (owner + 1) * own_rows, group * third : (group + 1) * third
            ]


def input_kernel(
    scalars, inner_kept, inner_came, embedded, middle_grad, gain, grad_kept, grad_away, sums
):
    core, seq, count = scalars[0], scalars[1], scalars[2]
    total_rows, width = embedded.shape
    rows = total_rows // 2
    found = [0.0] * (2 + PASSES)
    for block_id in range(2):
        span = slice(block_id * rows, (block_id + 1) * rows)
        unit, scale = normalize(embedded[span, :])
        inner = inner_kept[span, :] + inner_came[span, :].astype(F32)
        scaled = inner * gain[...]
        grad = middle_grad[span, :] + scale * (
            scaled - row_mean(scaled) - unit * row_mean(scaled * unit)
        )

        @pl.when(seq == block_id)
        def _():
            grad_kept[...] = grad

        @pl.when(seq != block_id)
        def _():
            grad_away[...] = grad.astype(BF16)

        section = lax.rem(places_of(block_id, core, 2, rows), count)
        terms = [inner * unit, inner]
        for section_id in range(PASSES):
            terms.append(jnp.where(section == section_id, grad, 0.0))
        found = [have + col_sum(term) for have, term in zip(found, terms)]
    sums[...] = jnp.concatenate(found + [jnp.zeros((1, width), F32)], axis=0)


MESH = pl.DeviceIdType.MESH

ORDERS = {
    "up0": "x1y2",
    "down0": "yx12",
    "up1": "x12y",
    "down1": "yx12",
    "up2": "1y2x",
    "down2": "x1y2",
    "square": "x12y",
    "heads0": "x12y",
    "heads1": "yx12",
    "heads2": "x12y",
}

PLAN = {
    "u0": ("up0",),
    "d0": ("down0",),
    "h11": ("up0",),
    "u1": ("down0", "up1"),
    "d1": ("down1",),
    "h21": ("up1",),
    "u2": ("up0", "down1", "up2"),
    "d2": ("down0", "down2"),
    "ow": ("up0", "up2", "square", "early"),
    "b0": ("up1", "down2", "out"),
    "a0": ("down1",),
    "b1": ("square",),
    "a1": ("up0", "down0"),
    "w0": ("heads0",),
    "b2": ("up2",),
    "a3": ("up1", "down2"),
    "w1": ("up0", "heads1"),
    "b4": ("down0", "early"),
    "a4": ("down1",),
    "b5": ("up2",),
    "a5": ("up0", "up1"),
    "n0": ("up0", "square", "down2", "early"),
    "w2": ("down0", "heads2"),
    "i0": ("down1", "heads1"),
    "n1": ("up1",),
    "i1": ("up2", "square", "heads0", "late"),
}
ENDING = (
    "up1", "down2", "down0", "down1", "down0", "square", "heads2", "heads0", "down2", "heads1",
    "up2", "heads2", "late", "down1", "heads0", "heads1", "down1", "square", "down2", "up2",
    "square", "heads2", "down2", "heads0", "up2", "heads1", "heads0", "heads2",
)


def add_low(left, right):
    return (left.astype(F32) + right.astype(F32)).astype(BF16)


def main_kernel(
    passes,
    first_gain,
    first_shift,
    query_bias,
    value_bias,
    out_bias,
    second_gain,
    second_shift,
    up_bias,
    down_bias,
    table,
    tokens_in,
    cot_in,
    weight_hbm,
    out_weight_hbm,
    up_weight_hbm,
    down_weight_hbm,
    out_hbm,
    tokens_kept_hbm,
    tokens_came_hbm,
    up_hbm,
    down_hbm,
    square_hbm,
    heads_hbm,
    early_out,
    late_out,
    tokens_land,
    cot_land,
    embedded,
    out_weight,
    whole,
    packed,
    mixed,
    mixed_rows,
    log_total,
    middle_grad,
    mixed_grad,
    mixed_grad_away,
    inner_came,
    out_stage,
    up_parts,
    up_core,
    up_land,
    down_parts,
    down_core,
    down_land,
    square_parts,
    square_core,
    square_land,
    heads_parts,
    heads_land,
    up_final,
    down_final,
    square_final,
    heads_final,
    early,
    early_owners,
    early_total,
    early_heads,
    late,
    late_owners,
    late_total,
    late_heads,
    send_sems,
    recv_sems,
    local_sems,
):
    dp, head = lax.axis_index("dp"), lax.axis_index("head")
    core, seq = head % 2, head // 2
    bit0, bit1, bit2 = dp % 2, (dp // 2) % 2, dp // 4
    far_core, far_seq = 1 - core, 1 - seq
    far0, far1, far2 = 1 - bit0, 1 - bit1, 1 - bit2
    to_core = {"head": head + far_core - core}
    to_seq = {"head": head + 2 * (far_seq - seq)}
    to0 = {"dp": dp + far0 - bit0}
    to1 = {"dp": dp + 2 * (far1 - bit1)}
    to2 = {"dp": dp + 4 * (far2 - bit2)}
    head_peers = [lax.rem(head + step, 4) for step in range(1, 4)]
    dp_peers = [lax.rem(dp + step, 8) for step in range(1, 8)]
    own_half = pl.multiple_of(core * 384, 128)
    far_half = pl.multiple_of(far_core * 384, 128)
    own_starts = [pl.multiple_of((block * 2 + core) * 320, 64) for block in range(2)]
    far_starts = [pl.multiple_of((block * 2 + far_core) * 320, 64) for block in range(2)]
    late_blocks = [far_seq, seq]
    late_own = [pl.multiple_of((block * 2 + core) * 320, 64) for block in late_blocks]
    late_far = [pl.multiple_of((block * 2 + far_core) * 320, 64) for block in late_blocks]
    late_spans = [pl.multiple_of(block * 320, 64) for block in late_blocks]
    owner_base = core * 4
    own_weight = pl.multiple_of(core * 1152, 128)
    own_lanes = [pl.multiple_of(core * 384 + index * 128, 128) for index in range(3)]
    count = passes[seq]
    length = count * BASE
    flat_starts = [pl.multiple_of(block * 320, 64) for block in (seq, far_seq)]
    front_own = [pl.multiple_of((block * 2 + core) * 320, 64) for block in (seq, far_seq)]
    front_far = [pl.multiple_of((block * 2 + far_core) * 320, 64) for block in (seq, far_seq)]
    rows, total_rows, width, half, full, tile = 320, 640, 768, 384, 1280, 1024

    sent = []
    used = [0, 0]

    def view(place):
        if isinstance(place, tuple):
            return place[0].at[place[1:]]
        return place

    class Sent:
        def __init__(self, source, target, device):
            self.parts = (source, target, device, used[0])
            used[0] += 1

        def make(self):
            source, target, device, index = self.parts
            return pltpu.make_async_remote_copy(
                src_ref=view(source),
                dst_ref=view(target),
                send_sem=send_sems.at[index],
                recv_sem=recv_sems.at[index],
                device_id=device,
                device_id_type=MESH,
            )

        def wait_recv(self):
            self.make().wait_recv()

        def wait_send(self):
            self.make().wait_send()

    class Fetched:
        def __init__(self, source, target):
            self.parts = (source, target, used[1])
            used[1] += 1

        def make(self):
            source, target, index = self.parts
            return pltpu.make_async_copy(view(source), view(target), local_sems.at[index])

        def wait(self):
            self.make().wait()

    def send(source, target, device):
        copy = Sent(source, target, device)
        copy.make().start()
        sent.append(copy)
        return copy

    def fetch(source, target):
        copy = Fetched(source, target)
        copy.make().start()
        return copy

    every = slice(None)

    barrier = pltpu.get_barrier_semaphore()
    for peer in head_peers:
        pl.semaphore_signal(barrier, inc=1, device_id={"head": peer}, device_id_type=MESH)
    for peer in dp_peers:
        pl.semaphore_signal(barrier, inc=1, device_id={"dp": peer}, device_id_type=MESH)

    def first_step(parts, at, cored):
        if cored is None:
            return at
        slot = (at[0] % 2,) if at else ()
        copy = send((parts,) + at + (far_core,), (cored,) + slot, to_core)
        yield
        copy.wait_recv()
        place = at + (core,)
        parts[place] = add_low(parts[place], cored[slot] if slot else cored[...])
        return place

    axes = {
        "2": (0, bit2, far2, to2),
        "1": (1, bit1, far1, to1),
        "x": (2, bit0, far0, to0),
        "y": (3, seq, far_seq, to_seq),
    }

    def chain(order, parts, at, cored, land, final):
        lead = at
        if cored is not None:
            lead = yield from first_step(parts, at, cored)
        place = [every] * 4
        for step, letter in enumerate(order):
            axis, own, far, device = axes[letter]
            target = (land[step],) + at
            if step == 3:
                target += (every,) if letter == "y" else (0,)
            source = list(place)
            if letter != "y" or step < 3:
                source[axis], place[axis] = far, own
            copy = send((parts,) + lead + tuple(source), target, device)
            yield
            copy.wait_recv()
            found = add_low(parts[lead + tuple(place)], target[0][target[1:] or ...])
            if step < 3:
                parts[lead + tuple(place)] = found
            elif letter == "y":
                final[at + (core,)] = found
            else:
                final[at + (core, seq)] = found
        if order[3] != "y":
            place = (final,) + at + (core, seq)
            copy = send(place, place, to_seq)
            yield
            copy.wait_recv()
        place = (final,) + at + (core,)
        copy = send(place, place, to_core)
        yield
        copy.wait_recv()
        yield

    def vector_sum(parts, by_owner, total, by_head, result):
        copies = [send((parts, peer), (by_owner, dp), {"dp": peer}) for peer in dp_peers]
        by_owner[dp] = parts[dp]
        yield
        for copy in copies:
            copy.wait_recv()
        found = by_owner[0]
        for place in range(1, 8):
            found = found + by_owner[place]
        total[...] = found
        copies = [send(total, (by_head, head), {"head": peer}) for peer in head_peers]
        by_head[head] = found
        yield
        for copy in copies:
            copy.wait_recv()
        result[...] = by_head[0] + by_head[1] + by_head[2] + by_head[3]
        yield

    class Chain:
        def __init__(self, name, steps):
            self.name, self.steps, self.taken, self.done = name, steps, 0, False

        def step(self):
            with jax.named_scope(f"{self.name}_{self.taken}"):
                self.taken += 1
                if next(self.steps, self) is self:
                    self.done = True

    chains = {}
    for group, parts, cored, land, final in (
        ("up", up_parts, up_core, up_land, up_final),
        ("down", down_parts, down_core, down_land, down_final),
        ("heads", heads_parts, None, heads_land, heads_final),
    ):
        for t in range(3):
            name = f"{group}{t}"
            chains[name] = Chain(name, chain(ORDERS[name], parts, (t,), cored, land, final))
    chains["square"] = Chain(
        "square",
        chain(ORDERS["square"], square_parts, (), square_core, square_land, square_final),
    )
    chains["early"] = Chain(
        "early", vector_sum(early, early_owners, early_total, early_heads, early_out)
    )
    chains["late"] = Chain("late", vector_sum(late, late_owners, late_total, late_heads, late_out))

    def tick(point):
        for name in PLAN.get(point, ()):
            if name == "out":
                out_sent.append(send((out_stage, far_seq), (out_hbm, seq), to_seq))
            else:
                chains[name].step()

    chunk = 32
    chunk_places = lax.broadcasted_iota(jnp.int32, (chunk, 1), 0)
    cot_sent, out_sent, exchanged = [], [], []
    out_fetch = fetch(out_weight_hbm, out_weight)

    def fold(term):
        return jnp.sum(term.reshape(-1, 8, width), axis=0)

    def front_phase(weight, tokens_own, bias):
        weight_fetch = fetch((weight_hbm, pl.ds(own_weight, 1152)), weight)
        own_fetch = fetch((tokens_in, seq), tokens_own)
        with jax.named_scope("barrier"):
            pl.semaphore_wait(barrier, 10)
        came = send((tokens_in, far_seq), tokens_land, to_seq)
        cot_sent.append(send((cot_in, far_seq), cot_land, to_seq))
        gain, shift = first_gain[...].reshape(1, width), first_shift[...].reshape(1, width)
        blank = jnp.zeros((1, HEAD), F32)
        for side in range(2):
            pieces = []
            for place in range(side * 6 * HEAD, (side + 1) * 6 * HEAD, HEAD):
                pieces.append(query_bias[place : place + HEAD].reshape(1, HEAD))
                pieces.append(blank)
                pieces.append(value_bias[place : place + HEAD].reshape(1, HEAD))
            bias[side] = jnp.concatenate(pieces, axis=1)

        def embed(source, order):
            block = (seq, far_seq)[order]
            for step in range(rows // chunk):
                span = slice(step * chunk, (step + 1) * chunk)
                hidden = source[span, :].astype(F32)
                place = (
                    (block * 2 + core) * rows
                    + step * chunk
                    + lax.broadcasted_iota(jnp.int32, (chunk, 1), 0)
                )
                section = lax.rem(place, count)
                added = jnp.zeros_like(hidden)
                for section_id in range(PASSES):
                    added = jnp.where(
                        section == section_id, table[section_id : section_id + 1, :], added
                    )
                hidden = hidden + added
                embedded[pl.ds(pl.multiple_of(flat_starts[order] + step * chunk, 32), chunk), :] = (
                    hidden
                )
                unit, _ = normalize(hidden)
                whole[pl.ds(pl.multiple_of(front_own[order] + step * chunk, 32), chunk), :] = (
                    unit * gain + shift
                ).astype(BF16)
            place = (whole, pl.ds(front_own[order], rows))
            return send(place, place, to_core)

        def project(start):
            span = pl.ds(start, rows)
            packed[span, :] = (dot_nt(whole[span, :], weight[...]) + bias[core]).astype(BF16)

        own_fetch.wait()
        for order, source in enumerate((tokens_own, tokens_land)):
            if order == 1:
                with jax.named_scope("tokens_in"):
                    came.wait_recv()
            with jax.named_scope("embed"):
                copy = embed(source, order)
            if order == 0:
                weight_fetch.wait()
            with jax.named_scope("packed"):
                project(front_own[order])
                copy.wait_recv()
                project(front_far[order])

        visible = causal_block(BASE)
        copies = []
        for index in range(3):
            block = packed[:, index * 384 : (index + 1) * 384]
            results = []
            for which in range(2):
                with jax.named_scope("attend"):
                    queries, keys, values = head_parts(block, which)
                    values_ext = jnp.concatenate([values.T, jnp.ones((16, full), BF16)], axis=0)
                    outs, totals = [], []
                    for start in range(0, full, BASE):
                        end = start + BASE
                        scores = dot_nt(keys[:end], queries[start:end])
                        last = jnp.where(visible, scores[start:], NEG_FILL)
                        scores = (
                            last
                            if start == 0
                            else jnp.concatenate([scores[:start], last], axis=0)
                        )
                        top = jnp.max(scores, axis=0, keepdims=True)
                        raised = jnp.exp(scores - top).astype(BF16)
                        grown = dot(values_ext[:, :end], raised)
                        total = grown[HEAD : HEAD + 1]
                        outs.append(grown[:HEAD] / total)
                        totals.append(top + jnp.log(total))
                    results.append(jnp.concatenate(outs, axis=1))
                    log_total[index, which : which + 1, :] = jnp.concatenate(totals, axis=1)
            lanes = slice(index * 128, (index + 1) * 128)
            mixed[:, lanes] = jnp.concatenate(results, axis=0).T.astype(BF16)
            lanes_out = pl.ds(own_lanes[index], 128)
            for place in range(2):
                copies.append(
                    send(
                        (mixed, pl.ds(far_starts[place], rows), lanes),
                        (mixed_rows, slice(place * rows, (place + 1) * rows), lanes_out),
                        to_core,
                    )
                )
        for place in range(2):
            mixed_rows[place * rows : (place + 1) * rows, pl.ds(own_half, half)] = mixed[
                pl.ds(own_starts[place], rows), :
            ]
        with jax.named_scope("mixed"):
            for copy in copies:
                copy.wait_recv()

    pl.run_scoped(
        front_phase,
        pltpu.VMEM((1152, width), BF16),
        pltpu.VMEM((rows, width), BF16),
        pltpu.VMEM((2, 1, 1152), F32),
    )

    def feed_phase(
        up_weight, down_weight, cot_own, middle, normed, normed_t, out_grad, branch,
        active, up_grads,
    ):
        cot_fetch = fetch((cot_in, seq), cot_own)

        def load(step):
            slot = step % 2
            copies = []
            for group in range(8):
                cols = pl.ds(group * half + step * 128, 128)
                into = pl.ds(group * 128, 128)
                copies.append(fetch((up_weight_hbm, every, cols), (up_weight, slot, every, into)))
                copies.append(fetch((down_weight_hbm, cols), (down_weight, slot, into)))
            return copies

        loads = [load(0), load(1)]
        gain, shift = second_gain[...].reshape(1, width), second_shift[...].reshape(1, width)
        cot_fetch.wait()
        cot_sent[0].wait_recv()
        out_fetch.wait()
        out_bias_row = out_bias[...].reshape(1, width)
        with jax.named_scope("project"):
            for block in range(2):
                span = slice(block * rows, (block + 1) * rows)
                middle[span, :] = (
                    embedded[span, :] + dot(mixed_rows[span, :], out_weight[...]) + out_bias_row
                )
                for step in range(rows // chunk):
                    first = block * rows + step * chunk
                    part = slice(first, first + chunk)
                    unit, _ = normalize(middle[part, :])
                    normed[part, :] = (unit * gain + shift).astype(BF16)
                    inside = slice(step * chunk, (step + 1) * chunk)
                    cot = jnp.where(
                        seq == block,
                        cot_own[inside, :].astype(F32),
                        cot_land[inside, :].astype(F32),
                    )
                    place = (block * 2 + core) * rows + step * chunk + chunk_places
                    out_grad[part, :] = jnp.where(place < length, cot, 0.0).astype(BF16)
            normed_t[...] = normed[...].T
            early[...] = jnp.zeros_like(early)
            late[...] = jnp.zeros_like(late)
        for step in range(3):
            slot = step % 2
            for copy in loads[step]:
                copy.wait()
            bias = up_bias[step]
            for block in range(2):
                span = slice(block * rows, (block + 1) * rows)
                with jax.named_scope("hidden"):
                    value = dot(normed[span, :], up_weight[slot]) + bias
                    square_of = value * value
                    tanh = jnp.tanh(value * (TANH_IN + TANH_IN * TANH_CUBE * square_of))
                    gate = 0.5 + 0.5 * tanh
                    act = (value * gate).astype(BF16)
                    slope = gate + (0.5 * value) * (1.0 - tanh * tanh) * (
                        TANH_IN + 3.0 * TANH_IN * TANH_CUBE * square_of
                    )
                    up_grad = (dot_nt(out_grad[span, :], down_weight[slot]) * slope).astype(BF16)
                    active[span, :] = act
                    up_grads[span, :] = up_grad
                    if step == 0:
                        branch[span, :] = dot(act, down_weight[slot])
                        middle_grad[span, :] = dot_nt(up_grad, up_weight[slot])
                    else:
                        branch[span, :] += dot(act, down_weight[slot])
                        middle_grad[span, :] += dot_nt(up_grad, up_weight[slot])
                tick(f"h{step}{block}")
            if step == 0:
                loads.append(load(2))
            sums = col_sum(up_grads[...].astype(F32))
            for group in range(8):
                early[group, 4 + step : 5 + step, :] = sums[:, group * 128 : (group + 1) * 128]
            with jax.named_scope("up_weight"):
                for side in range(2):
                    up_parts[step, side] = (
                        dot(normed_t[...], up_grads[:, side * 512 : (side + 1) * 512])
                        .astype(BF16)
                        .reshape(2, 2, 2, 2, 48, 512)
                    )
            tick(f"u{step}")
            with jax.named_scope("down_weight"):
                for side in range(2):
                    down_parts[step, side] = (
                        dot_tn(active[...], out_grad[:, side * half : (side + 1) * half])
                        .astype(BF16)
                        .reshape(2, 2, 2, 2, 64, half)
                    )
            tick(f"d{step}")
        down_bias_row = down_bias[...].reshape(1, width)
        sums = [jnp.zeros((8, width), F32)] * 4
        with jax.named_scope("middle_grad"):
            for block in range(2):
                span = slice(block * rows, (block + 1) * rows)
                for step in range(rows // chunk):
                    first = block * rows + step * chunk
                    part = slice(first, first + chunk)
                    value = middle[part, :]
                    unit, scale = normalize(value)
                    inner = middle_grad[part, :]
                    scaled = inner * gain
                    cot = out_grad[part, :].astype(F32)
                    grad = cot + scale * (
                        scaled - row_mean(scaled) - unit * row_mean(scaled * unit)
                    )
                    middle_grad[part, :] = grad
                    low = grad.astype(BF16)
                    normed[part, :] = low
                    place = (block * 2 + core) * rows + step * chunk + chunk_places
                    out_stage[block, step * chunk : (step + 1) * chunk, :] = jnp.where(
                        place < length, value + branch[part, :] + down_bias_row, 0.0
                    ).astype(BF16)
                    terms = (inner * unit, inner, low.astype(F32), cot)
                    sums = [have + fold(term) for have, term in zip(sums, terms)]
                mixed_grad_away[span, :] = dot_nt(
                    normed[span, :], out_weight[pl.ds(far_half, half), :]
                ).astype(BF16)
                exchanged.append(
                    send((mixed_grad_away, span), (mixed_grad, pl.ds(own_starts[block], rows)), to_core)
                )
        tick("mg")
        with jax.named_scope("output_weight"):
            for block in range(2):
                span = slice(block * rows, (block + 1) * rows)
                mixed_grad[pl.ds(own_starts[block], rows), :] = dot_nt(
                    normed[span, :], out_weight[pl.ds(own_half, half), :]
                ).astype(BF16)
            for line, found in enumerate(sums):
                found = col_sum(found)
                for group in range(8):
                    early[group, line : line + 1, :96] = found[:, group * 96 : (group + 1) * 96]
            for side in range(2):
                square_parts[side] = (
                    dot_tn(mixed_rows[...], normed[:, side * half : (side + 1) * half])
                    .astype(BF16)
                    .reshape(2, 2, 2, 2, 48, half)
                )
        tick("ow")

    pl.run_scoped(
        feed_phase,
        pltpu.VMEM((2, width, tile), BF16),
        pltpu.VMEM((2, tile, width), BF16),
        pltpu.VMEM((rows, width), BF16),
        pltpu.VMEM((total_rows, width), F32),
        pltpu.VMEM((total_rows, width), BF16),
        pltpu.VMEM((width, total_rows), BF16),
        pltpu.VMEM((total_rows, width), BF16),
        pltpu.VMEM((total_rows, width), F32),
        pltpu.VMEM((total_rows, tile), BF16),
        pltpu.VMEM((total_rows, tile), BF16),
    )
    out_kept = fetch((out_stage, seq), (out_hbm, seq))

    def back_phase(
        weight, packed_grad, inner_kept, inner_away, value_key_sum, tokens_stage, tokens_away
    ):
        weight_fetch = fetch((weight_hbm, pl.ds(own_weight, 1152)), weight)
        with jax.named_scope("mixed_grad"):
            for copy in exchanged:
                copy.wait_recv()
        visible = causal_block(BASE)

        def attend(index, which, block, both_grad, overlap):
            queries, keys, values = head_parts(block, which)
            grad = both_grad[:, HEAD * which : HEAD * (which + 1)]
            delta = jnp.sum(
                overlap[:, HEAD * which : HEAD * (which + 1)], axis=1, keepdims=True
            ).T
            logs = log_total[index][which : which + 1]
            keys_t = keys.T
            blank = jnp.zeros_like(queries)
            grad_ext = jnp.concatenate([blank, grad], axis=1)
            queries_ext = jnp.concatenate([queries, blank], axis=1)
            query_parts = []
            for start in range(0, full, BASE):
                with jax.named_scope("attend"):
                    end = start + BASE
                    span = slice(start, end)
                    weights = jnp.exp(dot_nt(keys[:end], queries[span]) - logs[:, span])
                    last = jnp.where(visible, weights[start:], 0.0)
                    weights = (
                        last if start == 0 else jnp.concatenate([weights[:start], last], axis=0)
                    )
                    weight_grad = dot_nt(values[:end], grad[span])
                    score_grad = (weights * (weight_grad - delta[:, span])).astype(BF16)
                    added = dot(weights.astype(BF16), grad_ext[span]) + dot(
                        score_grad, queries_ext[span]
                    )
                    if start > 0:
                        value_key_sum[which, :start, :] += added[:start]
                    value_key_sum[which, start:end, :] = added[start:]
                    query_parts.append(dot(keys_t[:, :end], score_grad) * HEAD**-0.5)
                if start == 3 * BASE:
                    tick(f"b{index * 2 + which}")
            return [jnp.concatenate(query_parts, axis=1).T, value_key_sum[which]]

        def heads_weight(index):
            with jax.named_scope("heads_weight"):
                heads_parts[index] = (
                    dot_tn(whole[...], packed_grad[:, index * 384 : (index + 1) * 384])
                    .astype(BF16)
                    .reshape(2, 2, 2, 2, 48, half)
                )
            tick(f"w{index}")

        for index in range(3):
            block = packed[:, index * 384 : (index + 1) * 384]
            both_grad = mixed_grad[:, index * 128 : (index + 1) * 128]
            overlap = both_grad.astype(F32) * mixed[:, index * 128 : (index + 1) * 128].astype(F32)
            parts = []
            for which in range(2):
                parts += attend(index, which, block, both_grad, overlap)
                tick(f"a{index * 2 + which}")
            low = jnp.concatenate(parts, axis=1).astype(BF16)
            packed_grad[:, index * 384 : (index + 1) * 384] = low
            sums = col_sum(low.astype(F32))
            for which in range(2):
                for line in range(2):
                    first = 192 * which + 128 * line
                    piece = sums[:, first : first + 64]
                    place = (index * 2 + which) * 64
                    while place < (index * 2 + which + 1) * 64:
                        group = place // 96
                        stop = min((group + 1) * 96, (index * 2 + which + 1) * 64)
                        offset = place - (index * 2 + which) * 64
                        late[
                            owner_base + group,
                            7 + line : 8 + line,
                            place - group * 96 : stop - group * 96,
                        ] = piece[:, offset : offset + stop - place]
                        place = stop
            if index < 2:
                heads_weight(index)
        weight_fetch.wait()
        gain = first_gain[...].reshape(1, width)
        found = [jnp.zeros((8, width), F32)] * (2 + PASSES)
        copies = []

        def inner_of(order):
            with jax.named_scope("inner"):
                inner_away[order] = dot(
                    packed_grad[pl.ds(late_far[order], rows), :], weight[...]
                ).astype(BF16)
                copies.append(send((inner_away, order), (inner_came, order), to_core))
                inner_kept[order] = dot(packed_grad[pl.ds(late_own[order], rows), :], weight[...])
            tick(f"n{order}")

        def input_of(order, found):
            with jax.named_scope("inner_came"):
                copies[order].wait_recv()
            with jax.named_scope("input"):
                for step in range(rows // chunk):
                    inside = slice(step * chunk, (step + 1) * chunk)
                    part = pl.ds(pl.multiple_of(late_spans[order] + step * chunk, 32), chunk)
                    unit, scale = normalize(embedded[part, :])
                    inner = inner_kept[order, inside, :] + inner_came[order, inside, :].astype(F32)
                    scaled = inner * gain
                    grad = middle_grad[part, :] + scale * (
                        scaled - row_mean(scaled) - unit * row_mean(scaled * unit)
                    )
                    if order == 0:
                        tokens_away[inside, :] = grad.astype(BF16)
                    else:
                        tokens_stage[inside, :] = grad
                    place = (late_blocks[order] * 2 + core) * rows + step * chunk + chunk_places
                    section = lax.rem(place, count)
                    terms = [inner * unit, inner]
                    for section_id in range(PASSES):
                        terms.append(jnp.where(section == section_id, grad, 0.0))
                    found = [have + fold(term) for have, term in zip(found, terms)]
            return found

        inner_of(0)
        heads_weight(2)
        found = input_of(0, found)
        tokens_sent = send(tokens_away, tokens_came_hbm, to_seq)
        tick("i0")
        inner_of(1)
        found = input_of(1, found)
        tokens_kept = fetch(tokens_stage, tokens_kept_hbm)
        for line, value in enumerate(found):
            value = col_sum(value)
            for group in range(8):
                late[group, line : line + 1, :96] = value[:, group * 96 : (group + 1) * 96]
        tick("i1")
        for name in ENDING:
            chains[name].step()
        for each in chains.values():
            while not each.done:
                each.step()
        writes = [
            fetch(up_final, up_hbm),
            fetch(down_final, down_hbm),
            fetch(square_final, square_hbm),
            fetch(heads_final, heads_hbm),
        ]
        with jax.named_scope("tokens"):
            tokens_sent.wait_recv()
        tokens_kept.wait()
        for copy in writes:
            copy.wait()
        out_kept.wait()
        out_sent[0].wait_recv()
        for copy in sent:
            copy.wait_send()

    pl.run_scoped(
        back_phase,
        pltpu.VMEM((1152, width), BF16),
        pltpu.VMEM((full, 1152), BF16),
        pltpu.VMEM((2, rows, width), F32),
        pltpu.VMEM((2, rows, width), BF16),
        pltpu.VMEM((2, full, 2 * HEAD), F32),
        pltpu.VMEM((rows, width), F32),
        pltpu.VMEM((rows, width), BF16),
    )


def swap(value, axis, bit):
    count = lax.axis_size(axis)
    return lax.ppermute(value, axis, [(place, place ^ bit) for place in range(count)])


def call(kernel, out_shapes, args, scratch=(), flops=0, moved=0):
    specs = [pl.BlockSpec(memory_space=pltpu.SMEM)] + [
        pl.BlockSpec(memory_space=pltpu.VMEM) for _ in args[1:]
    ]
    return pl.pallas_call(
        kernel,
        out_shape=tuple(jax.ShapeDtypeStruct(*item) for item in out_shapes),
        in_specs=specs,
        scratch_shapes=[pltpu.VMEM(*item) for item in scratch],
        compiler_params=pltpu.CompilerParams(vmem_limit_bytes=VMEM_LIMIT),
        cost_estimate=pl.CostEstimate(flops=flops, bytes_accessed=moved, transcendentals=0),
    )(*args)


def finish_kernel(
    tokens_kept, tokens_came, out, up_final, down_final, square_final, heads_final, early, late,
    out_result, tokens_result, first_gain, first_shift, heads, query_bias, value_bias, square,
    out_bias, second_gain, second_shift, up, up_bias, down, down_bias, table,
):
    seq = lax.axis_index("head") // 2
    out_result[...] = out[...]
    tokens_result[seq] = tokens_kept[...]
    tokens_result[1 - seq] = tokens_came[...].astype(F32)
    for side in range(2):
        for step in range(3):
            for group in range(4):
                first = (side * 4 + group) * 384 + step * 128
                for part in range(2):
                    up[part * 48 : (part + 1) * 48, first : first + 128] = up_final[
                        step, side, part, :, group * 128 : (group + 1) * 128
                    ].astype(F32)
            for part in range(2):
                first = step * 128 + part * 64
                down[first : first + 64, side * 384 : (side + 1) * 384] = down_final[
                    step, side, part
                ].astype(F32)
        for part in range(2):
            square[part * 48 : (part + 1) * 48, side * 384 : (side + 1) * 384] = square_final[
                side, part
            ].astype(F32)
            for index in range(3):
                for which in range(2):
                    heads[
                        side * 6 + index * 2 + which, part * 48 : (part + 1) * 48, :
                    ] = heads_final[
                        index, side, part, :, which * 192 : (which + 1) * 192
                    ].astype(F32)
    second_gain[...] = early[0, :96]
    second_shift[...] = early[1, :96]
    out_bias[...] = early[2, :96]
    down_bias[...] = early[3, :96]
    up_bias[...] = jnp.concatenate(
        [early[4:5, :], early[5:6, :], early[6:7, :]], axis=1
    ).reshape(384)
    first_gain[...] = late[0, :96]
    first_shift[...] = late[1, :96]
    table[...] = late[2:7, :96]
    query_bias[...] = late[7, :96]
    value_bias[...] = late[8, :96]


def fused_layer(
    tokens, passes, first_gain, first_shift, heads_weight, query_bias, value_bias, output_weight,
    output_bias, second_gain, second_shift, up_weight, up_bias, down_weight, down_bias,
    pass_embed, cotangent,
):
    rows, width, half, full = 320, 768, 384, 1280
    weight_t = heads_weight.transpose(1, 2, 0).reshape(3 * width, width)
    up_bias = up_bias.reshape(8, 3, 128).swapaxes(0, 1).reshape(3, 1, 1024)

    def lands(lead, count, wide):
        return (
            pltpu.VMEM(lead + (2, 2, 2, count, wide), BF16),
            pltpu.VMEM(lead + (2, 2, count, wide), BF16),
            pltpu.VMEM(lead + (2, count, wide), BF16),
            pltpu.VMEM(lead + (2, count, wide), BF16),
        )

    def sums(lines):
        return (
            pltpu.VMEM((8, lines, 128), F32),
            pltpu.VMEM((8, lines, 128), F32),
            pltpu.VMEM((lines, 128), F32),
            pltpu.VMEM((4, lines, 128), F32),
        )

    scratch = (
        pltpu.VMEM((rows, width), BF16),
        pltpu.VMEM((rows, width), BF16),
        pltpu.VMEM((2 * rows, width), F32),
        pltpu.VMEM((width, width), BF16),
        pltpu.VMEM((full, width), BF16),
        pltpu.VMEM((full, 3 * half), BF16),
        pltpu.VMEM((full, half), BF16),
        pltpu.VMEM((2 * rows, width), BF16),
        pltpu.VMEM((3, 2, full), F32),
        pltpu.VMEM((2 * rows, width), F32),
        pltpu.VMEM((full, half), BF16),
        pltpu.VMEM((2 * rows, half), BF16),
        pltpu.VMEM((2, rows, width), BF16),
        pltpu.VMEM((2, rows, width), BF16),
        pltpu.VMEM((3, 2, 2, 2, 2, 2, 48, 512), BF16),
        pltpu.VMEM((2, 2, 2, 2, 2, 48, 512), BF16),
        lands((3,), 48, 512),
        pltpu.VMEM((3, 2, 2, 2, 2, 2, 64, half), BF16),
        pltpu.VMEM((2, 2, 2, 2, 2, 64, half), BF16),
        lands((3,), 64, half),
        pltpu.VMEM((2, 2, 2, 2, 2, 48, half), BF16),
        pltpu.VMEM((2, 2, 2, 2, 48, half), BF16),
        lands((), 48, half),
        pltpu.VMEM((3, 2, 2, 2, 2, 48, half), BF16),
        lands((3,), 48, half),
        pltpu.VMEM((3, 2, 2, 48, 512), BF16),
        pltpu.VMEM((3, 2, 2, 64, half), BF16),
        pltpu.VMEM((2, 2, 48, half), BF16),
        pltpu.VMEM((3, 2, 2, 48, half), BF16),
        *sums(8),
        *sums(16),
        pltpu.SemaphoreType.DMA((112,)),
        pltpu.SemaphoreType.DMA((112,)),
        pltpu.SemaphoreType.DMA((80,)),
    )
    any_space = pl.BlockSpec(memory_space=pl.ANY)
    vmem = pl.BlockSpec(memory_space=pltpu.VMEM)

    def shapes(*items):
        return tuple(jax.ShapeDtypeStruct(*item) for item in items)

    found = pl.pallas_call(
        main_kernel,
        out_shape=shapes(
            ((2, rows, width), BF16),
            ((rows, width), F32),
            ((rows, width), BF16),
            ((3, 2, 2, 48, 512), BF16),
            ((3, 2, 2, 64, half), BF16),
            ((2, 2, 48, half), BF16),
            ((3, 2, 2, 48, half), BF16),
            ((8, 128), F32),
            ((16, 128), F32),
        ),
        in_specs=[pl.BlockSpec(memory_space=pltpu.SMEM)] + [vmem] * 10 + [any_space] * 6,
        out_specs=(any_space,) * 7 + (vmem,) * 2,
        scratch_shapes=scratch,
        compiler_params=pltpu.CompilerParams(
            vmem_limit_bytes=64 * 2**20, collective_id=0, has_side_effects=True
        ),
    )(
        passes, first_gain, first_shift, query_bias, value_bias, output_bias, second_gain,
        second_shift, up_bias, down_bias, pass_embed, tokens, cotangent, weight_t, output_weight,
        up_weight, down_weight,
    )
    out, tokens_kept, tokens_came, up, down, square, heads, early, late = found
    results = pl.pallas_call(
        finish_kernel,
        out_shape=shapes(
            ((2, rows, width), BF16),
            ((2, rows, width), F32),
            ((96,), F32),
            ((96,), F32),
            ((HEADS, 96, 192), F32),
            ((96,), F32),
            ((96,), F32),
            ((96, width), F32),
            ((96,), F32),
            ((96,), F32),
            ((96,), F32),
            ((96, 3072), F32),
            ((384,), F32),
            ((384, width), F32),
            ((96,), F32),
            ((PASSES, 96), F32),
        ),
        compiler_params=pltpu.CompilerParams(vmem_limit_bytes=VMEM_LIMIT),
    )(tokens_kept, tokens_came, out, up, down, square, heads, early, late)
    return results[:4] + (results[4].transpose(1, 0, 2),) + results[5:]


def both(left, right):
    return (left.astype(F32) + right.astype(F32)).astype(BF16)


def halve(value, axis, bit):
    mine = (lax.axis_index(axis) // bit) % 2
    pairs = value.reshape((value.shape[0] // 2, 2) + value.shape[1:])
    kept = lax.dynamic_index_in_dim(pairs, mine, 1, keepdims=False)
    away = lax.dynamic_index_in_dim(pairs, 1 - mine, 1, keepdims=False)
    return both(kept, swap(away, axis, bit))


def over_owners(value):
    bit = 1
    while bit < lax.axis_size("dp"):
        value = halve(value, "dp", bit)
        bit *= 2
    return value[0]


def total_share(value):
    count = value.shape[1] // 2
    seq = lax.axis_index("head") // 2
    first = over_owners(value[:, :count])
    first = both(first, swap(first, "head", 2))
    second = jnp.swapaxes(value[:, count:].reshape(value.shape[0], 2, -1, value.shape[2]), 0, 1)
    kept = lax.dynamic_index_in_dim(second, seq, 0, keepdims=False)
    away = lax.dynamic_index_in_dim(second, 1 - seq, 0, keepdims=False)
    second = over_owners(both(kept, swap(away, "head", 2)))
    other = swap(second, "head", 2)
    low_part = jnp.where(seq == 0, second, other)
    high_part = jnp.where(seq == 0, other, second)
    return jnp.concatenate([first, low_part, high_part], axis=0)


def on_device(
    tokens,
    passes,
    first_gain,
    first_shift,
    heads_weight,
    query_bias,
    value_bias,
    output_weight,
    output_bias,
    second_gain,
    second_shift,
    upward_weight,
    upward_bias,
    downward_weight,
    downward_bias,
    pass_embed,
    cotangent,
):
    owners = lax.axis_size("dp")
    _, rows, width = tokens.shape
    hidden = upward_weight.shape[1]
    half = width // 2
    full = 4 * rows
    if owners == 8 and (rows, width, hidden) == (320, 768, 3072):
        return fused_layer(
            tokens, passes, first_gain, first_shift, heads_weight, query_bias, value_bias,
            output_weight, output_bias, second_gain, second_shift, upward_weight, upward_bias,
            downward_weight, downward_bias, pass_embed, cotangent,
        )
    place = lax.axis_index("head")
    core, seq = place % 2, place // 2
    count = lax.dynamic_index_in_dim(passes, seq, 0, keepdims=False)
    scalars = jnp.stack([core, seq, count]).astype(jnp.int32)

    def pick(array, index, axis=0):
        return lax.dynamic_index_in_dim(array, index, axis, keepdims=False)

    tokens_came = swap(pick(tokens, 1 - seq), "head", 2)
    cot_came = swap(pick(cotangent, 1 - seq), "head", 2)
    row = lambda vector: vector.reshape(1, -1)
    weight_t = heads_weight.transpose(1, 2, 0).reshape(2, 3 * half, width)
    weight_own = pick(weight_t, core)
    bias_table = jnp.concatenate(
        [
            query_bias.reshape(HEADS, HEAD),
            jnp.zeros((HEADS, HEAD), F32),
            value_bias.reshape(HEADS, HEAD),
        ],
        axis=1,
    ).reshape(2, 1, 3 * half)
    bias_own = pick(bias_table, core)

    embedded, normed = call(
        embed_kernel,
        [((2 * rows, width), F32), ((2 * rows, width), BF16)],
        (
            scalars,
            pick(tokens, seq),
            tokens_came,
            pass_embed,
            row(first_gain),
            row(first_shift),
        ),
        moved=10 * 2**20,
    )
    normed_came = swap(normed, "head", 1)
    whole, packed, mixed, mixed_kept, mixed_away, log_total = call(
        forward_kernel,
        [
            ((full, width), BF16),
            ((full, 3 * half), BF16),
            ((full, half), BF16),
            ((2 * rows, half), BF16),
            ((2 * rows, half), BF16),
            ((HEADS // 4, 2, full), F32),
        ],
        (scalars, normed, normed_came, weight_own, bias_own),
        moved=70 * 2**20,
    )
    mixed_came = swap(mixed_away, "head", 1)
    up_rows, down_rows = width // owners, hidden // owners
    out_kept, out_away, middle_grad, mg_kept, mg_away, grads, row_sums, up_sums = call(
        feed_kernel,
        [
            ((rows, width), BF16),
            ((rows, width), BF16),
            ((2 * rows, width), F32),
            ((2 * rows, half), BF16),
            ((2 * rows, half), BF16),
            ((2, owners, 5 * up_rows + down_rows, half), BF16),
            ((8, width), F32),
            ((1, hidden), F32),
        ],
        (
            scalars,
            mixed_kept,
            mixed_came,
            embedded,
            pick(cotangent, seq),
            cot_came,
            output_weight,
            row(output_bias),
            row(second_gain),
            row(second_shift),
            upward_weight,
            row(upward_bias),
            downward_weight,
            row(downward_bias),
        ),
        scratch=[
            ((2 * rows, width), BF16),
            ((2 * rows, width), F32),
            ((2 * rows, width), BF16),
            ((width, 2 * rows), BF16),
            ((2 * rows, width), BF16),
            ((2 * rows, width), F32),
            ((2 * rows, width), F32),
        ],
        moved=120 * 2**20,
    )
    mg_came = swap(mg_away, "head", 1)
    out_came = swap(out_away, "head", 2)
    share = both(pick(grads, core), swap(pick(grads, 1 - core), "head", 1))
    inner_kept, inner_away, heads_grad, bias_sums = call(
        backward_kernel,
        [
            ((2 * rows, width), F32),
            ((2 * rows, width), BF16),
            ((owners, 3 * up_rows, half), BF16),
            ((1, 3 * half), F32),
        ],
        (
            scalars,
            packed,
            log_total,
            mixed_kept,
            mixed_away,
            mg_kept,
            mg_came,
            whole,
            weight_own,
        ),
        scratch=[
            ((full, half), BF16),
            ((full, half), BF16),
            ((full, 3 * half), BF16),
            ((full, width), F32),
            ((2, full, 2 * HEAD), F32),
        ],
        moved=100 * 2**20,
    )
    inner_came = swap(inner_away, "head", 1)
    grad_kept, grad_away, sums = call(
        input_kernel,
        [((rows, width), F32), ((rows, width), BF16), ((8, width), F32)],
        (scalars, inner_kept, inner_came, embedded, middle_grad, row(first_gain)),
        moved=10 * 2**20,
    )
    grad_came = swap(grad_away, "head", 2).astype(F32)

    def place_rows(kept, came):
        return jnp.stack([jnp.where(seq == 0, kept, came), jnp.where(seq == 0, came, kept)])

    bias_parts = jnp.where(
        (jnp.arange(2) == core)[:, None], bias_sums, 0.0
    ).reshape(HEADS, 3, HEAD)
    vectors = jnp.concatenate(
        [
            sums[:7],
            row_sums[:4],
            bias_parts[:, 0].reshape(1, width),
            bias_parts[:, 2].reshape(1, width),
            up_sums.reshape(-1, width // owners, owners).reshape(-1, width),
        ],
        axis=0,
    )
    vectors = lax.psum(vectors, ("dp", "head"))
    owner = lax.axis_index("dp")
    mine = lax.dynamic_slice_in_dim(vectors[:13], owner * up_rows, up_rows, 1)
    up_mine = lax.dynamic_slice_in_dim(vectors[13:].reshape(-1), owner * down_rows, down_rows, 0)

    share = total_share(share)
    share = jnp.stack([share, swap(share, "head", 1)])
    heads_share = total_share(heads_grad)
    heads_share = jnp.stack([heads_share, swap(heads_share, "head", 1)])
    share = jnp.where(core == 0, share, share[::-1]).astype(F32)
    heads_share = jnp.where(core == 0, heads_share, heads_share[::-1]).astype(F32)
    up_share = share[:, : 4 * up_rows].reshape(8, up_rows, half)
    up_share = up_share.transpose(1, 0, 2).reshape(up_rows, hidden)
    down_share = share[:, 4 * up_rows : 4 * up_rows + down_rows]
    down_share = down_share.transpose(1, 0, 2).reshape(down_rows, width)
    out_share = share[:, 4 * up_rows + down_rows :].transpose(1, 0, 2).reshape(up_rows, width)
    heads_share = heads_share.reshape(6, up_rows, half).transpose(1, 0, 2)
    heads_share = heads_share.reshape(up_rows, HEADS, 3 * HEAD)
    return (
        place_rows(out_kept, out_came),
        place_rows(grad_kept, grad_came),
        mine[0],
        mine[1],
        heads_share,
        mine[11],
        mine[12],
        out_share,
        mine[9],
        mine[7],
        mine[8],
        up_share,
        up_mine,
        down_share,
        mine[10],
        mine[2:7],
    )


def solution(mesh):
    rows_spec = P("dp", "head", None)
    in_specs = (rows_spec, P("dp")) + (P(),) * 14 + (rows_spec,)
    out_specs = (
        rows_spec,
        rows_spec,
        P("dp"),
        P("dp"),
        P("dp", None, None),
        P("dp"),
        P("dp"),
        P("dp", None),
        P("dp"),
        P("dp"),
        P("dp"),
        P("dp", None),
        P("dp"),
        P("dp", None),
        P("dp"),
        P(None, "dp"),
    )
    return jax.shard_map(
        on_device, mesh=mesh, in_specs=in_specs, out_specs=out_specs, check_vma=False
    )
```

```python
import functools

import jax
import jax.numpy as jnp
from jax import lax
from jax.experimental import pallas as pl
from jax.experimental.pallas import tpu as pltpu
from jax.sharding import PartitionSpec as P

HEADS = 12
HEAD = 64
BASE = 256
PASSES = 5
NEG_FILL = -1e30
EPSILON = 1e-05
TANH_IN = 0.7978845608028654
TANH_CUBE = 0.044715
F32 = jnp.float32
BF16 = jnp.bfloat16
VMEM_LIMIT = 60 * 2**20


def dot(left, right):
    return jnp.dot(left, right, preferred_element_type=F32)


def dot_nt(left, right):
    return lax.dot_general(
        left, right, (((1,), (1,)), ((), ())), preferred_element_type=F32
    )


def dot_tn(left, right):
    return lax.dot_general(
        left, right, (((0,), (0,)), ((), ())), preferred_element_type=F32
    )


def row_mean(block):
    return jnp.mean(block, axis=1, keepdims=True)


def col_sum(block):
    return jnp.sum(block, axis=0, keepdims=True)


def normalize(block):
    centre = block - row_mean(block)
    scale = lax.rsqrt(row_mean(centre * centre) + EPSILON)
    return centre * scale, scale


def places_of(block_id, core, half, rows):
    start = (block_id * half + core) * rows
    return start + lax.broadcasted_iota(jnp.int32, (rows, 1), 0)


def embed_kernel(scalars, kept, came, table, gain, shift, embedded, normed):
    core, seq, count = scalars[0], scalars[1], scalars[2]
    rows = kept.shape[0]
    for block_id in range(2):
        section = lax.rem(places_of(block_id, core, 2, rows), count)
        mine = kept[...].astype(F32)
        other = came[...].astype(F32)
        hidden = jnp.where(seq == block_id, mine, other)
        added = jnp.zeros_like(hidden)
        for section_id in range(PASSES):
            added = jnp.where(section == section_id, table[section_id : section_id + 1, :], added)
        hidden = hidden + added
        span = pl.ds(block_id * rows, rows)
        embedded[span, :] = hidden
        unit, _ = normalize(hidden)
        normed[span, :] = (unit * gain[...] + shift[...]).astype(BF16)


def gather_rows(core, kept, came, whole):
    rows = kept.shape[0] // 2
    for block_id in range(2):
        span = slice(block_id * rows, (block_id + 1) * rows)
        whole[pl.ds(pl.multiple_of((block_id * 2 + core) * rows, 64), rows), :] = kept[span, :]
        whole[pl.ds(pl.multiple_of((block_id * 2 + 1 - core) * rows, 64), rows), :] = came[span, :]


def split_rows(core, whole, kept, away):
    rows = kept.shape[0] // 2
    for block_id in range(2):
        span = slice(block_id * rows, (block_id + 1) * rows)
        kept[span, :] = whole[
            pl.ds(pl.multiple_of((block_id * 2 + core) * rows, 64), rows), :
        ].astype(kept.dtype)
        away[span, :] = whole[
            pl.ds(pl.multiple_of((block_id * 2 + 1 - core) * rows, 64), rows), :
        ].astype(away.dtype)


def head_parts(block, which):
    start = 3 * HEAD * which
    queries = block[:, start : start + HEAD] * jnp.asarray(HEAD**-0.5, BF16)
    keys = block[:, start + HEAD : start + 2 * HEAD]
    values = block[:, start + 2 * HEAD : start + 3 * HEAD]
    return queries, keys, values


def causal_block(size):
    key_place = lax.broadcasted_iota(jnp.int32, (size, size), 0)
    query_place = lax.broadcasted_iota(jnp.int32, (size, size), 1)
    return key_place <= query_place


def forward_kernel(
    scalars, kept, came, weight, bias, whole, packed, mixed, mixed_kept, mixed_away, log_total
):
    core = scalars[0]
    full = whole.shape[0]
    gather_rows(core, kept, came, whole)
    for start in range(0, full, BASE):
        span = pl.ds(start, BASE)
        packed[span, :] = (dot_nt(whole[span, :], weight[...]) + bias[...]).astype(BF16)
    visible = causal_block(BASE)

    def pair(index, carry):
        block = packed[:, pl.ds(pl.multiple_of(index * 6 * HEAD, 128), 6 * HEAD)]
        results, logs = [], []
        for which in range(2):
            queries, keys, values = head_parts(block, which)
            values_ext = jnp.concatenate([values.T, jnp.ones((16, full), BF16)], axis=0)
            outs, totals = [], []
            for start in range(0, full, BASE):
                end = start + BASE
                scores = dot_nt(keys[:end], queries[start:end])
                last = jnp.where(visible, scores[start:], NEG_FILL)
                scores = last if start == 0 else jnp.concatenate([scores[:start], last], axis=0)
                top = jnp.max(scores, axis=0, keepdims=True)
                raised = jnp.exp(scores - top).astype(BF16)
                grown = dot(values_ext[:, :end], raised)
                total = grown[HEAD : HEAD + 1]
                outs.append(grown[:HEAD] / total)
                totals.append(top + jnp.log(total))
            results.append(jnp.concatenate(outs, axis=1))
            logs.append(jnp.concatenate(totals, axis=1))
        mixed[:, pl.ds(pl.multiple_of(index * 2 * HEAD, 128), 2 * HEAD)] = jnp.concatenate(
            results, axis=0
        ).T.astype(BF16)
        log_total[index] = jnp.concatenate(logs, axis=0)
        return carry

    lax.fori_loop(0, HEADS // 4, pair, 0)
    split_rows(core, mixed, mixed_kept, mixed_away)


def feed_kernel(
    scalars,
    mixed_kept,
    mixed_came,
    embedded,
    cot_kept,
    cot_came,
    out_weight,
    out_bias,
    gain,
    shift,
    up_weight,
    up_bias,
    down_weight,
    down_bias,
    out_kept,
    out_away,
    middle_grad,
    mixed_grad_kept,
    mixed_grad_away,
    grads,
    row_sums,
    up_sums,
    mixed,
    middle,
    normed,
    normed_t,
    out_grad,
    branch,
    normed_grad,
):
    core, seq, count = scalars[0], scalars[1], scalars[2]
    total_rows, width = middle.shape
    rows = total_rows // 2
    half = width // 2
    hidden = up_weight.shape[1]
    owners = grads.shape[1]
    up_rows = width // owners
    down_rows = hidden // owners
    mixed[:, pl.ds(pl.multiple_of(core * half, 128), half)] = mixed_kept[...]
    mixed[:, pl.ds(pl.multiple_of((1 - core) * half, 128), half)] = mixed_came[...]
    valid = []
    for block_id in range(2):
        span = slice(block_id * rows, (block_id + 1) * rows)
        value = embedded[span, :] + dot(mixed[span, :], out_weight[...]) + out_bias[...]
        middle[span, :] = value
        unit, _ = normalize(value)
        normed[span, :] = (unit * gain[...] + shift[...]).astype(BF16)
        keep = places_of(block_id, core, 2, rows) < count * BASE
        valid.append(keep)
        cot = jnp.where(seq == block_id, cot_kept[...].astype(F32), cot_came[...].astype(F32))
        out_grad[span, :] = jnp.where(keep, cot, 0.0).astype(BF16)
    normed_t[...] = normed[...].T
    branch[...] = jnp.zeros_like(branch)
    normed_grad[...] = jnp.zeros_like(normed_grad)
    tile = 2 * half
    for step in range(hidden // tile):
        cols = pl.ds(step * tile, tile)
        value = dot(normed[...], up_weight[:, cols]) + up_bias[:, cols]
        square = value * value
        tanh = jnp.tanh(value * (TANH_IN + TANH_IN * TANH_CUBE * square))
        gate = 0.5 + 0.5 * tanh
        activated = (value * gate).astype(BF16)
        slope = gate + (0.5 * value) * (1.0 - tanh * tanh) * (
            TANH_IN + 3.0 * TANH_IN * TANH_CUBE * square
        )
        up_grad = (dot_nt(out_grad[...], down_weight[cols, :]) * slope).astype(BF16)
        branch[...] += dot(activated, down_weight[cols, :])
        normed_grad[...] += dot_nt(up_grad, up_weight[:, cols])
        up_sums[:, cols] = col_sum(up_grad.astype(F32))
        up_part = dot(normed_t[...], up_grad).astype(BF16)
        down_part = dot_tn(activated, out_grad[...]).astype(BF16)
        for sub in range(2):
            slot = (step * 2 + sub) % 4
            side = (step * 2 + sub) // 4
            for owner in range(owners):
                grads[side, owner, slot * up_rows : (slot + 1) * up_rows, :] = up_part[
                    owner * up_rows : (owner + 1) * up_rows, sub * half : (sub + 1) * half
                ]
        for owner in range(owners):
            first = max(owner * down_rows, step * tile)
            last = min((owner + 1) * down_rows, (step + 1) * tile)
            if first < last:
                place = 4 * up_rows + first - owner * down_rows
                for side in range(2):
                    grads[side, owner, place : place + last - first, :] = down_part[
                        first - step * tile : last - step * tile, side * half : (side + 1) * half
                    ]
    sums = [0.0] * 4
    for block_id in range(2):
        span = slice(block_id * rows, (block_id + 1) * rows)
        value = middle[span, :]
        unit, scale = normalize(value)
        inner = normed_grad[span, :]
        scaled = inner * gain[...]
        cot = out_grad[span, :].astype(F32)
        grad = cot + scale * (scaled - row_mean(scaled) - unit * row_mean(scaled * unit))
        middle_grad[span, :] = grad
        low = grad.astype(BF16)
        normed[span, :] = low
        result = jnp.where(
            valid[block_id], value + branch[span, :] + down_bias[...], 0.0
        ).astype(BF16)

        @pl.when(seq == block_id)
        def _():
            out_kept[...] = result

        @pl.when(seq != block_id)
        def _():
            out_away[...] = result

        mixed_grad_kept[span, :] = dot_nt(
            low, out_weight[pl.ds(pl.multiple_of(core * half, 128), half), :]
        ).astype(BF16)
        mixed_grad_away[span, :] = dot_nt(
            low, out_weight[pl.ds(pl.multiple_of((1 - core) * half, 128), half), :]
        ).astype(BF16)
        terms = (inner * unit, inner, low.astype(F32), cot)
        sums = [have + col_sum(term) for have, term in zip(sums, terms)]
    row_sums[...] = jnp.concatenate(sums + [jnp.zeros((4, width), F32)], axis=0)
    out_part = dot_tn(mixed[...], normed[...]).astype(BF16)
    base_row = 4 * up_rows + down_rows
    for owner in range(owners):
        for side in range(2):
            grads[side, owner, base_row : base_row + up_rows, :] = out_part[
                owner * up_rows : (owner + 1) * up_rows, side * half : (side + 1) * half
            ]


def backward_kernel(
    scalars,
    packed,
    log_total,
    mixed_kept,
    mixed_away,
    grad_kept,
    grad_came,
    whole,
    weight,
    inner_kept,
    inner_away,
    heads_grad,
    bias_sums,
    mixed,
    mixed_grad,
    packed_grad,
    inner,
    value_key_sum,
):
    core = scalars[0]
    full = whole.shape[0]
    owners = heads_grad.shape[0]
    own_rows = heads_grad.shape[1] // 3
    gather_rows(core, mixed_kept, mixed_away, mixed)
    gather_rows(core, grad_kept, grad_came, mixed_grad)
    visible = causal_block(BASE)

    def pair(index, carry):
        base = pl.multiple_of(index * 6 * HEAD, 128)
        block = packed[:, pl.ds(base, 6 * HEAD)]
        lanes = pl.ds(pl.multiple_of(index * 2 * HEAD, 128), 2 * HEAD)
        both_grad = mixed_grad[:, lanes]
        overlap = both_grad.astype(F32) * mixed[:, lanes].astype(F32)
        parts = []
        for which in range(2):
            queries, keys, values = head_parts(block, which)
            grad = both_grad[:, HEAD * which : HEAD * (which + 1)]
            delta = jnp.sum(
                overlap[:, HEAD * which : HEAD * (which + 1)], axis=1, keepdims=True
            ).T
            logs = log_total[index][which : which + 1]
            keys_t = keys.T
            blank = jnp.zeros_like(queries)
            grad_ext = jnp.concatenate([blank, grad], axis=1)
            queries_ext = jnp.concatenate([queries, blank], axis=1)
            query_parts = []
            for start in range(0, full, BASE):
                end = start + BASE
                span = slice(start, end)
                weights = jnp.exp(dot_nt(keys[:end], queries[span]) - logs[:, span])
                last = jnp.where(visible, weights[start:], 0.0)
                weights = (
                    last if start == 0 else jnp.concatenate([weights[:start], last], axis=0)
                )
                weight_grad = dot_nt(values[:end], grad[span])
                score_grad = (weights * (weight_grad - delta[:, span])).astype(BF16)
                added = dot(weights.astype(BF16), grad_ext[span]) + dot(
                    score_grad, queries_ext[span]
                )
                if start > 0:
                    value_key_sum[which, :start, :] += added[:start]
                value_key_sum[which, start:end, :] = added[start:]
                query_parts.append(dot(keys_t[:, :end], score_grad) * HEAD**-0.5)
            parts += [jnp.concatenate(query_parts, axis=1).T, value_key_sum[which]]
        packed_grad[:, pl.ds(base, 6 * HEAD)] = jnp.concatenate(parts, axis=1).astype(BF16)
        return carry

    lax.fori_loop(0, HEADS // 4, pair, 0)
    low = packed_grad[...]
    bias_sums[...] = col_sum(low.astype(F32))
    for start in range(0, full, BASE):
        inner[pl.ds(start, BASE), :] = dot(packed_grad[pl.ds(start, BASE), :], weight[...])
    split_rows(core, inner, inner_kept, inner_away)
    part = dot_tn(whole[...], low).astype(BF16)
    third = heads_grad.shape[2]
    for owner in range(owners):
        for group in range(3):
            heads_grad[owner, group * own_rows : (group + 1) * own_rows, :] = part[
                owner * own_rows : (owner + 1) * own_rows, group * third : (group + 1) * third
            ]


def input_kernel(
    scalars, inner_kept, inner_came, embedded, middle_grad, gain, grad_kept, grad_away, sums
):
    core, seq, count = scalars[0], scalars[1], scalars[2]
    total_rows, width = embedded.shape
    rows = total_rows // 2
    found = [0.0] * (2 + PASSES)
    for block_id in range(2):
        span = slice(block_id * rows, (block_id + 1) * rows)
        unit, scale = normalize(embedded[span, :])
        inner = inner_kept[span, :] + inner_came[span, :].astype(F32)
        scaled = inner * gain[...]
        grad = middle_grad[span, :] + scale * (
            scaled - row_mean(scaled) - unit * row_mean(scaled * unit)
        )

        @pl.when(seq == block_id)
        def _():
            grad_kept[...] = grad

        @pl.when(seq != block_id)
        def _():
            grad_away[...] = grad.astype(BF16)

        section = lax.rem(places_of(block_id, core, 2, rows), count)
        terms = [inner * unit, inner]
        for section_id in range(PASSES):
            terms.append(jnp.where(section == section_id, grad, 0.0))
        found = [have + col_sum(term) for have, term in zip(found, terms)]
    sums[...] = jnp.concatenate(found + [jnp.zeros((1, width), F32)], axis=0)


MESH = pl.DeviceIdType.MESH

UP_KIND, DOWN_KIND, SQUARE_KIND, HEADS_KIND = range(4)
Z2, Z1, X, Y = range(4)

(DOWN_0A, DOWN_0B, UP_0A, UP_0B, DOWN_1A, DOWN_1B, UP_1A, UP_1B, DOWN_2A, DOWN_2B, UP_2A, UP_2B,
    SQUARE, HEADS_0, HEADS_1A, HEADS_1B, HEADS_2A, HEADS_2B, VECTORS, OUT) = range(20)
SUMS = {
    DOWN_0A: (DOWN_KIND, 0, 1, (Z1, Z2, Y, X)),
    DOWN_0B: (DOWN_KIND, 0, 2, (Y, Z1, X, Z2)),
    UP_0A: (UP_KIND, 0, 1, (Z1, X, Z2, Y)),
    UP_0B: (UP_KIND, 0, 2, (X, Z1, Z2, Y)),
    DOWN_1A: (DOWN_KIND, 1, 1, (Y, X, Z1, Z2)),
    DOWN_1B: (DOWN_KIND, 1, 2, (X, Z1, Z2, Y)),
    UP_1A: (UP_KIND, 1, 1, (Y, Z1, X, Z2)),
    UP_1B: (UP_KIND, 1, 2, (Z1, X, Z2, Y)),
    DOWN_2A: (DOWN_KIND, 2, 1, (Y, X, Z1, Z2)),
    DOWN_2B: (DOWN_KIND, 2, 2, (X, Z1, Z2, Y)),
    UP_2A: (UP_KIND, 2, 1, (Y, X, Z1, Z2)),
    UP_2B: (UP_KIND, 2, 2, (X, Z1, Z2, Y)),
    SQUARE: (SQUARE_KIND, 0, 0, (Z1, X, Y, Z2)),
    HEADS_0: (HEADS_KIND, 0, 0, (X, Y, Z1, Z2)),
    HEADS_1A: (HEADS_KIND, 1, 1, (X, Z1, Z2, Y)),
    HEADS_1B: (HEADS_KIND, 1, 2, (Y, Z1, Z2, X)),
    HEADS_2A: (HEADS_KIND, 2, 1, (X, Z1, Z2, Y)),
    HEADS_2B: (HEADS_KIND, 2, 2, (X, Z1, Z2, Y)),
}
(AT_HIDDEN_0, AT_DOWN_0, AT_UP_0, AT_BRANCH_0, AT_HIDDEN_1, AT_DOWN_1, AT_UP_1, AT_BRANCH_1,
    AT_HIDDEN_2, AT_DOWN_2, AT_UP_2, AT_BRANCH_2, AT_MIDDLE, AT_SQUARED, AT_HALF_PAIR_0,
    AT_PAIR_0, AT_HEADS_WEIGHT_0, AT_HALF_PAIR_1, AT_PAIR_1, AT_HEADS_WEIGHT_1, AT_HALF_PAIR_2,
    AT_PAIR_2, AT_INNER_0, AT_HEADS_WEIGHT_2, AT_INPUT_0, AT_INNER_1, AT_INPUT_1) = range(27)
PLAN = {
    AT_DOWN_0: (DOWN_0A, DOWN_0B),
    AT_UP_0: (UP_0A, UP_0B),
    AT_BRANCH_0: (DOWN_0A,),
    AT_HIDDEN_1: (DOWN_0B,),
    AT_DOWN_1: (UP_0A, DOWN_1A, DOWN_1B),
    AT_UP_1: (UP_0B, UP_1A, UP_1B),
    AT_BRANCH_1: (DOWN_0A, DOWN_1A),
    AT_HIDDEN_2: (DOWN_0B, DOWN_1B, UP_0A),
    AT_DOWN_2: (UP_1A, UP_0B, DOWN_2A, DOWN_2B),
    AT_UP_2: (UP_1B, UP_2A, UP_2B),
    AT_BRANCH_2: (DOWN_1A, DOWN_0A, DOWN_0B, DOWN_2A),
    AT_MIDDLE: (OUT, DOWN_1B, UP_0B, DOWN_2B, UP_1A),
    AT_SQUARED: (UP_0A, UP_2A, DOWN_0A, SQUARE),
    AT_HALF_PAIR_0: (UP_2B, DOWN_1A, UP_1B, DOWN_0B, DOWN_1B, DOWN_2A, SQUARE),
    AT_PAIR_0: (UP_0B, UP_1A, DOWN_2B, DOWN_0A, DOWN_1A, UP_0A),
    AT_HEADS_WEIGHT_0: (DOWN_0B, UP_2B, HEADS_0),
    AT_HALF_PAIR_1: (DOWN_1B, UP_1B),
    AT_PAIR_1: (DOWN_2A, UP_1A, SQUARE),
    AT_HEADS_WEIGHT_1: (UP_2A, DOWN_2B, UP_0B, DOWN_1A, DOWN_0A, HEADS_1A, HEADS_1B),
    AT_HALF_PAIR_2: (UP_0A, UP_2B, DOWN_0B, UP_0B, DOWN_0A, DOWN_1B, HEADS_0, DOWN_1A, DOWN_2A,
        UP_1B),
    AT_PAIR_2: (UP_1A, HEADS_1B, UP_0A, SQUARE, DOWN_0B, DOWN_1B, DOWN_1A, DOWN_2B),
    AT_INNER_0: (UP_2A, HEADS_0, UP_2B, UP_1B, DOWN_2A),
    AT_HEADS_WEIGHT_2: (UP_1A, HEADS_1B, HEADS_2A, HEADS_2B),
    AT_INPUT_0: (SQUARE, UP_1B, HEADS_1A),
    AT_INNER_1: (UP_2A, DOWN_2B, UP_1A, UP_2B, HEADS_0, DOWN_2A),
    AT_INPUT_1: (HEADS_1B, VECTORS),
}
ENDING = (DOWN_2B, UP_2B, SQUARE, DOWN_2A, HEADS_2A, HEADS_1A, HEADS_2B, UP_2A, HEADS_1B, HEADS_0,
    VECTORS, HEADS_2A, HEADS_1A, HEADS_2B, SQUARE, UP_2A, HEADS_2A, HEADS_1B, HEADS_0, HEADS_2B,
    SQUARE, UP_2A, HEADS_1B, HEADS_1A, HEADS_0, VECTORS, HEADS_2A, HEADS_2B, HEADS_1A, HEADS_2A,
    HEADS_2B)

SENDS, RECEIVES, FETCHES = 37, 127, 17


def add_low(left, right):
    return (left.astype(F32) + right.astype(F32)).astype(BF16)


def main_kernel(
    passes,
    first_gain,
    first_shift,
    query_bias,
    value_bias,
    out_bias,
    second_gain,
    second_shift,
    up_bias,
    down_bias,
    table,
    tokens_in,
    cot_in,
    weight_hbm,
    out_weight_hbm,
    up_weight_hbm,
    down_weight_hbm,
    out_hbm,
    tokens_kept_hbm,
    tokens_came_hbm,
    up_hbm,
    down_hbm,
    square_hbm,
    heads_hbm,
    vectors_out,
    landed,
    embedded,
    out_weight,
    up_weight,
    down_weight,
    whole,
    packed,
    mixed,
    mixed_rows,
    log_total,
    middle_grad,
    mixed_grad,
    mixed_grad_away,
    up_parts,
    up_core,
    up_land,
    down_parts,
    down_core,
    down_land,
    square_parts,
    square_core,
    square_land,
    heads_parts,
    heads_land,
    up_final,
    down_final,
    square_final,
    heads_final,
    vectors,
    vector_owners,
    vector_total,
    vector_heads,
    send_sems,
    recv_sems,
    local_sems,
):
    dp, head = lax.axis_index("dp"), lax.axis_index("head")
    core, seq = head % 2, head // 2
    bit0, bit1, bit2 = dp % 2, (dp // 2) % 2, dp // 4
    far_core, far_seq = 1 - core, 1 - seq
    far0, far1, far2 = 1 - bit0, 1 - bit1, 1 - bit2
    to_core = {"head": head + far_core - core}
    to_seq = {"head": head + 2 * (far_seq - seq)}
    to0 = {"dp": dp + far0 - bit0}
    to1 = {"dp": dp + 2 * (far1 - bit1)}
    to2 = {"dp": dp + 4 * (far2 - bit2)}
    head_peers = [lax.rem(head + step, 4) for step in range(1, 4)]
    dp_peers = [lax.rem(dp + step, 8) for step in range(1, 8)]
    own_half = pl.multiple_of(core * 384, 128)
    far_half = pl.multiple_of(far_core * 384, 128)
    own_starts = [pl.multiple_of((block * 2 + core) * 320, 64) for block in range(2)]
    far_starts = [pl.multiple_of((block * 2 + far_core) * 320, 64) for block in range(2)]
    late_blocks = [far_seq, seq]
    late_own = [pl.multiple_of((block * 2 + core) * 320, 64) for block in late_blocks]
    late_far = [pl.multiple_of((block * 2 + far_core) * 320, 64) for block in late_blocks]
    late_spans = [pl.multiple_of(block * 320, 64) for block in late_blocks]
    owner_base = core * 4
    out_slots = [1 - seq, seq]
    own_weight = pl.multiple_of(core * 1152, 128)
    own_lanes = [pl.multiple_of(core * 384 + index * 128, 128) for index in range(3)]
    count = passes[seq]
    length = count * BASE
    own_second = pl.multiple_of((far_seq * 2 + core) * 320 + 160, 32)
    flat_starts = [pl.multiple_of(block * 320, 64) for block in (seq, far_seq)]
    front_own = [pl.multiple_of((block * 2 + core) * 320, 64) for block in (seq, far_seq)]
    front_far = [pl.multiple_of((block * 2 + far_core) * 320, 64) for block in (seq, far_seq)]
    rows, total_rows, width, half, full, tile = 320, 640, 768, 384, 1280, 1024

    sent = []
    used = [0, 0, 0]

    def view(place):
        if isinstance(place, tuple):
            return place[0].at[place[1:]]
        return place

    groups = {}

    def place_of(kind, group):
        if group is None:
            used[kind] += 1
            return used[kind] - 1
        if (kind, group) not in groups:
            groups[kind, group] = used[kind]
            used[kind] += 1
        return groups[kind, group]

    class Sent:
        def __init__(self, source, target, device, out_group, in_group):
            self.out_place = place_of(0, out_group) if out_group != "" else 0
            self.in_place = place_of(1, in_group) if in_group != "" else 0
            self.parts = (source, target, device)
            self.left = False

        def make(self):
            source, target, device = self.parts
            return pltpu.make_async_remote_copy(
                src_ref=view(source),
                dst_ref=view(target),
                send_sem=send_sems.at[self.out_place],
                recv_sem=recv_sems.at[self.in_place],
                device_id=device,
                device_id_type=MESH,
            )

        def wait_recv(self):
            self.make().wait_recv()

        def wait_send(self):
            if not self.left:
                self.make().wait_send()
            self.left = True

    class Fetched:
        def __init__(self, source, target, group):
            self.parts = (source, target, place_of(2, group))

        def make(self):
            source, target, place = self.parts
            return pltpu.make_async_copy(view(source), view(target), local_sems.at[place])

        def wait(self):
            self.make().wait()

    def send(source, target, device, out_group=None, in_group=None):
        copy = Sent(source, target, device, out_group, in_group)
        copy.make().start()
        if out_group is None:
            sent.append(copy)
        return copy

    def wait_out(group, place):
        Sent(place, place, to_core, group, "").wait_send()

    def wait_in(group, place):
        Sent(place, place, to_core, "", group).wait_recv()

    def fetch(source, target, group=None):
        copy = Fetched(source, target, group)
        copy.make().start()
        return copy

    def wait_fetched(group, place):
        Fetched(place, place, group).wait()

    every = slice(None)

    barrier = pltpu.get_barrier_semaphore()
    for peer in head_peers:
        pl.semaphore_signal(barrier, inc=1, device_id={"head": peer}, device_id_type=MESH)
    for peer in dp_peers:
        pl.semaphore_signal(barrier, inc=1, device_id={"dp": peer}, device_id_type=MESH)

    def first_step(name, parts, at, cored, tail):
        if cored is None:
            return at
        slot = (at[0] % 2,) if at else ()
        rest = (every,) * 4 + tail
        copy = send((parts,) + at + (far_core,) + rest, (cored,) + slot + rest, to_core, name)
        yield
        copy.wait_recv()
        place = at + (core,)
        parts[place + rest] = add_low(parts[place + rest], cored[slot + rest])
        return place

    axes = (
        (bit2, far2, to2),
        (bit1, far1, to1),
        (bit0, far0, to0),
        (seq, far_seq, to_seq),
    )

    def chain(name, kind, order, parts, at, cored, land, final, tail=()):
        lead = yield from first_step(name, parts, at, cored, tail)
        place = [every] * 4
        for step, axis in enumerate(order):
            own, far, device = axes[axis]
            remaining = (every,) * (3 - step) if step < 3 else (every if axis == Y else 0,)
            target = (land[step],) + at + remaining + tail
            source = list(place)
            if axis != Y or step < 3:
                source[axis], place[axis] = far, own
            copy = send((parts,) + lead + tuple(source) + tail, target, device, name)
            yield
            copy.wait_recv()
            found = add_low(parts[lead + tuple(place) + tail], target[0][target[1:]])
            if step < 3:
                parts[lead + tuple(place) + tail] = found
            elif axis == Y:
                final[at + (core, every) + tail] = found
            else:
                final[at + (core, seq) + tail] = found
        if order[3] != Y:
            place = (final,) + at + (core, seq) + tail
            copy = send(place, place, to_seq, name)
            yield
            copy.wait_recv()
        place = (final,) + at + (core, every) + tail
        copy = send(place, place, to_core, (kind,))
        yield
        copy.wait_recv()

    def vector_sum(parts, by_owner, total, by_head, result):
        for peer in dp_peers:
            send((parts, peer), (by_owner, dp), {"dp": peer}, "owners", "owners")
        by_owner[dp] = parts[dp]
        yield
        wait_in("owners", (by_owner, slice(0, 7)))
        found = by_owner[0]
        for place in range(1, 8):
            found = found + by_owner[place]
        total[...] = found
        for peer in head_peers:
            send(total, (by_head, head), {"head": peer}, "heads_sum", "heads_sum")
        by_head[head] = found
        yield
        wait_in("heads_sum", (by_head, slice(0, 3)))
        result[...] = by_head[0] + by_head[1] + by_head[2] + by_head[3]

    class Chain:
        def __init__(self, name, steps, group=None):
            self.name, self.steps, self.group = name, steps, group
            self.taken, self.done = 0, False

        def step(self):
            with jax.named_scope(f"sum{self.name}_{self.taken}"):
                self.taken += 1
                if next(self.steps, self) is self:
                    self.done = True
                    if self.group:
                        kind, final, result, _ = self.group
                        left[kind] -= 1
                        if left[kind] == 0:
                            writes.append(fetch(final, result))

    chains, left, writes = {}, {}, []
    arrays = (
        (up_parts, up_core, up_land, up_final, up_hbm),
        (down_parts, down_core, down_land, down_final, down_hbm),
        (square_parts, square_core, square_land, square_final, square_hbm),
        (heads_parts, None, heads_land, heads_final, heads_hbm),
    )
    for name, (kind, part, side, order) in SUMS.items():
        at = () if kind == SQUARE_KIND else (part,)
        parts, cored, land, final, result = arrays[kind]
        tail = ()
        if side > 0:
            if kind == DOWN_KIND:
                tail = (slice(0, 32) if side == 1 else slice(32, 64),)
            else:
                tail = (every, slice(0, 256) if side == 1 else slice(256, parts.shape[-1]))
        steps = chain(name, kind, order, parts, at, cored, land, final, tail)
        whole_of = (parts,) + at + (every,) * (4 if cored is None else 5) + tail
        chains[name] = Chain(name, steps, (kind, final, result, whole_of))
        left[kind] = left.get(kind, 0) + 1
    chains[VECTORS] = Chain(
        VECTORS, vector_sum(vectors, vector_owners, vector_total, vector_heads, vectors_out)
    )

    def tick(point):
        for name in PLAN.get(point, ()):
            if name == OUT:
                out_sent.append(send((landed, 0), (out_hbm, seq), to_seq))
            else:
                chains[name].step()

    chunk = 32
    chunk_places = lax.broadcasted_iota(jnp.int32, (chunk, 1), 0)
    cot_sent, out_sent = [], []
    out_fetch = fetch(out_weight_hbm, out_weight)

    def fold(term):
        return jnp.sum(term.reshape(-1, 8, width), axis=0)

    def load(step):
        slot = step % 2
        for group in range(8):
            cols = pl.ds(group * half + step * 128, 128)
            into = pl.ds(group * 128, 128)
            fetch((up_weight_hbm, every, cols), (up_weight, slot, every, into), (step,))
            fetch((down_weight_hbm, cols), (down_weight, slot, into), (3 + step,))

    def front_phase(weight, tokens_own, bias):
        weight_fetch = fetch((weight_hbm, pl.ds(own_weight, 1152)), weight)
        own_fetch = fetch((tokens_in, seq), tokens_own)
        with jax.named_scope("barrier"):
            pl.semaphore_wait(barrier, 10)
        pieces = (slice(0, rows // 2), slice(rows // 2, rows))

        def send_piece(piece):
            return send((tokens_in, far_seq, piece), (landed, 0, piece), to_seq)

        came = [send_piece(pieces[0])]
        gain, shift = first_gain[...].reshape(1, width), first_shift[...].reshape(1, width)
        blank = jnp.zeros((1, HEAD), F32)
        for side in range(2):
            parts = []
            for place in range(side * 6 * HEAD, (side + 1) * 6 * HEAD, HEAD):
                parts.append(query_bias[place : place + HEAD].reshape(1, HEAD))
                parts.append(blank)
                parts.append(value_bias[place : place + HEAD].reshape(1, HEAD))
            bias[side] = jnp.concatenate(parts, axis=1)

        def local_chunk(order, step):
            return pl.ds(pl.multiple_of(flat_starts[order] + step * chunk, 32), chunk)

        def embed_passes(order):
            block = (seq, far_seq)[order]
            for step in range(rows // chunk):
                place = (block * 2 + core) * rows + step * chunk + chunk_places
                section = lax.rem(place, count)
                added = jnp.zeros((chunk, width), F32)
                for section_id in range(PASSES):
                    added = jnp.where(
                        section == section_id, table[section_id : section_id + 1, :], added
                    )
                embedded[local_chunk(order, step), :] = added

        def embed(source, order, piece):
            for step in range(piece.start // chunk, piece.stop // chunk):
                place = local_chunk(order, step)
                hidden = source[step * chunk : (step + 1) * chunk, :].astype(F32) + embedded[place, :]
                embedded[place, :] = hidden
                unit, _ = normalize(hidden)
                whole[pl.ds(pl.multiple_of(front_own[order] + step * chunk, 32), chunk), :] = (
                    unit * gain + shift
                ).astype(BF16)
            start = front_own[order] if piece.start == 0 else own_second
            place = (whole, pl.ds(start, piece.stop - piece.start))
            return send(place, place, to_core)

        def project(start, piece):
            span = pl.ds(
                pl.multiple_of(start + piece.start, 32), piece.stop - piece.start
            )
            packed[span, :] = (dot_nt(whole[span, :], weight[...]) + bias[core]).astype(BF16)

        with jax.named_scope("embed"):
            embed_passes(0)
            own_fetch.wait()
            copy = embed(tokens_own, 0, slice(0, rows))
            embed_passes(1)
        weight_fetch.wait()
        with jax.named_scope("packed"):
            project(front_own[0], slice(0, rows))
            came[0].wait_send()
            came.append(send_piece(pieces[1]))
            copy.wait_recv()
            project(front_far[0], slice(0, rows))
        load(0)
        load(1)
        for place, piece in enumerate(pieces):
            with jax.named_scope("tokens_in"):
                came[place].wait_recv()
                if place == 1:
                    came[1].wait_send()
                    cot_sent.append(send((cot_in, far_seq), (landed, 1), to_seq))
            with jax.named_scope("embed"):
                copy = embed(landed.at[0], 1, piece)
            with jax.named_scope("packed"):
                project(front_own[1], piece)
                copy.wait_recv()
                project(front_far[1], piece)

        visible = causal_block(BASE)
        queues, results, logs = {}, {}, {}

        def prepare(index):
            block = packed[:, index * 384 : (index + 1) * 384]
            for which in range(2):
                queries, keys, values = head_parts(block, which)
                values_ext = jnp.concatenate([values.T, jnp.ones((16, full), BF16)], axis=0)
                queues[index, which] = (queries, keys, values_ext)
                results[index, which], logs[index, which] = [], []

        def scores_of(place, start):
            queries, keys, _ = queues[place]
            scores = dot_nt(keys[: start + BASE], queries[start : start + BASE])
            last = jnp.where(visible, scores[start:], NEG_FILL)
            return last if start == 0 else jnp.concatenate([scores[:start], last], axis=0)

        def raise_of(scores):
            top = jnp.max(scores, axis=0, keepdims=True)
            return jnp.exp(scores - top).astype(BF16), top

        def gather_of(place, start, raised, top):
            grown = dot(queues[place][2][:, : start + BASE], raised)
            total = grown[HEAD : HEAD + 1]
            results[place].append(grown[:HEAD] / total)
            logs[place].append(top + jnp.log(total))
            index, which = place
            if start + BASE < full:
                return
            log_total[index, which : which + 1, :] = jnp.concatenate(logs[place], axis=1)
            if which == 0:
                return
            lanes = slice(index * 128, (index + 1) * 128)
            mixed[:, lanes] = jnp.concatenate(
                [jnp.concatenate(results[index, each], axis=1) for each in range(2)], axis=0
            ).T.astype(BF16)
            lanes_out = pl.ds(own_lanes[index], 128)
            for block in range(2):
                send(
                    (mixed, pl.ds(far_starts[block], rows), lanes),
                    (mixed_rows, slice(block * rows, (block + 1) * rows), lanes_out),
                    to_core,
                    "mixed",
                    "mixed",
                )

        with jax.named_scope("attend"):
            first = second = None
            for place in [(index, which) for index in range(3) for which in range(2)]:
                for start in range(0, full, BASE):
                    if place[1] == 0 and start == 0:
                        prepare(place[0])
                    scores = scores_of(place, start)
                    raised = raise_of(first[2]) if first else None
                    if second:
                        gather_of(*second)
                    second = first[:2] + raised if first else None
                    first = (place, start, scores)
            raised = raise_of(first[2])
            gather_of(*second)
            gather_of(*(first[:2] + raised))

    pl.run_scoped(
        front_phase,
        pltpu.VMEM((1152, width), BF16),
        pltpu.VMEM((rows, width), BF16),
        pltpu.VMEM((2, 1, 1152), F32),
    )

    def feed_phase(
        middle, normed, normed_t, out_grad, branch,
        active, up_grads,
    ):
        cot_fetch = fetch((cot_in, seq), (out_grad, pl.ds(flat_starts[0], rows)))

        gain, shift = second_gain[...].reshape(1, width), second_shift[...].reshape(1, width)
        out_fetch.wait()
        out_bias_row = out_bias[...].reshape(1, width)
        with jax.named_scope("project"):
            for block in range(2):
                span = slice(block * rows, (block + 1) * rows)
                own = mixed[pl.ds(own_starts[block], rows), :]
                mixed_rows[span, pl.ds(own_half, half)] = own
                middle[span, :] = (
                    embedded[span, :]
                    + dot(own, out_weight[pl.ds(own_half, half), :])
                    + out_bias_row
                )
        with jax.named_scope("mixed"):
            wait_in("mixed", (mixed_rows, every, slice(0, half)))
            cot_fetch.wait()
            cot_sent[0].wait_recv()
        with jax.named_scope("project"):
            for block in range(2):
                span = slice(block * rows, (block + 1) * rows)
                middle[span, :] += dot(
                    mixed_rows[span, pl.ds(far_half, half)], out_weight[pl.ds(far_half, half), :]
                )
                for step in range(rows // chunk):
                    first = block * rows + step * chunk
                    part = slice(first, first + chunk)
                    unit, _ = normalize(middle[part, :])
                    normed[part, :] = (unit * gain + shift).astype(BF16)
                    inside = slice(step * chunk, (step + 1) * chunk)
                    cot = jnp.where(
                        seq == block,
                        out_grad[part, :].astype(F32),
                        landed[1, inside, :].astype(F32),
                    )
                    place = (block * 2 + core) * rows + step * chunk + chunk_places
                    out_grad[part, :] = jnp.where(place < length, cot, 0.0).astype(BF16)
            normed_t[...] = normed[...].T
            vectors[...] = jnp.zeros_like(vectors)
        for step in range(3):
            slot = step % 2
            wait_fetched((step,), (up_weight, slot))
            wait_fetched((3 + step,), (down_weight, slot))
            with jax.named_scope("hidden"):
                def block_of(place):
                    return slice(place * 256, (place + 1) * 256)

                def value_of(place):
                    bias = jnp.concatenate(
                        [
                            up_bias[
                                group * half + step * 128 : group * half + (step + 1) * 128
                            ].reshape(1, 128)
                            for group in (2 * place, 2 * place + 1)
                        ],
                        axis=1,
                    )
                    return dot(normed[...], up_weight[slot, :, block_of(place)]) + bias

                value = value_of(0)
                for place in range(4):
                    later = value_of(place + 1) if place < 3 else None
                    square_of = value * value
                    tanh = jnp.tanh(value * (TANH_IN + TANH_IN * TANH_CUBE * square_of))
                    gate = 0.5 + 0.5 * tanh
                    active[:, block_of(place)] = (value * gate).astype(BF16)
                    slope = gate + (0.5 * value) * (1.0 - tanh * tanh) * (
                        TANH_IN + 3.0 * TANH_IN * TANH_CUBE * square_of
                    )
                    up_grads[:, block_of(place)] = (
                        dot_nt(out_grad[...], down_weight[slot, block_of(place), :]) * slope
                    ).astype(BF16)
                    value = later
            tick(AT_HIDDEN_0 + 4 * step)

            with jax.named_scope("down_weight"):
                for upper in range(2):
                    part = dot_tn(active[:, upper * 512 : (upper + 1) * 512], out_grad[...])
                    for side in range(2):
                        down_parts[step, side, upper] = (
                            part[:, side * half : (side + 1) * half]
                            .astype(BF16)
                            .reshape(2, 2, 2, 64, half)
                        )
            tick(AT_DOWN_0 + 4 * step)
            with jax.named_scope("up_weight"):
                for side in range(2):
                    up_parts[step, side] = (
                        dot(normed_t[...], up_grads[:, side * 512 : (side + 1) * 512])
                        .astype(BF16)
                        .reshape(2, 2, 2, 2, 48, 512)
                    )
            tick(AT_UP_0 + 4 * step)
            with jax.named_scope("branch"):
                for place in range(3):
                    cols = block_of(place)
                    grown = dot(active[...], down_weight[slot, :, cols])
                    returned = dot_nt(up_grads[...], up_weight[slot, cols, :])
                    if step > 0:
                        grown, returned = grown + branch[:, cols], returned + middle_grad[:, cols]
                    branch[:, cols], middle_grad[:, cols] = grown, returned
                sums = col_sum(up_grads[...].astype(F32))
                for group in range(8):
                    vectors[group, 4 + step : 5 + step, :] = sums[:, group * 128 : (group + 1) * 128]
            if step == 0:
                load(2)
            tick(AT_BRANCH_0 + 4 * step)
        down_bias_row = down_bias[...].reshape(1, width)
        sums = [jnp.zeros((8, width), F32)] * 4
        with jax.named_scope("middle_grad"):
            for block in range(2):
                span = slice(block * rows, (block + 1) * rows)
                for step in range(rows // chunk):
                    first = block * rows + step * chunk
                    part = slice(first, first + chunk)
                    value = middle[part, :]
                    unit, scale = normalize(value)
                    inner = middle_grad[part, :]
                    scaled = inner * gain
                    cot = out_grad[part, :].astype(F32)
                    grad = cot + scale * (
                        scaled - row_mean(scaled) - unit * row_mean(scaled * unit)
                    )
                    middle_grad[part, :] = grad
                    low = grad.astype(BF16)
                    normed[part, :] = low
                    place = (block * 2 + core) * rows + step * chunk + chunk_places
                    landed[out_slots[block], step * chunk : (step + 1) * chunk, :] = jnp.where(
                        place < length, value + branch[part, :] + down_bias_row, 0.0
                    ).astype(BF16)
                    terms = (inner * unit, inner, low.astype(F32), cot)
                    sums = [have + fold(term) for have, term in zip(sums, terms)]
                mixed_grad_away[span, :] = dot_nt(
                    normed[span, :], out_weight[pl.ds(far_half, half), :]
                ).astype(BF16)
                send(
                    (mixed_grad_away, span),
                    (mixed_grad, pl.ds(own_starts[block], rows)),
                    to_core,
                    "mixed_grad",
                    "mixed_grad",
                )
        tick(AT_MIDDLE)
        with jax.named_scope("output_weight"):
            for block in range(2):
                span = slice(block * rows, (block + 1) * rows)
                mixed_grad[pl.ds(own_starts[block], rows), :] = dot_nt(
                    normed[span, :], out_weight[pl.ds(own_half, half), :]
                ).astype(BF16)
            for line, found in enumerate(sums):
                found = col_sum(found)
                for group in range(8):
                    vectors[group, line : line + 1, :96] = found[:, group * 96 : (group + 1) * 96]
            for upper in range(2):
                part = dot_tn(mixed_rows[:, upper * half : (upper + 1) * half], normed[...])
                for side in range(2):
                    square_parts[side, upper] = (
                        part[:, side * half : (side + 1) * half]
                        .astype(BF16)
                        .reshape(2, 2, 2, 48, half)
                    )
        tick(AT_SQUARED)

    pl.run_scoped(
        feed_phase,
        pltpu.VMEM((total_rows, width), F32),
        pltpu.VMEM((total_rows, width), BF16),
        pltpu.VMEM((width, total_rows), BF16),
        pltpu.VMEM((total_rows, width), BF16),
        pltpu.VMEM((total_rows, width), F32),
        pltpu.VMEM((total_rows, tile), BF16),
        pltpu.VMEM((total_rows, tile), BF16),
    )
    out_kept = fetch((landed, 1), (out_hbm, seq))

    def back_phase(
        weight, packed_grad, inner_kept, inner_away, value_key_sum, tokens_stage, tokens_away
    ):
        weight_fetch = fetch((weight_hbm, pl.ds(own_weight, 1152)), weight)
        visible = causal_block(BASE)

        def prepare_heads(index):
            block = packed[:, index * 384 : (index + 1) * 384]
            found = []
            for which in range(2):
                queries, keys, values = head_parts(block, which)
                blank = jnp.zeros_like(queries)
                queries_ext = jnp.concatenate([queries, blank], axis=1)
                found.append((queries, keys, values, keys.T, queries_ext))
            return found

        def prepare_grads(index, heads):
            both_grad = mixed_grad[:, index * 128 : (index + 1) * 128]
            overlap = both_grad.astype(F32) * mixed[:, index * 128 : (index + 1) * 128].astype(F32)
            given = []
            for which in range(2):
                queries, keys, values, keys_t, queries_ext = heads[which]
                grad = both_grad[:, HEAD * which : HEAD * (which + 1)]
                delta = jnp.sum(
                    overlap[:, HEAD * which : HEAD * (which + 1)], axis=1, keepdims=True
                ).T
                logs = log_total[index][which : which + 1]
                grad_ext = jnp.concatenate([jnp.zeros_like(grad), grad], axis=1)
                given.append(
                    (queries, keys, values, grad, delta, logs, keys_t, grad_ext, queries_ext)
                )
            return given

        def attend(index, given):
            query_parts = ([], [])
            coming = None

            def begin(which, start):
                queries, keys, values, grad = given[which][:4]
                end = start + BASE
                return (
                    dot_nt(keys[:end], queries[start:end]),
                    dot_nt(values[:end], grad[start:end]),
                )

            def finish(which, start, scores, weight_grad):
                delta, logs, keys_t, grad_ext, queries_ext = given[which][4:]
                end = start + BASE
                span = slice(start, end)
                weights = jnp.exp(scores - logs[:, span])
                last = jnp.where(visible, weights[start:], 0.0)
                weights = (
                    last if start == 0 else jnp.concatenate([weights[:start], last], axis=0)
                )
                score_grad = (weights * (weight_grad - delta[:, span])).astype(BF16)
                added = dot(weights.astype(BF16), grad_ext[span]) + dot(
                    score_grad, queries_ext[span]
                )
                if start > 0:
                    value_key_sum[which, :start, :] += added[:start]
                value_key_sum[which, start:end, :] = added[start:]
                query_parts[which].append(dot(keys_t[:, :end], score_grad) * HEAD**-0.5)

            waiting = None
            for which in range(2):
                for start in range(0, full, BASE):
                    with jax.named_scope("attend"):
                        begun = begin(which, start)
                        if waiting:
                            finish(*waiting)
                        waiting = (which, start) + begun
                    if which == 1 and start == 2 * BASE and index < 2:
                        coming = prepare_grads(index + 1, prepare_heads(index + 1))
                    if which == 1 and start == 0:
                        tick((AT_HALF_PAIR_0, AT_HALF_PAIR_1, AT_HALF_PAIR_2)[index])
            with jax.named_scope("attend"):
                finish(*waiting)
                parts = []
                for which in range(2):
                    parts += [jnp.concatenate(query_parts[which], axis=1).T, value_key_sum[which]]
                low = jnp.concatenate(parts, axis=1).astype(BF16)
                packed_grad[:, index * 384 : (index + 1) * 384] = low
                sums = col_sum(low.astype(F32))
            for which in range(2):
                for line in range(2):
                    first = 192 * which + 128 * line
                    piece = sums[:, first : first + 64]
                    place = (index * 2 + which) * 64
                    while place < (index * 2 + which + 1) * 64:
                        group = place // 96
                        stop = min((group + 1) * 96, (index * 2 + which + 1) * 64)
                        offset = place - (index * 2 + which) * 64
                        vectors[
                            owner_base + group,
                            15 + line : 16 + line,
                            place - group * 96 : stop - group * 96,
                        ] = piece[:, offset : offset + stop - place]
                        place = stop
            tick((AT_PAIR_0, AT_PAIR_1, AT_PAIR_2)[index])
            return coming

        def heads_weight(index):
            with jax.named_scope("heads_weight"):
                heads_parts[index] = (
                    dot_tn(whole[...], packed_grad[:, index * 384 : (index + 1) * 384])
                    .astype(BF16)
                    .reshape(2, 2, 2, 2, 48, half)
                )
            tick((AT_HEADS_WEIGHT_0, AT_HEADS_WEIGHT_1, AT_HEADS_WEIGHT_2)[index])

        with jax.named_scope("prepare"):
            first_heads = prepare_heads(0)
        with jax.named_scope("mixed_grad"):
            wait_in("mixed_grad", mixed_grad_away)
        with jax.named_scope("prepare"):
            given = prepare_grads(0, first_heads)
        for index in range(3):
            given = attend(index, given)
            if index < 2:
                heads_weight(index)
        weight_fetch.wait()
        gain = first_gain[...].reshape(1, width)
        found = [jnp.zeros((8, width), F32)] * (2 + PASSES)
        copies, tokens_sent = [], []

        def inner_of(order):
            with jax.named_scope("inner"):
                inner_away[order] = dot(
                    packed_grad[pl.ds(late_far[order], rows), :], weight[...]
                ).astype(BF16)
                copies.append(send(
                    (inner_away, order),
                    (mixed_rows, slice(order * rows, (order + 1) * rows)),
                    to_core,
                ))
                inner_kept[order] = dot(packed_grad[pl.ds(late_own[order], rows), :], weight[...])
            tick((AT_INNER_0, AT_INNER_1)[order])

        def input_of(order, found):
            with jax.named_scope("inner_came"):
                copies[order].wait_recv()
            with jax.named_scope("input"):
                for step in range(rows // chunk):
                    inside = slice(step * chunk, (step + 1) * chunk)
                    part = pl.ds(pl.multiple_of(late_spans[order] + step * chunk, 32), chunk)
                    unit, scale = normalize(embedded[part, :])
                    inner = inner_kept[order, inside, :] + mixed_rows[
                        order * rows + step * chunk : order * rows + (step + 1) * chunk, :
                    ].astype(F32)
                    scaled = inner * gain
                    grad = middle_grad[part, :] + scale * (
                        scaled - row_mean(scaled) - unit * row_mean(scaled * unit)
                    )
                    if order == 0:
                        tokens_away[inside, :] = grad.astype(BF16)
                        if step % 5 == 4:
                            piece = slice((step - 4) * chunk, (step + 1) * chunk)
                            tokens_sent.append(
                                send((tokens_away, piece), (tokens_came_hbm, piece), to_seq)
                            )
                    else:
                        tokens_stage[inside, :] = grad
                    place = (late_blocks[order] * 2 + core) * rows + step * chunk + chunk_places
                    section = lax.rem(place, count)
                    terms = [inner * unit, inner]
                    for section_id in range(PASSES):
                        terms.append(jnp.where(section == section_id, grad, 0.0))
                    found = [have + fold(term) for have, term in zip(found, terms)]
            return found

        inner_of(0)
        heads_weight(2)
        found = input_of(0, found)
        tick(AT_INPUT_0)
        inner_of(1)
        found = input_of(1, found)
        tokens_kept = fetch(tokens_stage, tokens_kept_hbm)
        for line, value in enumerate(found):
            value = col_sum(value)
            for group in range(8):
                vectors[group, 8 + line : 9 + line, :96] = value[:, group * 96 : (group + 1) * 96]
        tick(AT_INPUT_1)
        for name in ENDING:
            chains[name].step()
        for each in chains.values():
            while not each.done:
                each.step()
        with jax.named_scope("ends"):
            for copy in tokens_sent:
                copy.wait_recv()
            out_sent[0].wait_recv()
            tokens_kept.wait()
            out_kept.wait()
            for copy in sent:
                copy.wait_send()
            wait_out("mixed", (mixed_rows, every, slice(0, half)))
            wait_out("mixed_grad", mixed_grad_away)
            wait_out("owners", (vector_owners, slice(0, 7)))
            wait_out("heads_sum", (vector_heads, slice(0, 3)))
            finals = {}
            for name, each in chains.items():
                if each.group:
                    finals[each.group[0]] = each.group[1]
                    wait_out(name, each.group[3])
            for kind, final in finals.items():
                lead = (core,) if kind == SQUARE_KIND else (every, core)
                wait_out((kind,), (final,) + lead)
            for copy in writes:
                copy.wait()

    pl.run_scoped(
        back_phase,
        pltpu.VMEM((1152, width), BF16),
        pltpu.VMEM((full, 1152), BF16),
        pltpu.VMEM((2, rows, width), F32),
        pltpu.VMEM((2, rows, width), BF16),
        pltpu.VMEM((2, full, 2 * HEAD), F32),
        pltpu.VMEM((rows, width), F32),
        pltpu.VMEM((rows, width), BF16),
    )


def swap(value, axis, bit):
    count = lax.axis_size(axis)
    return lax.ppermute(value, axis, [(place, place ^ bit) for place in range(count)])


def call(kernel, out_shapes, args, scratch=(), flops=0, moved=0):
    specs = [pl.BlockSpec(memory_space=pltpu.SMEM)] + [
        pl.BlockSpec(memory_space=pltpu.VMEM) for _ in args[1:]
    ]
    return pl.pallas_call(
        kernel,
        out_shape=tuple(jax.ShapeDtypeStruct(*item) for item in out_shapes),
        in_specs=specs,
        scratch_shapes=[pltpu.VMEM(*item) for item in scratch],
        compiler_params=pltpu.CompilerParams(vmem_limit_bytes=VMEM_LIMIT),
        cost_estimate=pl.CostEstimate(flops=flops, bytes_accessed=moved, transcendentals=0),
    )(*args)


def finish_kernel(
    tokens_kept, tokens_came, out, up_final, down_final, square_final, heads_final, vectors,
    out_result, tokens_result, first_gain, first_shift, heads, query_bias, value_bias, square,
    out_bias, second_gain, second_shift, up, up_bias, down, down_bias, table,
    came_low, up_low, down_low, square_low, heads_low, out_low, kept_wide,
    came_wide, up_wide, down_wide, square_wide, heads_wide, sems,
):
    seq = lax.axis_index("head") // 2
    pairs = [
        (up_final, up_low),
        (down_final, down_low),
        (tokens_came, came_low),
        (heads_final, heads_low),
        (square_final, square_low),
        (out, out_low),
        (tokens_kept, kept_wide),
        (out_low, out_result),
        (kept_wide, tokens_result.at[seq]),
        (up_wide, up),
        (down_wide, down),
        (came_wide, tokens_result.at[1 - seq]),
        (heads_wide, heads),
        (square_wide, square),
    ]
    copies = [
        pltpu.make_async_copy(source, target, sems.at[place])
        for place, (source, target) in enumerate(pairs)
    ]
    for copy in copies[:7]:
        copy.start()
    copies[0].wait()
    for side in range(2):
        for step in range(3):
            for group in range(4):
                first = (side * 4 + group) * 384 + step * 128
                for part in range(2):
                    up_wide[part * 48 : (part + 1) * 48, first : first + 128] = up_low[
                        step, side, part, :, group * 128 : (group + 1) * 128
                    ].astype(F32)
    copies[9].start()
    copies[1].wait()
    for side in range(2):
        for step in range(3):
            for part in range(2):
                first = step * 128 + part * 64
                down_wide[first : first + 64, side * 384 : (side + 1) * 384] = down_low[
                    step, side, part
                ].astype(F32)
    copies[10].start()
    copies[2].wait()
    came_wide[...] = came_low[...].astype(F32)
    copies[11].start()
    copies[3].wait()
    for side in range(2):
        for part in range(2):
            for index in range(3):
                for which in range(2):
                    heads_wide[
                        side * 6 + index * 2 + which, part * 48 : (part + 1) * 48, :
                    ] = heads_low[
                        index, side, part, :, which * 192 : (which + 1) * 192
                    ].astype(F32)
    copies[12].start()
    copies[4].wait()
    for side in range(2):
        for part in range(2):
            square_wide[part * 48 : (part + 1) * 48, side * 384 : (side + 1) * 384] = square_low[
                side, part
            ].astype(F32)
    copies[13].start()
    for place in (5, 6):
        copies[place].wait()
        copies[place + 2].start()
    second_gain[...] = vectors[0, :96]
    second_shift[...] = vectors[1, :96]
    out_bias[...] = vectors[2, :96]
    down_bias[...] = vectors[3, :96]
    up_bias[...] = jnp.concatenate(
        [vectors[4:5, :], vectors[5:6, :], vectors[6:7, :]], axis=1
    ).reshape(384)
    first_gain[...] = vectors[8, :96]
    first_shift[...] = vectors[9, :96]
    table[...] = vectors[10:15, :96]
    query_bias[...] = vectors[15, :96]
    value_bias[...] = vectors[16, :96]
    for copy in copies[7:]:
        copy.wait()


def fused_layer(
    tokens, passes, first_gain, first_shift, heads_weight, query_bias, value_bias, output_weight,
    output_bias, second_gain, second_shift, up_weight, up_bias, down_weight, down_bias,
    pass_embed, cotangent,
):
    rows, width, half, full = 320, 768, 384, 1280
    weight_t = heads_weight.transpose(1, 2, 0).reshape(3 * width, width)

    def lands(lead, count, wide):
        return (
            pltpu.VMEM(lead + (2, 2, 2, count, wide), BF16),
            pltpu.VMEM(lead + (2, 2, count, wide), BF16),
            pltpu.VMEM(lead + (2, count, wide), BF16),
            pltpu.VMEM(lead + (2, count, wide), BF16),
        )

    def sums(lines):
        return (
            pltpu.VMEM((8, lines, 128), F32),
            pltpu.VMEM((8, lines, 128), F32),
            pltpu.VMEM((lines, 128), F32),
            pltpu.VMEM((4, lines, 128), F32),
        )

    scratch = (
        pltpu.VMEM((2, rows, width), BF16),
        pltpu.VMEM((2 * rows, width), F32),
        pltpu.VMEM((width, width), BF16),
        pltpu.VMEM((2, width, 1024), BF16),
        pltpu.VMEM((2, 1024, width), BF16),
        pltpu.VMEM((full, width), BF16),
        pltpu.VMEM((full, 3 * half), BF16),
        pltpu.VMEM((full, half), BF16),
        pltpu.VMEM((2 * rows, width), BF16),
        pltpu.VMEM((3, 2, full), F32),
        pltpu.VMEM((2 * rows, width), F32),
        pltpu.VMEM((full, half), BF16),
        pltpu.VMEM((2 * rows, half), BF16),
        pltpu.VMEM((3, 2, 2, 2, 2, 2, 48, 512), BF16),
        pltpu.VMEM((2, 2, 2, 2, 2, 48, 512), BF16),
        lands((3,), 48, 512),
        pltpu.VMEM((3, 2, 2, 2, 2, 2, 64, half), BF16),
        pltpu.VMEM((2, 2, 2, 2, 2, 64, half), BF16),
        lands((3,), 64, half),
        pltpu.VMEM((2, 2, 2, 2, 2, 48, half), BF16),
        pltpu.VMEM((2, 2, 2, 2, 48, half), BF16),
        lands((), 48, half),
        pltpu.VMEM((3, 2, 2, 2, 2, 48, half), BF16),
        lands((3,), 48, half),
        pltpu.VMEM((3, 2, 2, 48, 512), BF16),
        pltpu.VMEM((3, 2, 2, 64, half), BF16),
        pltpu.VMEM((2, 2, 48, half), BF16),
        pltpu.VMEM((3, 2, 2, 48, half), BF16),
        *sums(24),
        pltpu.SemaphoreType.DMA((SENDS,)),
        pltpu.SemaphoreType.DMA((RECEIVES,)),
        pltpu.SemaphoreType.DMA((FETCHES,)),
    )
    any_space = pl.BlockSpec(memory_space=pl.ANY)
    vmem = pl.BlockSpec(memory_space=pltpu.VMEM)

    def shapes(*items):
        return tuple(jax.ShapeDtypeStruct(*item) for item in items)

    found = pl.pallas_call(
        main_kernel,
        out_shape=shapes(
            ((2, rows, width), BF16),
            ((rows, width), F32),
            ((rows, width), BF16),
            ((3, 2, 2, 48, 512), BF16),
            ((3, 2, 2, 64, half), BF16),
            ((2, 2, 48, half), BF16),
            ((3, 2, 2, 48, half), BF16),
            ((24, 128), F32),
        ),
        in_specs=[pl.BlockSpec(memory_space=pltpu.SMEM)] + [vmem] * 10 + [any_space] * 6,
        out_specs=(any_space,) * 7 + (vmem,),
        scratch_shapes=scratch,
        compiler_params=pltpu.CompilerParams(
            vmem_limit_bytes=64 * 2**20, collective_id=0, has_side_effects=True
        ),
    )(
        passes, first_gain, first_shift, query_bias, value_bias, output_bias, second_gain,
        second_shift, up_bias, down_bias, pass_embed, tokens, cotangent, weight_t, output_weight,
        up_weight, down_weight,
    )
    out, tokens_kept, tokens_came, up, down, square, heads, vectors = found
    wide = (any_space, any_space, vmem, vmem, any_space, vmem, vmem, any_space)
    results = pl.pallas_call(
        finish_kernel,
        out_shape=shapes(
            ((2, rows, width), BF16),
            ((2, rows, width), F32),
            ((96,), F32),
            ((96,), F32),
            ((HEADS, 96, 192), F32),
            ((96,), F32),
            ((96,), F32),
            ((96, width), F32),
            ((96,), F32),
            ((96,), F32),
            ((96,), F32),
            ((96, 3072), F32),
            ((384,), F32),
            ((384, width), F32),
            ((96,), F32),
            ((PASSES, 96), F32),
        ),
        in_specs=[any_space] * 7 + [vmem],
        out_specs=wide + (vmem, vmem, vmem, any_space, vmem, any_space, vmem, vmem),
        scratch_shapes=[
            pltpu.VMEM((rows, width), BF16),
            pltpu.VMEM((3, 2, 2, 48, 512), BF16),
            pltpu.VMEM((3, 2, 2, 64, half), BF16),
            pltpu.VMEM((2, 2, 48, half), BF16),
            pltpu.VMEM((3, 2, 2, 48, half), BF16),
            pltpu.VMEM((2, rows, width), BF16),
            pltpu.VMEM((rows, width), F32),
            pltpu.VMEM((rows, width), F32),
            pltpu.VMEM((96, 3072), F32),
            pltpu.VMEM((384, width), F32),
            pltpu.VMEM((96, width), F32),
            pltpu.VMEM((HEADS, 96, 192), F32),
            pltpu.SemaphoreType.DMA((14,)),
        ],
        compiler_params=pltpu.CompilerParams(vmem_limit_bytes=VMEM_LIMIT),
    )(tokens_kept, tokens_came, out, up, down, square, heads, vectors)
    return results[:4] + (results[4].transpose(1, 0, 2),) + results[5:]


def both(left, right):
    return (left.astype(F32) + right.astype(F32)).astype(BF16)


def halve(value, axis, bit):
    mine = (lax.axis_index(axis) // bit) % 2
    pairs = value.reshape((value.shape[0] // 2, 2) + value.shape[1:])
    kept = lax.dynamic_index_in_dim(pairs, mine, 1, keepdims=False)
    away = lax.dynamic_index_in_dim(pairs, 1 - mine, 1, keepdims=False)
    return both(kept, swap(away, axis, bit))


def over_owners(value):
    bit = 1
    while bit < lax.axis_size("dp"):
        value = halve(value, "dp", bit)
        bit *= 2
    return value[0]


def total_share(value):
    count = value.shape[1] // 2
    seq = lax.axis_index("head") // 2
    first = over_owners(value[:, :count])
    first = both(first, swap(first, "head", 2))
    second = jnp.swapaxes(value[:, count:].reshape(value.shape[0], 2, -1, value.shape[2]), 0, 1)
    kept = lax.dynamic_index_in_dim(second, seq, 0, keepdims=False)
    away = lax.dynamic_index_in_dim(second, 1 - seq, 0, keepdims=False)
    second = over_owners(both(kept, swap(away, "head", 2)))
    other = swap(second, "head", 2)
    low_part = jnp.where(seq == 0, second, other)
    high_part = jnp.where(seq == 0, other, second)
    return jnp.concatenate([first, low_part, high_part], axis=0)


def on_device(
    tokens,
    passes,
    first_gain,
    first_shift,
    heads_weight,
    query_bias,
    value_bias,
    output_weight,
    output_bias,
    second_gain,
    second_shift,
    upward_weight,
    upward_bias,
    downward_weight,
    downward_bias,
    pass_embed,
    cotangent,
):
    owners = lax.axis_size("dp")
    _, rows, width = tokens.shape
    hidden = upward_weight.shape[1]
    half = width // 2
    full = 4 * rows
    if owners == 8 and (rows, width, hidden) == (320, 768, 3072):
        return fused_layer(
            tokens, passes, first_gain, first_shift, heads_weight, query_bias, value_bias,
            output_weight, output_bias, second_gain, second_shift, upward_weight, upward_bias,
            downward_weight, downward_bias, pass_embed, cotangent,
        )
    place = lax.axis_index("head")
    core, seq = place % 2, place // 2
    count = lax.dynamic_index_in_dim(passes, seq, 0, keepdims=False)
    scalars = jnp.stack([core, seq, count]).astype(jnp.int32)

    def pick(array, index, axis=0):
        return lax.dynamic_index_in_dim(array, index, axis, keepdims=False)

    tokens_came = swap(pick(tokens, 1 - seq), "head", 2)
    cot_came = swap(pick(cotangent, 1 - seq), "head", 2)
    row = lambda vector: vector.reshape(1, -1)
    weight_t = heads_weight.transpose(1, 2, 0).reshape(2, 3 * half, width)
    weight_own = pick(weight_t, core)
    bias_table = jnp.concatenate(
        [
            query_bias.reshape(HEADS, HEAD),
            jnp.zeros((HEADS, HEAD), F32),
            value_bias.reshape(HEADS, HEAD),
        ],
        axis=1,
    ).reshape(2, 1, 3 * half)
    bias_own = pick(bias_table, core)

    embedded, normed = call(
        embed_kernel,
        [((2 * rows, width), F32), ((2 * rows, width), BF16)],
        (
            scalars,
            pick(tokens, seq),
            tokens_came,
            pass_embed,
            row(first_gain),
            row(first_shift),
        ),
        moved=10 * 2**20,
    )
    normed_came = swap(normed, "head", 1)
    whole, packed, mixed, mixed_kept, mixed_away, log_total = call(
        forward_kernel,
        [
            ((full, width), BF16),
            ((full, 3 * half), BF16),
            ((full, half), BF16),
            ((2 * rows, half), BF16),
            ((2 * rows, half), BF16),
            ((HEADS // 4, 2, full), F32),
        ],
        (scalars, normed, normed_came, weight_own, bias_own),
        moved=70 * 2**20,
    )
    mixed_came = swap(mixed_away, "head", 1)
    up_rows, down_rows = width // owners, hidden // owners
    out_kept, out_away, middle_grad, mg_kept, mg_away, grads, row_sums, up_sums = call(
        feed_kernel,
        [
            ((rows, width), BF16),
            ((rows, width), BF16),
            ((2 * rows, width), F32),
            ((2 * rows, half), BF16),
            ((2 * rows, half), BF16),
            ((2, owners, 5 * up_rows + down_rows, half), BF16),
            ((8, width), F32),
            ((1, hidden), F32),
        ],
        (
            scalars,
            mixed_kept,
            mixed_came,
            embedded,
            pick(cotangent, seq),
            cot_came,
            output_weight,
            row(output_bias),
            row(second_gain),
            row(second_shift),
            upward_weight,
            row(upward_bias),
            downward_weight,
            row(downward_bias),
        ),
        scratch=[
            ((2 * rows, width), BF16),
            ((2 * rows, width), F32),
            ((2 * rows, width), BF16),
            ((width, 2 * rows), BF16),
            ((2 * rows, width), BF16),
            ((2 * rows, width), F32),
            ((2 * rows, width), F32),
        ],
        moved=120 * 2**20,
    )
    mg_came = swap(mg_away, "head", 1)
    out_came = swap(out_away, "head", 2)
    share = both(pick(grads, core), swap(pick(grads, 1 - core), "head", 1))
    inner_kept, inner_away, heads_grad, bias_sums = call(
        backward_kernel,
        [
            ((2 * rows, width), F32),
            ((2 * rows, width), BF16),
            ((owners, 3 * up_rows, half), BF16),
            ((1, 3 * half), F32),
        ],
        (
            scalars,
            packed,
            log_total,
            mixed_kept,
            mixed_away,
            mg_kept,
            mg_came,
            whole,
            weight_own,
        ),
        scratch=[
            ((full, half), BF16),
            ((full, half), BF16),
            ((full, 3 * half), BF16),
            ((full, width), F32),
            ((2, full, 2 * HEAD), F32),
        ],
        moved=100 * 2**20,
    )
    inner_came = swap(inner_away, "head", 1)
    grad_kept, grad_away, sums = call(
        input_kernel,
        [((rows, width), F32), ((rows, width), BF16), ((8, width), F32)],
        (scalars, inner_kept, inner_came, embedded, middle_grad, row(first_gain)),
        moved=10 * 2**20,
    )
    grad_came = swap(grad_away, "head", 2).astype(F32)

    def place_rows(kept, came):
        return jnp.stack([jnp.where(seq == 0, kept, came), jnp.where(seq == 0, came, kept)])

    bias_parts = jnp.where(
        (jnp.arange(2) == core)[:, None], bias_sums, 0.0
    ).reshape(HEADS, 3, HEAD)
    vectors = jnp.concatenate(
        [
            sums[:7],
            row_sums[:4],
            bias_parts[:, 0].reshape(1, width),
            bias_parts[:, 2].reshape(1, width),
            up_sums.reshape(-1, width // owners, owners).reshape(-1, width),
        ],
        axis=0,
    )
    vectors = lax.psum(vectors, ("dp", "head"))
    owner = lax.axis_index("dp")
    mine = lax.dynamic_slice_in_dim(vectors[:13], owner * up_rows, up_rows, 1)
    up_mine = lax.dynamic_slice_in_dim(vectors[13:].reshape(-1), owner * down_rows, down_rows, 0)

    share = total_share(share)
    share = jnp.stack([share, swap(share, "head", 1)])
    heads_share = total_share(heads_grad)
    heads_share = jnp.stack([heads_share, swap(heads_share, "head", 1)])
    share = jnp.where(core == 0, share, share[::-1]).astype(F32)
    heads_share = jnp.where(core == 0, heads_share, heads_share[::-1]).astype(F32)
    up_share = share[:, : 4 * up_rows].reshape(8, up_rows, half)
    up_share = up_share.transpose(1, 0, 2).reshape(up_rows, hidden)
    down_share = share[:, 4 * up_rows : 4 * up_rows + down_rows]
    down_share = down_share.transpose(1, 0, 2).reshape(down_rows, width)
    out_share = share[:, 4 * up_rows + down_rows :].transpose(1, 0, 2).reshape(up_rows, width)
    heads_share = heads_share.reshape(6, up_rows, half).transpose(1, 0, 2)
    heads_share = heads_share.reshape(up_rows, HEADS, 3 * HEAD)
    return (
        place_rows(out_kept, out_came),
        place_rows(grad_kept, grad_came),
        mine[0],
        mine[1],
        heads_share,
        mine[11],
        mine[12],
        out_share,
        mine[9],
        mine[7],
        mine[8],
        up_share,
        up_mine,
        down_share,
        mine[10],
        mine[2:7],
    )


def solution(mesh):
    rows_spec = P("dp", "head", None)
    in_specs = (rows_spec, P("dp")) + (P(),) * 14 + (rows_spec,)
    out_specs = (
        rows_spec,
        rows_spec,
        P("dp"),
        P("dp"),
        P("dp", None, None),
        P("dp"),
        P("dp"),
        P("dp", None),
        P("dp"),
        P("dp"),
        P("dp"),
        P("dp", None),
        P("dp"),
        P("dp", None),
        P("dp"),
        P(None, "dp"),
    )
    return jax.shard_map(
        on_device, mesh=mesh, in_specs=in_specs, out_specs=out_specs, check_vma=False
    )
```

```python
import functools

import jax
import jax.numpy as jnp
from jax import lax
from jax.experimental import pallas as pl
from jax.experimental.pallas import tpu as pltpu
from jax.sharding import PartitionSpec as P

HEADS = 12
HEAD = 64
BASE = 256
PASSES = 5
NEG_FILL = -1e30
EPSILON = 1e-05
TANH_IN = 0.7978845608028654
TANH_CUBE = 0.044715
F32 = jnp.float32
BF16 = jnp.bfloat16
VMEM_LIMIT = 60 * 2**20


def dot(left, right):
    return jnp.dot(left, right, preferred_element_type=F32)


def dot_nt(left, right):
    return lax.dot_general(
        left, right, (((1,), (1,)), ((), ())), preferred_element_type=F32
    )


def dot_tn(left, right):
    return lax.dot_general(
        left, right, (((0,), (0,)), ((), ())), preferred_element_type=F32
    )


def row_mean(block):
    return jnp.mean(block, axis=1, keepdims=True)


def col_sum(block):
    return jnp.sum(block, axis=0, keepdims=True)


def normalize(block):
    centre = block - row_mean(block)
    scale = lax.rsqrt(row_mean(centre * centre) + EPSILON)
    return centre * scale, scale


def places_of(block_id, core, half, rows):
    start = (block_id * half + core) * rows
    return start + lax.broadcasted_iota(jnp.int32, (rows, 1), 0)


def embed_kernel(scalars, kept, came, table, gain, shift, embedded, normed):
    core, seq, count = scalars[0], scalars[1], scalars[2]
    rows = kept.shape[0]
    for block_id in range(2):
        section = lax.rem(places_of(block_id, core, 2, rows), count)
        mine = kept[...].astype(F32)
        other = came[...].astype(F32)
        hidden = jnp.where(seq == block_id, mine, other)
        added = jnp.zeros_like(hidden)
        for section_id in range(PASSES):
            added = jnp.where(section == section_id, table[section_id : section_id + 1, :], added)
        hidden = hidden + added
        span = pl.ds(block_id * rows, rows)
        embedded[span, :] = hidden
        unit, _ = normalize(hidden)
        normed[span, :] = (unit * gain[...] + shift[...]).astype(BF16)


def gather_rows(core, kept, came, whole):
    rows = kept.shape[0] // 2
    for block_id in range(2):
        span = slice(block_id * rows, (block_id + 1) * rows)
        whole[pl.ds(pl.multiple_of((block_id * 2 + core) * rows, 64), rows), :] = kept[span, :]
        whole[pl.ds(pl.multiple_of((block_id * 2 + 1 - core) * rows, 64), rows), :] = came[span, :]


def split_rows(core, whole, kept, away):
    rows = kept.shape[0] // 2
    for block_id in range(2):
        span = slice(block_id * rows, (block_id + 1) * rows)
        kept[span, :] = whole[
            pl.ds(pl.multiple_of((block_id * 2 + core) * rows, 64), rows), :
        ].astype(kept.dtype)
        away[span, :] = whole[
            pl.ds(pl.multiple_of((block_id * 2 + 1 - core) * rows, 64), rows), :
        ].astype(away.dtype)


def head_parts(block, which):
    start = 3 * HEAD * which
    queries = block[:, start : start + HEAD] * jnp.asarray(HEAD**-0.5, BF16)
    keys = block[:, start + HEAD : start + 2 * HEAD]
    values = block[:, start + 2 * HEAD : start + 3 * HEAD]
    return queries, keys, values


def causal_block(size):
    key_place = lax.broadcasted_iota(jnp.int32, (size, size), 0)
    query_place = lax.broadcasted_iota(jnp.int32, (size, size), 1)
    return key_place <= query_place


def forward_kernel(
    scalars, kept, came, weight, bias, whole, packed, mixed, mixed_kept, mixed_away, log_total
):
    core = scalars[0]
    full = whole.shape[0]
    gather_rows(core, kept, came, whole)
    for start in range(0, full, BASE):
        span = pl.ds(start, BASE)
        packed[span, :] = (dot_nt(whole[span, :], weight[...]) + bias[...]).astype(BF16)
    visible = causal_block(BASE)

    def pair(index, carry):
        block = packed[:, pl.ds(pl.multiple_of(index * 6 * HEAD, 128), 6 * HEAD)]
        results, logs = [], []
        for which in range(2):
            queries, keys, values = head_parts(block, which)
            values_ext = jnp.concatenate([values.T, jnp.ones((16, full), BF16)], axis=0)
            outs, totals = [], []
            for start in range(0, full, BASE):
                end = start + BASE
                scores = dot_nt(keys[:end], queries[start:end])
                last = jnp.where(visible, scores[start:], NEG_FILL)
                scores = last if start == 0 else jnp.concatenate([scores[:start], last], axis=0)
                top = jnp.max(scores, axis=0, keepdims=True)
                raised = jnp.exp(scores - top).astype(BF16)
                grown = dot(values_ext[:, :end], raised)
                total = grown[HEAD : HEAD + 1]
                outs.append(grown[:HEAD] / total)
                totals.append(top + jnp.log(total))
            results.append(jnp.concatenate(outs, axis=1))
            logs.append(jnp.concatenate(totals, axis=1))
        mixed[:, pl.ds(pl.multiple_of(index * 2 * HEAD, 128), 2 * HEAD)] = jnp.concatenate(
            results, axis=0
        ).T.astype(BF16)
        log_total[index] = jnp.concatenate(logs, axis=0)
        return carry

    lax.fori_loop(0, HEADS // 4, pair, 0)
    split_rows(core, mixed, mixed_kept, mixed_away)


def feed_kernel(
    scalars,
    mixed_kept,
    mixed_came,
    embedded,
    cot_kept,
    cot_came,
    out_weight,
    out_bias,
    gain,
    shift,
    up_weight,
    up_bias,
    down_weight,
    down_bias,
    out_kept,
    out_away,
    middle_grad,
    mixed_grad_kept,
    mixed_grad_away,
    grads,
    row_sums,
    up_sums,
    mixed,
    middle,
    normed,
    normed_t,
    out_grad,
    branch,
    normed_grad,
):
    core, seq, count = scalars[0], scalars[1], scalars[2]
    total_rows, width = middle.shape
    rows = total_rows // 2
    half = width // 2
    hidden = up_weight.shape[1]
    owners = grads.shape[1]
    up_rows = width // owners
    down_rows = hidden // owners
    mixed[:, pl.ds(pl.multiple_of(core * half, 128), half)] = mixed_kept[...]
    mixed[:, pl.ds(pl.multiple_of((1 - core) * half, 128), half)] = mixed_came[...]
    valid = []
    for block_id in range(2):
        span = slice(block_id * rows, (block_id + 1) * rows)
        value = embedded[span, :] + dot(mixed[span, :], out_weight[...]) + out_bias[...]
        middle[span, :] = value
        unit, _ = normalize(value)
        normed[span, :] = (unit * gain[...] + shift[...]).astype(BF16)
        keep = places_of(block_id, core, 2, rows) < count * BASE
        valid.append(keep)
        cot = jnp.where(seq == block_id, cot_kept[...].astype(F32), cot_came[...].astype(F32))
        out_grad[span, :] = jnp.where(keep, cot, 0.0).astype(BF16)
    normed_t[...] = normed[...].T
    branch[...] = jnp.zeros_like(branch)
    normed_grad[...] = jnp.zeros_like(normed_grad)
    tile = 2 * half
    for step in range(hidden // tile):
        cols = pl.ds(step * tile, tile)
        value = dot(normed[...], up_weight[:, cols]) + up_bias[:, cols]
        square = value * value
        tanh = jnp.tanh(value * (TANH_IN + TANH_IN * TANH_CUBE * square))
        gate = 0.5 + 0.5 * tanh
        activated = (value * gate).astype(BF16)
        slope = gate + (0.5 * value) * (1.0 - tanh * tanh) * (
            TANH_IN + 3.0 * TANH_IN * TANH_CUBE * square
        )
        up_grad = (dot_nt(out_grad[...], down_weight[cols, :]) * slope).astype(BF16)
        branch[...] += dot(activated, down_weight[cols, :])
        normed_grad[...] += dot_nt(up_grad, up_weight[:, cols])
        up_sums[:, cols] = col_sum(up_grad.astype(F32))
        up_part = dot(normed_t[...], up_grad).astype(BF16)
        down_part = dot_tn(activated, out_grad[...]).astype(BF16)
        for sub in range(2):
            slot = (step * 2 + sub) % 4
            side = (step * 2 + sub) // 4
            for owner in range(owners):
                grads[side, owner, slot * up_rows : (slot + 1) * up_rows, :] = up_part[
                    owner * up_rows : (owner + 1) * up_rows, sub * half : (sub + 1) * half
                ]
        for owner in range(owners):
            first = max(owner * down_rows, step * tile)
            last = min((owner + 1) * down_rows, (step + 1) * tile)
            if first < last:
                place = 4 * up_rows + first - owner * down_rows
                for side in range(2):
                    grads[side, owner, place : place + last - first, :] = down_part[
                        first - step * tile : last - step * tile, side * half : (side + 1) * half
                    ]
    sums = [0.0] * 4
    for block_id in range(2):
        span = slice(block_id * rows, (block_id + 1) * rows)
        value = middle[span, :]
        unit, scale = normalize(value)
        inner = normed_grad[span, :]
        scaled = inner * gain[...]
        cot = out_grad[span, :].astype(F32)
        grad = cot + scale * (scaled - row_mean(scaled) - unit * row_mean(scaled * unit))
        middle_grad[span, :] = grad
        low = grad.astype(BF16)
        normed[span, :] = low
        result = jnp.where(
            valid[block_id], value + branch[span, :] + down_bias[...], 0.0
        ).astype(BF16)

        @pl.when(seq == block_id)
        def _():
            out_kept[...] = result

        @pl.when(seq != block_id)
        def _():
            out_away[...] = result

        mixed_grad_kept[span, :] = dot_nt(
            low, out_weight[pl.ds(pl.multiple_of(core * half, 128), half), :]
        ).astype(BF16)
        mixed_grad_away[span, :] = dot_nt(
            low, out_weight[pl.ds(pl.multiple_of((1 - core) * half, 128), half), :]
        ).astype(BF16)
        terms = (inner * unit, inner, low.astype(F32), cot)
        sums = [have + col_sum(term) for have, term in zip(sums, terms)]
    row_sums[...] = jnp.concatenate(sums + [jnp.zeros((4, width), F32)], axis=0)
    out_part = dot_tn(mixed[...], normed[...]).astype(BF16)
    base_row = 4 * up_rows + down_rows
    for owner in range(owners):
        for side in range(2):
            grads[side, owner, base_row : base_row + up_rows, :] = out_part[
                owner * up_rows : (owner + 1) * up_rows, side * half : (side + 1) * half
            ]


def backward_kernel(
    scalars,
    packed,
    log_total,
    mixed_kept,
    mixed_away,
    grad_kept,
    grad_came,
    whole,
    weight,
    inner_kept,
    inner_away,
    heads_grad,
    bias_sums,
    mixed,
    mixed_grad,
    packed_grad,
    inner,
    value_key_sum,
):
    core = scalars[0]
    full = whole.shape[0]
    owners = heads_grad.shape[0]
    own_rows = heads_grad.shape[1] // 3
    gather_rows(core, mixed_kept, mixed_away, mixed)
    gather_rows(core, grad_kept, grad_came, mixed_grad)
    visible = causal_block(BASE)

    def pair(index, carry):
        base = pl.multiple_of(index * 6 * HEAD, 128)
        block = packed[:, pl.ds(base, 6 * HEAD)]
        lanes = pl.ds(pl.multiple_of(index * 2 * HEAD, 128), 2 * HEAD)
        both_grad = mixed_grad[:, lanes]
        overlap = both_grad.astype(F32) * mixed[:, lanes].astype(F32)
        parts = []
        for which in range(2):
            queries, keys, values = head_parts(block, which)
            grad = both_grad[:, HEAD * which : HEAD * (which + 1)]
            delta = jnp.sum(
                overlap[:, HEAD * which : HEAD * (which + 1)], axis=1, keepdims=True
            ).T
            logs = log_total[index][which : which + 1]
            keys_t = keys.T
            blank = jnp.zeros_like(queries)
            grad_ext = jnp.concatenate([blank, grad], axis=1)
            queries_ext = jnp.concatenate([queries, blank], axis=1)
            query_parts = []
            for start in range(0, full, BASE):
                end = start + BASE
                span = slice(start, end)
                weights = jnp.exp(dot_nt(keys[:end], queries[span]) - logs[:, span])
                last = jnp.where(visible, weights[start:], 0.0)
                weights = (
                    last if start == 0 else jnp.concatenate([weights[:start], last], axis=0)
                )
                weight_grad = dot_nt(values[:end], grad[span])
                score_grad = (weights * (weight_grad - delta[:, span])).astype(BF16)
                added = dot(weights.astype(BF16), grad_ext[span]) + dot(
                    score_grad, queries_ext[span]
                )
                if start > 0:
                    value_key_sum[which, :start, :] += added[:start]
                value_key_sum[which, start:end, :] = added[start:]
                query_parts.append(dot(keys_t[:, :end], score_grad) * HEAD**-0.5)
            parts += [jnp.concatenate(query_parts, axis=1).T, value_key_sum[which]]
        packed_grad[:, pl.ds(base, 6 * HEAD)] = jnp.concatenate(parts, axis=1).astype(BF16)
        return carry

    lax.fori_loop(0, HEADS // 4, pair, 0)
    low = packed_grad[...]
    bias_sums[...] = col_sum(low.astype(F32))
    for start in range(0, full, BASE):
        inner[pl.ds(start, BASE), :] = dot(packed_grad[pl.ds(start, BASE), :], weight[...])
    split_rows(core, inner, inner_kept, inner_away)
    part = dot_tn(whole[...], low).astype(BF16)
    third = heads_grad.shape[2]
    for owner in range(owners):
        for group in range(3):
            heads_grad[owner, group * own_rows : (group + 1) * own_rows, :] = part[
                owner * own_rows : (owner + 1) * own_rows, group * third : (group + 1) * third
            ]


def input_kernel(
    scalars, inner_kept, inner_came, embedded, middle_grad, gain, grad_kept, grad_away, sums
):
    core, seq, count = scalars[0], scalars[1], scalars[2]
    total_rows, width = embedded.shape
    rows = total_rows // 2
    found = [0.0] * (2 + PASSES)
    for block_id in range(2):
        span = slice(block_id * rows, (block_id + 1) * rows)
        unit, scale = normalize(embedded[span, :])
        inner = inner_kept[span, :] + inner_came[span, :].astype(F32)
        scaled = inner * gain[...]
        grad = middle_grad[span, :] + scale * (
            scaled - row_mean(scaled) - unit * row_mean(scaled * unit)
        )

        @pl.when(seq == block_id)
        def _():
            grad_kept[...] = grad

        @pl.when(seq != block_id)
        def _():
            grad_away[...] = grad.astype(BF16)

        section = lax.rem(places_of(block_id, core, 2, rows), count)
        terms = [inner * unit, inner]
        for section_id in range(PASSES):
            terms.append(jnp.where(section == section_id, grad, 0.0))
        found = [have + col_sum(term) for have, term in zip(found, terms)]
    sums[...] = jnp.concatenate(found + [jnp.zeros((1, width), F32)], axis=0)


MESH = pl.DeviceIdType.MESH

UP_KIND, DOWN_KIND, SQUARE_KIND, HEADS_KIND = range(4)
Z2, Z1, X, Y = range(4)

(DOWN_0A, DOWN_0B, UP_0A, UP_0B, DOWN_1A, DOWN_1B, UP_1A, UP_1B, DOWN_2A, DOWN_2B, UP_2A, UP_2B,
    SQUARE, HEADS_0, HEADS_1A, HEADS_1B, HEADS_2A, HEADS_2B, VECTORS, OUT) = range(20)
SUMS = {
    DOWN_0A: (DOWN_KIND, 0, 1, (Z1, Z2, Y, X)),
    DOWN_0B: (DOWN_KIND, 0, 2, (Y, Z1, X, Z2)),
    UP_0A: (UP_KIND, 0, 1, (Z1, X, Z2, Y)),
    UP_0B: (UP_KIND, 0, 2, (X, Z1, Z2, Y)),
    DOWN_1A: (DOWN_KIND, 1, 1, (Y, X, Z1, Z2)),
    DOWN_1B: (DOWN_KIND, 1, 2, (X, Z1, Z2, Y)),
    UP_1A: (UP_KIND, 1, 1, (Y, Z1, X, Z2)),
    UP_1B: (UP_KIND, 1, 2, (Z1, X, Z2, Y)),
    DOWN_2A: (DOWN_KIND, 2, 1, (Y, X, Z1, Z2)),
    DOWN_2B: (DOWN_KIND, 2, 2, (X, Z1, Z2, Y)),
    UP_2A: (UP_KIND, 2, 1, (Y, X, Z1, Z2)),
    UP_2B: (UP_KIND, 2, 2, (X, Z1, Z2, Y)),
    SQUARE: (SQUARE_KIND, 0, 0, (Z1, X, Y, Z2)),
    HEADS_0: (HEADS_KIND, 0, 0, (X, Y, Z1, Z2)),
    HEADS_1A: (HEADS_KIND, 1, 1, (X, Z1, Z2, Y)),
    HEADS_1B: (HEADS_KIND, 1, 2, (Y, Z1, Z2, X)),
    HEADS_2A: (HEADS_KIND, 2, 1, (X, Z1, Z2, Y)),
    HEADS_2B: (HEADS_KIND, 2, 2, (X, Z1, Z2, Y)),
}
(AT_HIDDEN_0, AT_DOWN_0, AT_UP_0, AT_BRANCH_0, AT_HIDDEN_1, AT_DOWN_1, AT_UP_1, AT_BRANCH_1,
    AT_HIDDEN_2, AT_DOWN_2, AT_UP_2, AT_BRANCH_2, AT_MIDDLE, AT_SQUARED, AT_HALF_PAIR_0,
    AT_PAIR_0, AT_HEADS_WEIGHT_0, AT_HALF_PAIR_1, AT_PAIR_1, AT_HEADS_WEIGHT_1, AT_HALF_PAIR_2,
    AT_PAIR_2, AT_INNER_0, AT_HEADS_WEIGHT_2, AT_INPUT_0, AT_INNER_1, AT_INPUT_1) = range(27)
PLAN = {
    AT_DOWN_0: (DOWN_0A, DOWN_0B),
    AT_UP_0: (UP_0A, UP_0B),
    AT_BRANCH_0: (DOWN_0A,),
    AT_HIDDEN_1: (DOWN_0B,),
    AT_DOWN_1: (UP_0A, DOWN_1A, DOWN_1B),
    AT_UP_1: (UP_0B, UP_1A, UP_1B),
    AT_BRANCH_1: (DOWN_0A, DOWN_1A),
    AT_HIDDEN_2: (DOWN_0B, DOWN_1B, UP_0A),
    AT_DOWN_2: (UP_1A, UP_0B, DOWN_2A, DOWN_2B),
    AT_UP_2: (UP_1B, UP_2A, UP_2B),
    AT_BRANCH_2: (DOWN_1A, DOWN_0A, DOWN_0B, DOWN_2A),
    AT_MIDDLE: (OUT, DOWN_1B, UP_0B, DOWN_2B, UP_1A),
    AT_SQUARED: (UP_0A, UP_2A, DOWN_0A, SQUARE),
    AT_HALF_PAIR_0: (UP_2B, DOWN_1A, UP_1B, DOWN_0B, DOWN_1B, DOWN_2A, SQUARE),
    AT_PAIR_0: (UP_0B, UP_1A, DOWN_2B, DOWN_0A, DOWN_1A, UP_0A),
    AT_HEADS_WEIGHT_0: (DOWN_0B, UP_2B, HEADS_0),
    AT_HALF_PAIR_1: (DOWN_1B, UP_1B),
    AT_PAIR_1: (DOWN_2A, UP_1A, SQUARE),
    AT_HEADS_WEIGHT_1: (UP_2A, DOWN_2B, UP_0B, DOWN_1A, DOWN_0A, HEADS_1A, HEADS_1B),
    AT_HALF_PAIR_2: (UP_0A, UP_2B, DOWN_0B, UP_0B, DOWN_0A, DOWN_1B, HEADS_0, DOWN_1A, DOWN_2A,
        UP_1B),
    AT_PAIR_2: (UP_1A, HEADS_1B, UP_0A, SQUARE, DOWN_0B, DOWN_1B, DOWN_1A, DOWN_2B),
    AT_INNER_0: (UP_2A, HEADS_0, UP_2B, UP_1B, DOWN_2A),
    AT_HEADS_WEIGHT_2: (UP_1A, HEADS_1B, HEADS_2A, HEADS_2B),
    AT_INPUT_0: (SQUARE, UP_1B, HEADS_1A),
    AT_INNER_1: (UP_2A, DOWN_2B, UP_1A, UP_2B, HEADS_0, DOWN_2A),
    AT_INPUT_1: (HEADS_1B, VECTORS),
}
ENDING = (DOWN_2B, UP_2B, SQUARE, DOWN_2A, HEADS_2A, HEADS_1A, HEADS_2B, UP_2A, HEADS_1B, HEADS_0,
    VECTORS, HEADS_2A, HEADS_1A, HEADS_2B, SQUARE, UP_2A, HEADS_2A, HEADS_1B, HEADS_0, HEADS_2B,
    SQUARE, UP_2A, HEADS_1B, HEADS_1A, HEADS_0, VECTORS, HEADS_2A, HEADS_2B, HEADS_1A, HEADS_2A,
    HEADS_2B)

SENDS, RECEIVES, FETCHES = 37, 127, 17


def add_low(left, right):
    return (left.astype(F32) + right.astype(F32)).astype(BF16)


def main_kernel(
    passes,
    first_gain,
    first_shift,
    query_bias,
    value_bias,
    out_bias,
    second_gain,
    second_shift,
    up_bias,
    down_bias,
    table,
    tokens_in,
    cot_in,
    weight_hbm,
    out_weight_hbm,
    up_weight_hbm,
    down_weight_hbm,
    out_hbm,
    tokens_kept_hbm,
    tokens_came_hbm,
    up_hbm,
    down_hbm,
    square_hbm,
    heads_hbm,
    vectors_out,
    landed,
    embedded,
    out_weight,
    up_weight,
    down_weight,
    whole,
    packed,
    mixed,
    mixed_rows,
    log_total,
    middle_grad,
    mixed_grad,
    mixed_grad_away,
    up_parts,
    up_core,
    up_land,
    down_parts,
    down_core,
    down_land,
    square_parts,
    square_core,
    square_land,
    heads_parts,
    heads_land,
    up_final,
    down_final,
    square_final,
    heads_final,
    vectors,
    vector_owners,
    vector_total,
    vector_heads,
    send_sems,
    recv_sems,
    local_sems,
):
    dp, head = lax.axis_index("dp"), lax.axis_index("head")
    core, seq = head % 2, head // 2
    bit0, bit1, bit2 = dp % 2, (dp // 2) % 2, dp // 4
    far_core, far_seq = 1 - core, 1 - seq
    far0, far1, far2 = 1 - bit0, 1 - bit1, 1 - bit2
    to_core = {"head": head + far_core - core}
    to_seq = {"head": head + 2 * (far_seq - seq)}
    to0 = {"dp": dp + far0 - bit0}
    to1 = {"dp": dp + 2 * (far1 - bit1)}
    to2 = {"dp": dp + 4 * (far2 - bit2)}
    head_peers = [lax.rem(head + step, 4) for step in range(1, 4)]
    dp_peers = [lax.rem(dp + step, 8) for step in range(1, 8)]
    own_half = pl.multiple_of(core * 384, 128)
    far_half = pl.multiple_of(far_core * 384, 128)
    own_starts = [pl.multiple_of((block * 2 + core) * 320, 64) for block in range(2)]
    far_starts = [pl.multiple_of((block * 2 + far_core) * 320, 64) for block in range(2)]
    late_blocks = [far_seq, seq]
    late_own = [pl.multiple_of((block * 2 + core) * 320, 64) for block in late_blocks]
    late_far = [pl.multiple_of((block * 2 + far_core) * 320, 64) for block in late_blocks]
    late_spans = [pl.multiple_of(block * 320, 64) for block in late_blocks]
    owner_base = core * 4
    out_slots = [1 - seq, seq]
    own_weight = pl.multiple_of(core * 1152, 128)
    own_lanes = [pl.multiple_of(core * 384 + index * 128, 128) for index in range(3)]
    count = passes[seq]
    length = count * BASE
    own_second = pl.multiple_of((far_seq * 2 + core) * 320 + 160, 32)
    flat_starts = [pl.multiple_of(block * 320, 64) for block in (seq, far_seq)]
    front_own = [pl.multiple_of((block * 2 + core) * 320, 64) for block in (seq, far_seq)]
    front_far = [pl.multiple_of((block * 2 + far_core) * 320, 64) for block in (seq, far_seq)]
    rows, total_rows, width, half, full, tile = 320, 640, 768, 384, 1280, 1024

    sent = []
    used = [0, 0, 0]

    def view(place):
        if isinstance(place, tuple):
            return place[0].at[place[1:]]
        return place

    groups = {}

    def place_of(kind, group):
        if group is None:
            used[kind] += 1
            return used[kind] - 1
        if (kind, group) not in groups:
            groups[kind, group] = used[kind]
            used[kind] += 1
        return groups[kind, group]

    class Sent:
        def __init__(self, source, target, device, out_group, in_group):
            self.out_place = place_of(0, out_group) if out_group != "" else 0
            self.in_place = place_of(1, in_group) if in_group != "" else 0
            self.parts = (source, target, device)
            self.left = False

        def make(self):
            source, target, device = self.parts
            return pltpu.make_async_remote_copy(
                src_ref=view(source),
                dst_ref=view(target),
                send_sem=send_sems.at[self.out_place],
                recv_sem=recv_sems.at[self.in_place],
                device_id=device,
                device_id_type=MESH,
            )

        def wait_recv(self):
            self.make().wait_recv()

        def wait_send(self):
            if not self.left:
                self.make().wait_send()
            self.left = True

    class Fetched:
        def __init__(self, source, target, group):
            self.parts = (source, target, place_of(2, group))

        def make(self):
            source, target, place = self.parts
            return pltpu.make_async_copy(view(source), view(target), local_sems.at[place])

        def wait(self):
            self.make().wait()

    def send(source, target, device, out_group=None, in_group=None):
        copy = Sent(source, target, device, out_group, in_group)
        copy.make().start()
        if out_group is None:
            sent.append(copy)
        return copy

    def wait_out(group, place):
        Sent(place, place, to_core, group, "").wait_send()

    def wait_in(group, place):
        Sent(place, place, to_core, "", group).wait_recv()

    def fetch(source, target, group=None):
        copy = Fetched(source, target, group)
        copy.make().start()
        return copy

    def wait_fetched(group, place):
        Fetched(place, place, group).wait()

    every = slice(None)

    barrier = pltpu.get_barrier_semaphore()
    for peer in head_peers:
        pl.semaphore_signal(barrier, inc=1, device_id={"head": peer}, device_id_type=MESH)
    for peer in dp_peers:
        pl.semaphore_signal(barrier, inc=1, device_id={"dp": peer}, device_id_type=MESH)

    def first_step(name, parts, at, cored, tail):
        if cored is None:
            return at
        slot = (at[0] % 2,) if at else ()
        rest = (every,) * 4 + tail
        copy = send((parts,) + at + (far_core,) + rest, (cored,) + slot + rest, to_core, name)
        yield
        copy.wait_recv()
        place = at + (core,)
        parts[place + rest] = add_low(parts[place + rest], cored[slot + rest])
        return place

    axes = (
        (bit2, far2, to2),
        (bit1, far1, to1),
        (bit0, far0, to0),
        (seq, far_seq, to_seq),
    )

    def chain(name, kind, order, parts, at, cored, land, final, tail=()):
        lead = yield from first_step(name, parts, at, cored, tail)
        place = [every] * 4
        for step, axis in enumerate(order):
            own, far, device = axes[axis]
            remaining = (every,) * (3 - step) if step < 3 else (every if axis == Y else 0,)
            target = (land[step],) + at + remaining + tail
            source = list(place)
            if axis != Y or step < 3:
                source[axis], place[axis] = far, own
            copy = send((parts,) + lead + tuple(source) + tail, target, device, name)
            yield
            copy.wait_recv()
            found = add_low(parts[lead + tuple(place) + tail], target[0][target[1:]])
            if step < 3:
                parts[lead + tuple(place) + tail] = found
            elif axis == Y:
                final[at + (core, every) + tail] = found
            else:
                final[at + (core, seq) + tail] = found
        if order[3] != Y:
            place = (final,) + at + (core, seq) + tail
            copy = send(place, place, to_seq, name)
            yield
            copy.wait_recv()
        place = (final,) + at + (core, every) + tail
        copy = send(place, place, to_core, (kind,))
        yield
        copy.wait_recv()

    def vector_sum(parts, by_owner, total, by_head, result):
        for peer in dp_peers:
            send((parts, peer), (by_owner, dp), {"dp": peer}, "owners", "owners")
        by_owner[dp] = parts[dp]
        yield
        wait_in("owners", (by_owner, slice(0, 7)))
        found = by_owner[0]
        for place in range(1, 8):
            found = found + by_owner[place]
        total[...] = found
        for peer in head_peers:
            send(total, (by_head, head), {"head": peer}, "heads_sum", "heads_sum")
        by_head[head] = found
        yield
        wait_in("heads_sum", (by_head, slice(0, 3)))
        result[...] = by_head[0] + by_head[1] + by_head[2] + by_head[3]

    class Chain:
        def __init__(self, name, steps, group=None):
            self.name, self.steps, self.group = name, steps, group
            self.taken, self.done = 0, False

        def step(self):
            with jax.named_scope(f"sum{self.name}_{self.taken}"):
                self.taken += 1
                if next(self.steps, self) is self:
                    self.done = True
                    if self.group:
                        kind, final, result, _ = self.group
                        left[kind] -= 1
                        if left[kind] == 0:
                            writes.append(fetch(final, result))

    chains, left, writes = {}, {}, []
    arrays = (
        (up_parts, up_core, up_land, up_final, up_hbm),
        (down_parts, down_core, down_land, down_final, down_hbm),
        (square_parts, square_core, square_land, square_final, square_hbm),
        (heads_parts, None, heads_land, heads_final, heads_hbm),
    )
    for name, (kind, part, side, order) in SUMS.items():
        at = () if kind == SQUARE_KIND else (part,)
        parts, cored, land, final, result = arrays[kind]
        tail = ()
        if side > 0:
            if kind == DOWN_KIND:
                tail = (slice(0, 32) if side == 1 else slice(32, 64),)
            else:
                tail = (every, slice(0, 256) if side == 1 else slice(256, parts.shape[-1]))
        steps = chain(name, kind, order, parts, at, cored, land, final, tail)
        whole_of = (parts,) + at + (every,) * (4 if cored is None else 5) + tail
        chains[name] = Chain(name, steps, (kind, final, result, whole_of))
        left[kind] = left.get(kind, 0) + 1
    chains[VECTORS] = Chain(
        VECTORS, vector_sum(vectors, vector_owners, vector_total, vector_heads, vectors_out)
    )

    def tick(point):
        for name in PLAN.get(point, ()):
            if name == OUT:
                out_sent.append(send((landed, 0), (out_hbm, seq), to_seq))
            else:
                chains[name].step()

    chunk = 32
    chunk_places = lax.broadcasted_iota(jnp.int32, (chunk, 1), 0)
    cot_sent, out_sent = [], []
    out_fetch = fetch(out_weight_hbm, out_weight)

    def fold(term):
        return jnp.sum(term.reshape(-1, 8, width), axis=0)

    def load(step):
        slot = step % 2
        for group in range(8):
            cols = pl.ds(group * half + step * 128, 128)
            into = pl.ds(group * 128, 128)
            fetch((up_weight_hbm, every, cols), (up_weight, slot, every, into), (step,))
            fetch((down_weight_hbm, cols), (down_weight, slot, into), (3 + step,))

    def front_phase(weight, tokens_own, bias):
        weight_fetch = fetch((weight_hbm, pl.ds(own_weight, 1152)), weight)
        own_fetch = fetch((tokens_in, seq), tokens_own)
        with jax.named_scope("barrier"):
            pl.semaphore_wait(barrier, 10)
        pieces = (slice(0, rows // 2), slice(rows // 2, rows))

        def send_piece(piece):
            return send((tokens_in, far_seq, piece), (landed, 0, piece), to_seq)

        came = [send_piece(pieces[0])]
        gain, shift = first_gain[...].reshape(1, width), first_shift[...].reshape(1, width)
        blank = jnp.zeros((1, HEAD), F32)
        for side in range(2):
            parts = []
            for place in range(side * 6 * HEAD, (side + 1) * 6 * HEAD, HEAD):
                parts.append(query_bias[place : place + HEAD].reshape(1, HEAD))
                parts.append(blank)
                parts.append(value_bias[place : place + HEAD].reshape(1, HEAD))
            bias[side] = jnp.concatenate(parts, axis=1)

        def local_chunk(order, step):
            return pl.ds(pl.multiple_of(flat_starts[order] + step * chunk, 32), chunk)

        def embed_passes(order):
            block = (seq, far_seq)[order]
            for step in range(rows // chunk):
                place = (block * 2 + core) * rows + step * chunk + chunk_places
                section = lax.rem(place, count)
                added = jnp.zeros((chunk, width), F32)
                for section_id in range(PASSES):
                    added = jnp.where(
                        section == section_id, table[section_id : section_id + 1, :], added
                    )
                embedded[local_chunk(order, step), :] = added

        def embed(source, order, piece):
            for step in range(piece.start // chunk, piece.stop // chunk):
                place = local_chunk(order, step)
                hidden = source[step * chunk : (step + 1) * chunk, :].astype(F32) + embedded[place, :]
                embedded[place, :] = hidden
                unit, _ = normalize(hidden)
                whole[pl.ds(pl.multiple_of(front_own[order] + step * chunk, 32), chunk), :] = (
                    unit * gain + shift
                ).astype(BF16)
            start = front_own[order] if piece.start == 0 else own_second
            place = (whole, pl.ds(start, piece.stop - piece.start))
            return send(place, place, to_core)

        def project(start, piece):
            span = pl.ds(
                pl.multiple_of(start + piece.start, 32), piece.stop - piece.start
            )
            packed[span, :] = (dot_nt(whole[span, :], weight[...]) + bias[core]).astype(BF16)

        with jax.named_scope("embed"):
            embed_passes(0)
            own_fetch.wait()
            copy = embed(tokens_own, 0, slice(0, rows))
            embed_passes(1)
        weight_fetch.wait()
        with jax.named_scope("packed"):
            project(front_own[0], slice(0, rows))
            came[0].wait_send()
            came.append(send_piece(pieces[1]))
            copy.wait_recv()
            project(front_far[0], slice(0, rows))
        load(0)
        load(1)
        for place, piece in enumerate(pieces):
            with jax.named_scope("tokens_in"):
                came[place].wait_recv()
                if place == 1:
                    came[1].wait_send()
                    cot_sent.append(send((cot_in, far_seq), (landed, 1), to_seq))
            with jax.named_scope("embed"):
                copy = embed(landed.at[0], 1, piece)
            with jax.named_scope("packed"):
                project(front_own[1], piece)
                copy.wait_recv()
                project(front_far[1], piece)

        visible = causal_block(BASE)
        queues, results, logs = {}, {}, {}

        def prepare(index):
            block = packed[:, index * 384 : (index + 1) * 384]
            for which in range(2):
                queries, keys, values = head_parts(block, which)
                values_ext = jnp.concatenate([values.T, jnp.ones((16, full), BF16)], axis=0)
                queues[index, which] = (queries, keys, values_ext)
                results[index, which], logs[index, which] = [], []

        def scores_of(place, start):
            queries, keys, _ = queues[place]
            scores = dot_nt(keys[: start + BASE], queries[start : start + BASE])
            last = jnp.where(visible, scores[start:], NEG_FILL)
            return last if start == 0 else jnp.concatenate([scores[:start], last], axis=0)

        def raise_of(scores):
            top = jnp.max(scores, axis=0, keepdims=True)
            return jnp.exp(scores - top).astype(BF16), top

        def gather_of(place, start, raised, top):
            grown = dot(queues[place][2][:, : start + BASE], raised)
            total = grown[HEAD : HEAD + 1]
            results[place].append(grown[:HEAD] / total)
            logs[place].append(top + jnp.log(total))
            index, which = place
            if start + BASE < full:
                return
            log_total[index, which : which + 1, :] = jnp.concatenate(logs[place], axis=1)
            if which == 0:
                return
            lanes = slice(index * 128, (index + 1) * 128)
            mixed[:, lanes] = jnp.concatenate(
                [jnp.concatenate(results[index, each], axis=1) for each in range(2)], axis=0
            ).T.astype(BF16)
            lanes_out = pl.ds(own_lanes[index], 128)
            for block in range(2):
                send(
                    (mixed, pl.ds(far_starts[block], rows), lanes),
                    (mixed_rows, slice(block * rows, (block + 1) * rows), lanes_out),
                    to_core,
                    "mixed",
                    "mixed",
                )

        with jax.named_scope("attend"):
            first = second = None
            for place in [(index, which) for index in range(3) for which in range(2)]:
                for start in range(0, full, BASE):
                    if place[1] == 0 and start == 0:
                        prepare(place[0])
                    scores = scores_of(place, start)
                    raised = raise_of(first[2]) if first else None
                    if second:
                        gather_of(*second)
                    second = first[:2] + raised if first else None
                    first = (place, start, scores)
            raised = raise_of(first[2])
            gather_of(*second)
            gather_of(*(first[:2] + raised))

    pl.run_scoped(
        front_phase,
        pltpu.VMEM((1152, width), BF16),
        pltpu.VMEM((rows, width), BF16),
        pltpu.VMEM((2, 1, 1152), F32),
    )

    def feed_phase(
        middle, normed, normed_t, out_grad, branch,
        active, up_grads,
    ):
        cot_fetch = fetch((cot_in, seq), (out_grad, pl.ds(flat_starts[0], rows)))

        gain, shift = second_gain[...].reshape(1, width), second_shift[...].reshape(1, width)
        out_fetch.wait()
        out_bias_row = out_bias[...].reshape(1, width)
        with jax.named_scope("project"):
            for block in range(2):
                span = slice(block * rows, (block + 1) * rows)
                own = mixed[pl.ds(own_starts[block], rows), :]
                mixed_rows[span, pl.ds(own_half, half)] = own
                middle[span, :] = (
                    embedded[span, :]
                    + dot(own, out_weight[pl.ds(own_half, half), :])
                    + out_bias_row
                )
        with jax.named_scope("mixed"):
            wait_in("mixed", (mixed_rows, every, slice(0, half)))
        with jax.named_scope("project"):
            for block in range(2):
                span = slice(block * rows, (block + 1) * rows)
                middle[span, :] += dot(
                    mixed_rows[span, pl.ds(far_half, half)], out_weight[pl.ds(far_half, half), :]
                )
                for step in range(rows // chunk):
                    first = block * rows + step * chunk
                    part = slice(first, first + chunk)
                    unit, _ = normalize(middle[part, :])
                    normed[part, :] = (unit * gain + shift).astype(BF16)
            normed_t[...] = normed[...].T
            vectors[...] = jnp.zeros_like(vectors)
        with jax.named_scope("out_grad"):
            cot_fetch.wait()
            cot_sent[0].wait_recv()
            for block in range(2):
                for step in range(rows // chunk):
                    part = slice(block * rows + step * chunk, block * rows + (step + 1) * chunk)
                    inside = slice(step * chunk, (step + 1) * chunk)
                    cot = jnp.where(
                        seq == block,
                        out_grad[part, :].astype(F32),
                        landed[1, inside, :].astype(F32),
                    )
                    place = (block * 2 + core) * rows + step * chunk + chunk_places
                    out_grad[part, :] = jnp.where(place < length, cot, 0.0).astype(BF16)
        for step in range(3):
            slot = step % 2
            wait_fetched((step,), (up_weight, slot))
            wait_fetched((3 + step,), (down_weight, slot))
            with jax.named_scope("hidden"):
                def block_of(place):
                    return slice(place * 256, (place + 1) * 256)

                def value_of(place):
                    bias = jnp.concatenate(
                        [
                            up_bias[
                                group * half + step * 128 : group * half + (step + 1) * 128
                            ].reshape(1, 128)
                            for group in (2 * place, 2 * place + 1)
                        ],
                        axis=1,
                    )
                    return dot(normed[...], up_weight[slot, :, block_of(place)]) + bias

                value = value_of(0)
                for place in range(4):
                    later = value_of(place + 1) if place < 3 else None
                    square_of = value * value
                    tanh = jnp.tanh(value * (TANH_IN + TANH_IN * TANH_CUBE * square_of))
                    gate = 0.5 + 0.5 * tanh
                    active[:, block_of(place)] = (value * gate).astype(BF16)
                    slope = gate * (
                        1.0
                        + (1.0 - gate)
                        * (value * (2.0 * TANH_IN + 6.0 * TANH_IN * TANH_CUBE * square_of))
                    )
                    up_grads[:, block_of(place)] = (
                        dot_nt(out_grad[...], down_weight[slot, block_of(place), :]) * slope
                    ).astype(BF16)
                    value = later
            tick(AT_HIDDEN_0 + 4 * step)

            with jax.named_scope("down_weight"):
                for quarter in range(4):
                    part = dot_tn(active[:, block_of(quarter)], out_grad[...])
                    for side in range(2):
                        down_parts[step, side, quarter // 2, quarter % 2] = (
                            part[:, side * half : (side + 1) * half]
                            .astype(BF16)
                            .reshape(2, 2, 64, half)
                        )
            tick(AT_DOWN_0 + 4 * step)
            with jax.named_scope("up_weight"):
                for side in range(2):
                    for upper in range(2):
                        up_parts[step, side, upper] = (
                            dot(
                                normed_t[upper * half : (upper + 1) * half, :],
                                up_grads[:, side * 512 : (side + 1) * 512],
                            )
                            .astype(BF16)
                            .reshape(2, 2, 2, 48, 512)
                        )
            tick(AT_UP_0 + 4 * step)
            with jax.named_scope("branch"):
                for place in range(3):
                    cols = block_of(place)
                    grown = dot(active[...], down_weight[slot, :, cols])
                    returned = dot_nt(up_grads[...], up_weight[slot, cols, :])
                    if step > 0:
                        grown, returned = grown + branch[:, cols], returned + middle_grad[:, cols]
                    branch[:, cols], middle_grad[:, cols] = grown, returned
                sums = col_sum(up_grads[...].astype(F32))
                for group in range(8):
                    vectors[group, 4 + step : 5 + step, :] = sums[:, group * 128 : (group + 1) * 128]
            if step == 0:
                load(2)
            tick(AT_BRANCH_0 + 4 * step)
        down_bias_row = down_bias[...].reshape(1, width)
        sums = [jnp.zeros((8, width), F32)] * 4
        with jax.named_scope("middle_grad"):
            for block in range(2):
                span = slice(block * rows, (block + 1) * rows)
                for step in range(rows // chunk):
                    first = block * rows + step * chunk
                    part = slice(first, first + chunk)
                    value = middle[part, :]
                    unit, scale = normalize(value)
                    inner = middle_grad[part, :]
                    scaled = inner * gain
                    cot = out_grad[part, :].astype(F32)
                    grad = cot + scale * (
                        scaled - row_mean(scaled) - unit * row_mean(scaled * unit)
                    )
                    middle_grad[part, :] = grad
                    low = grad.astype(BF16)
                    normed[part, :] = low
                    place = (block * 2 + core) * rows + step * chunk + chunk_places
                    landed[out_slots[block], step * chunk : (step + 1) * chunk, :] = jnp.where(
                        place < length, value + branch[part, :] + down_bias_row, 0.0
                    ).astype(BF16)
                    terms = (inner * unit, inner, low.astype(F32), cot)
                    sums = [have + fold(term) for have, term in zip(sums, terms)]
                mixed_grad_away[span, :] = dot_nt(
                    normed[span, :], out_weight[pl.ds(far_half, half), :]
                ).astype(BF16)
                send(
                    (mixed_grad_away, span),
                    (mixed_grad, pl.ds(own_starts[block], rows)),
                    to_core,
                    "mixed_grad",
                    "mixed_grad",
                )
        tick(AT_MIDDLE)
        with jax.named_scope("output_weight"):
            for block in range(2):
                span = slice(block * rows, (block + 1) * rows)
                mixed_grad[pl.ds(own_starts[block], rows), :] = dot_nt(
                    normed[span, :], out_weight[pl.ds(own_half, half), :]
                ).astype(BF16)
            for line, found in enumerate(sums):
                found = col_sum(found)
                for group in range(8):
                    vectors[group, line : line + 1, :96] = found[:, group * 96 : (group + 1) * 96]
            for upper in range(2):
                part = dot_tn(mixed_rows[:, upper * half : (upper + 1) * half], normed[...])
                for side in range(2):
                    square_parts[side, upper] = (
                        part[:, side * half : (side + 1) * half]
                        .astype(BF16)
                        .reshape(2, 2, 2, 48, half)
                    )
        tick(AT_SQUARED)

    pl.run_scoped(
        feed_phase,
        pltpu.VMEM((total_rows, width), F32),
        pltpu.VMEM((total_rows, width), BF16),
        pltpu.VMEM((width, total_rows), BF16),
        pltpu.VMEM((total_rows, width), BF16),
        pltpu.VMEM((total_rows, width), F32),
        pltpu.VMEM((total_rows, tile), BF16),
        pltpu.VMEM((total_rows, tile), BF16),
    )
    out_kept = fetch((landed, 1), (out_hbm, seq))

    def back_phase(
        weight, packed_grad, inner_kept, inner_away, value_key_sum, tokens_away
    ):
        weight_fetch = fetch((weight_hbm, pl.ds(own_weight, 1152)), weight)
        visible = causal_block(BASE)

        def prepare_heads(index):
            block = packed[:, index * 384 : (index + 1) * 384]
            found = []
            for which in range(2):
                queries, keys, values = head_parts(block, which)
                blank = jnp.zeros_like(queries)
                queries_ext = jnp.concatenate([queries, blank], axis=1)
                found.append((queries, keys, values, keys.T, queries_ext))
            return found

        def prepare_grads(index, heads):
            both_grad = mixed_grad[:, index * 128 : (index + 1) * 128]
            overlap = both_grad.astype(F32) * mixed[:, index * 128 : (index + 1) * 128].astype(F32)
            given = []
            for which in range(2):
                queries, keys, values, keys_t, queries_ext = heads[which]
                grad = both_grad[:, HEAD * which : HEAD * (which + 1)]
                delta = jnp.sum(
                    overlap[:, HEAD * which : HEAD * (which + 1)], axis=1, keepdims=True
                ).T
                logs = log_total[index][which : which + 1]
                grad_ext = jnp.concatenate([jnp.zeros_like(grad), grad], axis=1)
                given.append(
                    (queries, keys, values, grad, delta, logs, keys_t, grad_ext, queries_ext)
                )
            return given

        def attend(index, given):
            query_parts = ([], [])
            coming = None

            def begin(which, start):
                queries, keys, values, grad = given[which][:4]
                end = start + BASE
                return (
                    dot_nt(keys[:end], queries[start:end]),
                    dot_nt(values[:end], grad[start:end]),
                )

            def finish(which, start, scores, weight_grad):
                delta, logs, keys_t, grad_ext, queries_ext = given[which][4:]
                end = start + BASE
                span = slice(start, end)
                weights = jnp.exp(scores - logs[:, span])
                last = jnp.where(visible, weights[start:], 0.0)
                weights = (
                    last if start == 0 else jnp.concatenate([weights[:start], last], axis=0)
                )
                score_grad = (weights * (weight_grad - delta[:, span])).astype(BF16)
                added = dot(weights.astype(BF16), grad_ext[span]) + dot(
                    score_grad, queries_ext[span]
                )
                if start > 0:
                    value_key_sum[which, :start, :] += added[:start]
                value_key_sum[which, start:end, :] = added[start:]
                query_parts[which].append(dot(keys_t[:, :end], score_grad) * HEAD**-0.5)

            waiting = None
            for which in range(2):
                for start in range(0, full, BASE):
                    with jax.named_scope("attend"):
                        begun = begin(which, start)
                        if waiting:
                            finish(*waiting)
                        waiting = (which, start) + begun
                    if which == 1 and start == 2 * BASE and index < 2:
                        coming = prepare_grads(index + 1, prepare_heads(index + 1))
                    if which == 1 and start == 0:
                        tick((AT_HALF_PAIR_0, AT_HALF_PAIR_1, AT_HALF_PAIR_2)[index])
            with jax.named_scope("attend"):
                finish(*waiting)
                parts = []
                for which in range(2):
                    parts += [jnp.concatenate(query_parts[which], axis=1).T, value_key_sum[which]]
                low = jnp.concatenate(parts, axis=1).astype(BF16)
                packed_grad[:, index * 384 : (index + 1) * 384] = low
                sums = col_sum(low.astype(F32))
            for which in range(2):
                for line in range(2):
                    first = 192 * which + 128 * line
                    piece = sums[:, first : first + 64]
                    place = (index * 2 + which) * 64
                    while place < (index * 2 + which + 1) * 64:
                        group = place // 96
                        stop = min((group + 1) * 96, (index * 2 + which + 1) * 64)
                        offset = place - (index * 2 + which) * 64
                        vectors[
                            owner_base + group,
                            15 + line : 16 + line,
                            place - group * 96 : stop - group * 96,
                        ] = piece[:, offset : offset + stop - place]
                        place = stop
            tick((AT_PAIR_0, AT_PAIR_1, AT_PAIR_2)[index])
            return coming

        def heads_weight(index):
            with jax.named_scope("heads_weight"):
                heads_parts[index] = (
                    dot_tn(whole[...], packed_grad[:, index * 384 : (index + 1) * 384])
                    .astype(BF16)
                    .reshape(2, 2, 2, 2, 48, half)
                )
            tick((AT_HEADS_WEIGHT_0, AT_HEADS_WEIGHT_1, AT_HEADS_WEIGHT_2)[index])

        with jax.named_scope("prepare"):
            first_heads = prepare_heads(0)
        with jax.named_scope("mixed_grad"):
            wait_in("mixed_grad", mixed_grad_away)
        with jax.named_scope("prepare"):
            given = prepare_grads(0, first_heads)
        for index in range(3):
            given = attend(index, given)
            if index < 2:
                heads_weight(index)
        weight_fetch.wait()
        gain = first_gain[...].reshape(1, width)
        found = [jnp.zeros((8, width), F32)] * (2 + PASSES)
        copies, tokens_sent = [], []

        def inner_of(order):
            with jax.named_scope("inner"):
                inner_away[order] = dot(
                    packed_grad[pl.ds(late_far[order], rows), :], weight[...]
                ).astype(BF16)
                copies.append(send(
                    (inner_away, order),
                    (mixed_rows, slice(order * rows, (order + 1) * rows)),
                    to_core,
                ))
                inner_kept[order] = dot(packed_grad[pl.ds(late_own[order], rows), :], weight[...])
            tick((AT_INNER_0, AT_INNER_1)[order])

        def input_of(order):
            with jax.named_scope("inner_came"):
                copies[order].wait_recv()
            with jax.named_scope("input"):
                for step in range(rows // chunk):
                    inside = slice(step * chunk, (step + 1) * chunk)
                    part = pl.ds(pl.multiple_of(late_spans[order] + step * chunk, 32), chunk)
                    unit, scale = normalize(embedded[part, :])
                    inner = inner_kept[order, inside, :] + mixed_rows[
                        order * rows + step * chunk : order * rows + (step + 1) * chunk, :
                    ].astype(F32)
                    scaled = inner * gain
                    grad = middle_grad[part, :] + scale * (
                        scaled - row_mean(scaled) - unit * row_mean(scaled * unit)
                    )
                    middle_grad[part, :] = grad
                    found[0] += fold(inner * unit)
                    found[1] += fold(inner)
                    if order == 0:
                        tokens_away[inside, :] = grad.astype(BF16)
                        if step % 5 == 4:
                            piece = slice((step - 4) * chunk, (step + 1) * chunk)
                            tokens_sent.append(
                                send((tokens_away, piece), (tokens_came_hbm, piece), to_seq)
                            )

        def sections_of(order):
            with jax.named_scope("sections"):
                for step in range(rows // chunk):
                    part = pl.ds(pl.multiple_of(late_spans[order] + step * chunk, 32), chunk)
                    grad = middle_grad[part, :]
                    place = (late_blocks[order] * 2 + core) * rows + step * chunk + chunk_places
                    section = lax.rem(place, count)
                    for section_id in range(PASSES):
                        found[2 + section_id] += fold(jnp.where(section == section_id, grad, 0.0))

        inner_of(0)
        heads_weight(2)
        input_of(0)
        tick(AT_INPUT_0)
        inner_of(1)
        sections_of(0)
        input_of(1)
        tokens_kept = fetch((middle_grad, pl.ds(late_spans[1], rows)), tokens_kept_hbm)
        sections_of(1)
        for line, value in enumerate(found):
            value = col_sum(value)
            for group in range(8):
                vectors[group, 8 + line : 9 + line, :96] = value[:, group * 96 : (group + 1) * 96]
        tick(AT_INPUT_1)
        for name in ENDING:
            chains[name].step()
        for each in chains.values():
            while not each.done:
                each.step()
        with jax.named_scope("ends"):
            for copy in tokens_sent:
                copy.wait_recv()
            out_sent[0].wait_recv()
            tokens_kept.wait()
            out_kept.wait()
            for copy in sent:
                copy.wait_send()
            wait_out("mixed", (mixed_rows, every, slice(0, half)))
            wait_out("mixed_grad", mixed_grad_away)
            wait_out("owners", (vector_owners, slice(0, 7)))
            wait_out("heads_sum", (vector_heads, slice(0, 3)))
            finals = {}
            for name, each in chains.items():
                if each.group:
                    finals[each.group[0]] = each.group[1]
                    wait_out(name, each.group[3])
            for kind, final in finals.items():
                lead = (core,) if kind == SQUARE_KIND else (every, core)
                wait_out((kind,), (final,) + lead)
            for copy in writes:
                copy.wait()

    pl.run_scoped(
        back_phase,
        pltpu.VMEM((1152, width), BF16),
        pltpu.VMEM((full, 1152), BF16),
        pltpu.VMEM((2, rows, width), F32),
        pltpu.VMEM((2, rows, width), BF16),
        pltpu.VMEM((2, full, 2 * HEAD), F32),
        pltpu.VMEM((rows, width), BF16),
    )


def swap(value, axis, bit):
    count = lax.axis_size(axis)
    return lax.ppermute(value, axis, [(place, place ^ bit) for place in range(count)])


def call(kernel, out_shapes, args, scratch=(), flops=0, moved=0):
    specs = [pl.BlockSpec(memory_space=pltpu.SMEM)] + [
        pl.BlockSpec(memory_space=pltpu.VMEM) for _ in args[1:]
    ]
    return pl.pallas_call(
        kernel,
        out_shape=tuple(jax.ShapeDtypeStruct(*item) for item in out_shapes),
        in_specs=specs,
        scratch_shapes=[pltpu.VMEM(*item) for item in scratch],
        compiler_params=pltpu.CompilerParams(vmem_limit_bytes=VMEM_LIMIT),
        cost_estimate=pl.CostEstimate(flops=flops, bytes_accessed=moved, transcendentals=0),
    )(*args)


def finish_kernel(
    tokens_kept, tokens_came, out, up_final, down_final, square_final, heads_final, vectors,
    out_result, tokens_result, first_gain, first_shift, heads, query_bias, value_bias, square,
    out_bias, second_gain, second_shift, up, up_bias, down, down_bias, table,
    came_low, up_low, down_low, square_low, heads_low, out_low, kept_wide,
    came_wide, up_wide, down_wide, square_wide, heads_wide, sems,
):
    seq = lax.axis_index("head") // 2
    pairs = [
        (up_final, up_low),
        (down_final, down_low),
        (tokens_came, came_low),
        (heads_final, heads_low),
        (square_final, square_low),
        (out, out_low),
        (tokens_kept, kept_wide),
        (out_low, out_result),
        (kept_wide, tokens_result.at[seq]),
        (up_wide, up),
        (down_wide, down),
        (came_wide, tokens_result.at[1 - seq]),
        (heads_wide, heads),
        (square_wide, square),
    ]
    copies = [
        pltpu.make_async_copy(source, target, sems.at[place])
        for place, (source, target) in enumerate(pairs)
    ]
    for copy in copies[:7]:
        copy.start()
    copies[0].wait()
    for side in range(2):
        for step in range(3):
            for group in range(4):
                first = (side * 4 + group) * 384 + step * 128
                for part in range(2):
                    up_wide[part * 48 : (part + 1) * 48, first : first + 128] = up_low[
                        step, side, part, :, group * 128 : (group + 1) * 128
                    ].astype(F32)
    copies[9].start()
    copies[1].wait()
    for side in range(2):
        for step in range(3):
            for part in range(2):
                first = step * 128 + part * 64
                down_wide[first : first + 64, side * 384 : (side + 1) * 384] = down_low[
                    step, side, part
                ].astype(F32)
    copies[10].start()
    copies[2].wait()
    came_wide[...] = came_low[...].astype(F32)
    copies[11].start()
    copies[3].wait()
    for side in range(2):
        for part in range(2):
            for index in range(3):
                for which in range(2):
                    heads_wide[
                        side * 6 + index * 2 + which, part * 48 : (part + 1) * 48, :
                    ] = heads_low[
                        index, side, part, :, which * 192 : (which + 1) * 192
                    ].astype(F32)
    copies[12].start()
    copies[4].wait()
    for side in range(2):
        for part in range(2):
            square_wide[part * 48 : (part + 1) * 48, side * 384 : (side + 1) * 384] = square_low[
                side, part
            ].astype(F32)
    copies[13].start()
    for place in (5, 6):
        copies[place].wait()
        copies[place + 2].start()
    second_gain[...] = vectors[0, :96]
    second_shift[...] = vectors[1, :96]
    out_bias[...] = vectors[2, :96]
    down_bias[...] = vectors[3, :96]
    up_bias[...] = jnp.concatenate(
        [vectors[4:5, :], vectors[5:6, :], vectors[6:7, :]], axis=1
    ).reshape(384)
    first_gain[...] = vectors[8, :96]
    first_shift[...] = vectors[9, :96]
    table[...] = vectors[10:15, :96]
    query_bias[...] = vectors[15, :96]
    value_bias[...] = vectors[16, :96]
    for copy in copies[7:]:
        copy.wait()


def fused_layer(
    tokens, passes, first_gain, first_shift, heads_weight, query_bias, value_bias, output_weight,
    output_bias, second_gain, second_shift, up_weight, up_bias, down_weight, down_bias,
    pass_embed, cotangent,
):
    rows, width, half, full = 320, 768, 384, 1280
    weight_t = heads_weight.transpose(1, 2, 0).reshape(3 * width, width)

    def lands(lead, count, wide):
        return (
            pltpu.VMEM(lead + (2, 2, 2, count, wide), BF16),
            pltpu.VMEM(lead + (2, 2, count, wide), BF16),
            pltpu.VMEM(lead + (2, count, wide), BF16),
            pltpu.VMEM(lead + (2, count, wide), BF16),
        )

    def sums(lines):
        return (
            pltpu.VMEM((8, lines, 128), F32),
            pltpu.VMEM((8, lines, 128), F32),
            pltpu.VMEM((lines, 128), F32),
            pltpu.VMEM((4, lines, 128), F32),
        )

    scratch = (
        pltpu.VMEM((2, rows, width), BF16),
        pltpu.VMEM((2 * rows, width), F32),
        pltpu.VMEM((width, width), BF16),
        pltpu.VMEM((2, width, 1024), BF16),
        pltpu.VMEM((2, 1024, width), BF16),
        pltpu.VMEM((full, width), BF16),
        pltpu.VMEM((full, 3 * half), BF16),
        pltpu.VMEM((full, half), BF16),
        pltpu.VMEM((2 * rows, width), BF16),
        pltpu.VMEM((3, 2, full), F32),
        pltpu.VMEM((2 * rows, width), F32),
        pltpu.VMEM((full, half), BF16),
        pltpu.VMEM((2 * rows, half), BF16),
        pltpu.VMEM((3, 2, 2, 2, 2, 2, 48, 512), BF16),
        pltpu.VMEM((2, 2, 2, 2, 2, 48, 512), BF16),
        lands((3,), 48, 512),
        pltpu.VMEM((3, 2, 2, 2, 2, 2, 64, half), BF16),
        pltpu.VMEM((2, 2, 2, 2, 2, 64, half), BF16),
        lands((3,), 64, half),
        pltpu.VMEM((2, 2, 2, 2, 2, 48, half), BF16),
        pltpu.VMEM((2, 2, 2, 2, 48, half), BF16),
        lands((), 48, half),
        pltpu.VMEM((3, 2, 2, 2, 2, 48, half), BF16),
        lands((3,), 48, half),
        pltpu.VMEM((3, 2, 2, 48, 512), BF16),
        pltpu.VMEM((3, 2, 2, 64, half), BF16),
        pltpu.VMEM((2, 2, 48, half), BF16),
        pltpu.VMEM((3, 2, 2, 48, half), BF16),
        *sums(24),
        pltpu.SemaphoreType.DMA((SENDS,)),
        pltpu.SemaphoreType.DMA((RECEIVES,)),
        pltpu.SemaphoreType.DMA((FETCHES,)),
    )
    any_space = pl.BlockSpec(memory_space=pl.ANY)
    vmem = pl.BlockSpec(memory_space=pltpu.VMEM)

    def shapes(*items):
        return tuple(jax.ShapeDtypeStruct(*item) for item in items)

    found = pl.pallas_call(
        main_kernel,
        out_shape=shapes(
            ((2, rows, width), BF16),
            ((rows, width), F32),
            ((rows, width), BF16),
            ((3, 2, 2, 48, 512), BF16),
            ((3, 2, 2, 64, half), BF16),
            ((2, 2, 48, half), BF16),
            ((3, 2, 2, 48, half), BF16),
            ((24, 128), F32),
        ),
        in_specs=[pl.BlockSpec(memory_space=pltpu.SMEM)] + [vmem] * 10 + [any_space] * 6,
        out_specs=(any_space,) * 7 + (vmem,),
        scratch_shapes=scratch,
        compiler_params=pltpu.CompilerParams(
            vmem_limit_bytes=64 * 2**20, collective_id=0, has_side_effects=True
        ),
    )(
        passes, first_gain, first_shift, query_bias, value_bias, output_bias, second_gain,
        second_shift, up_bias, down_bias, pass_embed, tokens, cotangent, weight_t, output_weight,
        up_weight, down_weight,
    )
    out, tokens_kept, tokens_came, up, down, square, heads, vectors = found
    wide = (any_space, any_space, vmem, vmem, any_space, vmem, vmem, any_space)
    results = pl.pallas_call(
        finish_kernel,
        out_shape=shapes(
            ((2, rows, width), BF16),
            ((2, rows, width), F32),
            ((96,), F32),
            ((96,), F32),
            ((HEADS, 96, 192), F32),
            ((96,), F32),
            ((96,), F32),
            ((96, width), F32),
            ((96,), F32),
            ((96,), F32),
            ((96,), F32),
            ((96, 3072), F32),
            ((384,), F32),
            ((384, width), F32),
            ((96,), F32),
            ((PASSES, 96), F32),
        ),
        in_specs=[any_space] * 7 + [vmem],
        out_specs=wide + (vmem, vmem, vmem, any_space, vmem, any_space, vmem, vmem),
        scratch_shapes=[
            pltpu.VMEM((rows, width), BF16),
            pltpu.VMEM((3, 2, 2, 48, 512), BF16),
            pltpu.VMEM((3, 2, 2, 64, half), BF16),
            pltpu.VMEM((2, 2, 48, half), BF16),
            pltpu.VMEM((3, 2, 2, 48, half), BF16),
            pltpu.VMEM((2, rows, width), BF16),
            pltpu.VMEM((rows, width), F32),
            pltpu.VMEM((rows, width), F32),
            pltpu.VMEM((96, 3072), F32),
            pltpu.VMEM((384, width), F32),
            pltpu.VMEM((96, width), F32),
            pltpu.VMEM((HEADS, 96, 192), F32),
            pltpu.SemaphoreType.DMA((14,)),
        ],
        compiler_params=pltpu.CompilerParams(vmem_limit_bytes=VMEM_LIMIT),
    )(tokens_kept, tokens_came, out, up, down, square, heads, vectors)
    return results[:4] + (results[4].transpose(1, 0, 2),) + results[5:]


def both(left, right):
    return (left.astype(F32) + right.astype(F32)).astype(BF16)


def halve(value, axis, bit):
    mine = (lax.axis_index(axis) // bit) % 2
    pairs = value.reshape((value.shape[0] // 2, 2) + value.shape[1:])
    kept = lax.dynamic_index_in_dim(pairs, mine, 1, keepdims=False)
    away = lax.dynamic_index_in_dim(pairs, 1 - mine, 1, keepdims=False)
    return both(kept, swap(away, axis, bit))


def over_owners(value):
    bit = 1
    while bit < lax.axis_size("dp"):
        value = halve(value, "dp", bit)
        bit *= 2
    return value[0]


def total_share(value):
    count = value.shape[1] // 2
    seq = lax.axis_index("head") // 2
    first = over_owners(value[:, :count])
    first = both(first, swap(first, "head", 2))
    second = jnp.swapaxes(value[:, count:].reshape(value.shape[0], 2, -1, value.shape[2]), 0, 1)
    kept = lax.dynamic_index_in_dim(second, seq, 0, keepdims=False)
    away = lax.dynamic_index_in_dim(second, 1 - seq, 0, keepdims=False)
    second = over_owners(both(kept, swap(away, "head", 2)))
    other = swap(second, "head", 2)
    low_part = jnp.where(seq == 0, second, other)
    high_part = jnp.where(seq == 0, other, second)
    return jnp.concatenate([first, low_part, high_part], axis=0)


def on_device(
    tokens,
    passes,
    first_gain,
    first_shift,
    heads_weight,
    query_bias,
    value_bias,
    output_weight,
    output_bias,
    second_gain,
    second_shift,
    upward_weight,
    upward_bias,
    downward_weight,
    downward_bias,
    pass_embed,
    cotangent,
):
    owners = lax.axis_size("dp")
    _, rows, width = tokens.shape
    hidden = upward_weight.shape[1]
    half = width // 2
    full = 4 * rows
    if owners == 8 and (rows, width, hidden) == (320, 768, 3072):
        return fused_layer(
            tokens, passes, first_gain, first_shift, heads_weight, query_bias, value_bias,
            output_weight, output_bias, second_gain, second_shift, upward_weight, upward_bias,
            downward_weight, downward_bias, pass_embed, cotangent,
        )
    place = lax.axis_index("head")
    core, seq = place % 2, place // 2
    count = lax.dynamic_index_in_dim(passes, seq, 0, keepdims=False)
    scalars = jnp.stack([core, seq, count]).astype(jnp.int32)

    def pick(array, index, axis=0):
        return lax.dynamic_index_in_dim(array, index, axis, keepdims=False)

    tokens_came = swap(pick(tokens, 1 - seq), "head", 2)
    cot_came = swap(pick(cotangent, 1 - seq), "head", 2)
    row = lambda vector: vector.reshape(1, -1)
    weight_t = heads_weight.transpose(1, 2, 0).reshape(2, 3 * half, width)
    weight_own = pick(weight_t, core)
    bias_table = jnp.concatenate(
        [
            query_bias.reshape(HEADS, HEAD),
            jnp.zeros((HEADS, HEAD), F32),
            value_bias.reshape(HEADS, HEAD),
        ],
        axis=1,
    ).reshape(2, 1, 3 * half)
    bias_own = pick(bias_table, core)

    embedded, normed = call(
        embed_kernel,
        [((2 * rows, width), F32), ((2 * rows, width), BF16)],
        (
            scalars,
            pick(tokens, seq),
            tokens_came,
            pass_embed,
            row(first_gain),
            row(first_shift),
        ),
        moved=10 * 2**20,
    )
    normed_came = swap(normed, "head", 1)
    whole, packed, mixed, mixed_kept, mixed_away, log_total = call(
        forward_kernel,
        [
            ((full, width), BF16),
            ((full, 3 * half), BF16),
            ((full, half), BF16),
            ((2 * rows, half), BF16),
            ((2 * rows, half), BF16),
            ((HEADS // 4, 2, full), F32),
        ],
        (scalars, normed, normed_came, weight_own, bias_own),
        moved=70 * 2**20,
    )
    mixed_came = swap(mixed_away, "head", 1)
    up_rows, down_rows = width // owners, hidden // owners
    out_kept, out_away, middle_grad, mg_kept, mg_away, grads, row_sums, up_sums = call(
        feed_kernel,
        [
            ((rows, width), BF16),
            ((rows, width), BF16),
            ((2 * rows, width), F32),
            ((2 * rows, half), BF16),
            ((2 * rows, half), BF16),
            ((2, owners, 5 * up_rows + down_rows, half), BF16),
            ((8, width), F32),
            ((1, hidden), F32),
        ],
        (
            scalars,
            mixed_kept,
            mixed_came,
            embedded,
            pick(cotangent, seq),
            cot_came,
            output_weight,
            row(output_bias),
            row(second_gain),
            row(second_shift),
            upward_weight,
            row(upward_bias),
            downward_weight,
            row(downward_bias),
        ),
        scratch=[
            ((2 * rows, width), BF16),
            ((2 * rows, width), F32),
            ((2 * rows, width), BF16),
            ((width, 2 * rows), BF16),
            ((2 * rows, width), BF16),
            ((2 * rows, width), F32),
            ((2 * rows, width), F32),
        ],
        moved=120 * 2**20,
    )
    mg_came = swap(mg_away, "head", 1)
    out_came = swap(out_away, "head", 2)
    share = both(pick(grads, core), swap(pick(grads, 1 - core), "head", 1))
    inner_kept, inner_away, heads_grad, bias_sums = call(
        backward_kernel,
        [
            ((2 * rows, width), F32),
            ((2 * rows, width), BF16),
            ((owners, 3 * up_rows, half), BF16),
            ((1, 3 * half), F32),
        ],
        (
            scalars,
            packed,
            log_total,
            mixed_kept,
            mixed_away,
            mg_kept,
            mg_came,
            whole,
            weight_own,
        ),
        scratch=[
            ((full, half), BF16),
            ((full, half), BF16),
            ((full, 3 * half), BF16),
            ((full, width), F32),
            ((2, full, 2 * HEAD), F32),
        ],
        moved=100 * 2**20,
    )
    inner_came = swap(inner_away, "head", 1)
    grad_kept, grad_away, sums = call(
        input_kernel,
        [((rows, width), F32), ((rows, width), BF16), ((8, width), F32)],
        (scalars, inner_kept, inner_came, embedded, middle_grad, row(first_gain)),
        moved=10 * 2**20,
    )
    grad_came = swap(grad_away, "head", 2).astype(F32)

    def place_rows(kept, came):
        return jnp.stack([jnp.where(seq == 0, kept, came), jnp.where(seq == 0, came, kept)])

    bias_parts = jnp.where(
        (jnp.arange(2) == core)[:, None], bias_sums, 0.0
    ).reshape(HEADS, 3, HEAD)
    vectors = jnp.concatenate(
        [
            sums[:7],
            row_sums[:4],
            bias_parts[:, 0].reshape(1, width),
            bias_parts[:, 2].reshape(1, width),
            up_sums.reshape(-1, width // owners, owners).reshape(-1, width),
        ],
        axis=0,
    )
    vectors = lax.psum(vectors, ("dp", "head"))
    owner = lax.axis_index("dp")
    mine = lax.dynamic_slice_in_dim(vectors[:13], owner * up_rows, up_rows, 1)
    up_mine = lax.dynamic_slice_in_dim(vectors[13:].reshape(-1), owner * down_rows, down_rows, 0)

    share = total_share(share)
    share = jnp.stack([share, swap(share, "head", 1)])
    heads_share = total_share(heads_grad)
    heads_share = jnp.stack([heads_share, swap(heads_share, "head", 1)])
    share = jnp.where(core == 0, share, share[::-1]).astype(F32)
    heads_share = jnp.where(core == 0, heads_share, heads_share[::-1]).astype(F32)
    up_share = share[:, : 4 * up_rows].reshape(8, up_rows, half)
    up_share = up_share.transpose(1, 0, 2).reshape(up_rows, hidden)
    down_share = share[:, 4 * up_rows : 4 * up_rows + down_rows]
    down_share = down_share.transpose(1, 0, 2).reshape(down_rows, width)
    out_share = share[:, 4 * up_rows + down_rows :].transpose(1, 0, 2).reshape(up_rows, width)
    heads_share = heads_share.reshape(6, up_rows, half).transpose(1, 0, 2)
    heads_share = heads_share.reshape(up_rows, HEADS, 3 * HEAD)
    return (
        place_rows(out_kept, out_came),
        place_rows(grad_kept, grad_came),
        mine[0],
        mine[1],
        heads_share,
        mine[11],
        mine[12],
        out_share,
        mine[9],
        mine[7],
        mine[8],
        up_share,
        up_mine,
        down_share,
        mine[10],
        mine[2:7],
    )


def solution(mesh):
    rows_spec = P("dp", "head", None)
    in_specs = (rows_spec, P("dp")) + (P(),) * 14 + (rows_spec,)
    out_specs = (
        rows_spec,
        rows_spec,
        P("dp"),
        P("dp"),
        P("dp", None, None),
        P("dp"),
        P("dp"),
        P("dp", None),
        P("dp"),
        P("dp"),
        P("dp"),
        P("dp", None),
        P("dp"),
        P("dp", None),
        P("dp"),
        P(None, "dp"),
    )
    return jax.shard_map(
        on_device, mesh=mesh, in_specs=in_specs, out_specs=out_specs, check_vma=False
    )
```

```python
import functools

import jax
import jax.numpy as jnp
from jax import lax
from jax.experimental import pallas as pl
from jax.experimental.pallas import tpu as pltpu
from jax.sharding import PartitionSpec as P

HEADS = 12
HEAD = 64
BASE = 256
PASSES = 5
NEG_FILL = -1e30
EPSILON = 1e-05
TANH_IN = 0.7978845608028654
TANH_CUBE = 0.044715
F32 = jnp.float32
BF16 = jnp.bfloat16
VMEM_LIMIT = 60 * 2**20


def dot(left, right):
    return jnp.dot(left, right, preferred_element_type=F32)


def dot_nt(left, right):
    return lax.dot_general(
        left, right, (((1,), (1,)), ((), ())), preferred_element_type=F32
    )


def dot_tn(left, right):
    return lax.dot_general(
        left, right, (((0,), (0,)), ((), ())), preferred_element_type=F32
    )


def row_mean(block):
    return jnp.mean(block, axis=1, keepdims=True)


def col_sum(block):
    return jnp.sum(block, axis=0, keepdims=True)


def normalize(block):
    centre = block - row_mean(block)
    scale = lax.rsqrt(row_mean(centre * centre) + EPSILON)
    return centre * scale, scale


def places_of(block_id, core, half, rows):
    start = (block_id * half + core) * rows
    return start + lax.broadcasted_iota(jnp.int32, (rows, 1), 0)


def embed_kernel(scalars, kept, came, table, gain, shift, embedded, normed):
    core, seq, count = scalars[0], scalars[1], scalars[2]
    rows = kept.shape[0]
    for block_id in range(2):
        section = lax.rem(places_of(block_id, core, 2, rows), count)
        mine = kept[...].astype(F32)
        other = came[...].astype(F32)
        hidden = jnp.where(seq == block_id, mine, other)
        added = jnp.zeros_like(hidden)
        for section_id in range(PASSES):
            added = jnp.where(section == section_id, table[section_id : section_id + 1, :], added)
        hidden = hidden + added
        span = pl.ds(block_id * rows, rows)
        embedded[span, :] = hidden
        unit, _ = normalize(hidden)
        normed[span, :] = (unit * gain[...] + shift[...]).astype(BF16)


def gather_rows(core, kept, came, whole):
    rows = kept.shape[0] // 2
    for block_id in range(2):
        span = slice(block_id * rows, (block_id + 1) * rows)
        whole[pl.ds(pl.multiple_of((block_id * 2 + core) * rows, 64), rows), :] = kept[span, :]
        whole[pl.ds(pl.multiple_of((block_id * 2 + 1 - core) * rows, 64), rows), :] = came[span, :]


def split_rows(core, whole, kept, away):
    rows = kept.shape[0] // 2
    for block_id in range(2):
        span = slice(block_id * rows, (block_id + 1) * rows)
        kept[span, :] = whole[
            pl.ds(pl.multiple_of((block_id * 2 + core) * rows, 64), rows), :
        ].astype(kept.dtype)
        away[span, :] = whole[
            pl.ds(pl.multiple_of((block_id * 2 + 1 - core) * rows, 64), rows), :
        ].astype(away.dtype)


def head_parts(block, which):
    start = 3 * HEAD * which
    queries = block[:, start : start + HEAD] * jnp.asarray(HEAD**-0.5, BF16)
    keys = block[:, start + HEAD : start + 2 * HEAD]
    values = block[:, start + 2 * HEAD : start + 3 * HEAD]
    return queries, keys, values


def causal_block(size):
    key_place = lax.broadcasted_iota(jnp.int32, (size, size), 0)
    query_place = lax.broadcasted_iota(jnp.int32, (size, size), 1)
    return key_place <= query_place


def forward_kernel(
    scalars, kept, came, weight, bias, whole, packed, mixed, mixed_kept, mixed_away, log_total
):
    core = scalars[0]
    full = whole.shape[0]
    gather_rows(core, kept, came, whole)
    for start in range(0, full, BASE):
        span = pl.ds(start, BASE)
        packed[span, :] = (dot_nt(whole[span, :], weight[...]) + bias[...]).astype(BF16)
    visible = causal_block(BASE)

    def pair(index, carry):
        block = packed[:, pl.ds(pl.multiple_of(index * 6 * HEAD, 128), 6 * HEAD)]
        results, logs = [], []
        for which in range(2):
            queries, keys, values = head_parts(block, which)
            values_ext = jnp.concatenate([values.T, jnp.ones((16, full), BF16)], axis=0)
            outs, totals = [], []
            for start in range(0, full, BASE):
                end = start + BASE
                scores = dot_nt(keys[:end], queries[start:end])
                last = jnp.where(visible, scores[start:], NEG_FILL)
                scores = last if start == 0 else jnp.concatenate([scores[:start], last], axis=0)
                top = jnp.max(scores, axis=0, keepdims=True)
                raised = jnp.exp(scores - top).astype(BF16)
                grown = dot(values_ext[:, :end], raised)
                total = grown[HEAD : HEAD + 1]
                outs.append(grown[:HEAD] / total)
                totals.append(top + jnp.log(total))
            results.append(jnp.concatenate(outs, axis=1))
            logs.append(jnp.concatenate(totals, axis=1))
        mixed[:, pl.ds(pl.multiple_of(index * 2 * HEAD, 128), 2 * HEAD)] = jnp.concatenate(
            results, axis=0
        ).T.astype(BF16)
        log_total[index] = jnp.concatenate(logs, axis=0)
        return carry

    lax.fori_loop(0, HEADS // 4, pair, 0)
    split_rows(core, mixed, mixed_kept, mixed_away)


def feed_kernel(
    scalars,
    mixed_kept,
    mixed_came,
    embedded,
    cot_kept,
    cot_came,
    out_weight,
    out_bias,
    gain,
    shift,
    up_weight,
    up_bias,
    down_weight,
    down_bias,
    out_kept,
    out_away,
    middle_grad,
    mixed_grad_kept,
    mixed_grad_away,
    grads,
    row_sums,
    up_sums,
    mixed,
    middle,
    normed,
    normed_t,
    out_grad,
    branch,
    normed_grad,
):
    core, seq, count = scalars[0], scalars[1], scalars[2]
    total_rows, width = middle.shape
    rows = total_rows // 2
    half = width // 2
    hidden = up_weight.shape[1]
    owners = grads.shape[1]
    up_rows = width // owners
    down_rows = hidden // owners
    mixed[:, pl.ds(pl.multiple_of(core * half, 128), half)] = mixed_kept[...]
    mixed[:, pl.ds(pl.multiple_of((1 - core) * half, 128), half)] = mixed_came[...]
    valid = []
    for block_id in range(2):
        span = slice(block_id * rows, (block_id + 1) * rows)
        value = embedded[span, :] + dot(mixed[span, :], out_weight[...]) + out_bias[...]
        middle[span, :] = value
        unit, _ = normalize(value)
        normed[span, :] = (unit * gain[...] + shift[...]).astype(BF16)
        keep = places_of(block_id, core, 2, rows) < count * BASE
        valid.append(keep)
        cot = jnp.where(seq == block_id, cot_kept[...].astype(F32), cot_came[...].astype(F32))
        out_grad[span, :] = jnp.where(keep, cot, 0.0).astype(BF16)
    normed_t[...] = normed[...].T
    branch[...] = jnp.zeros_like(branch)
    normed_grad[...] = jnp.zeros_like(normed_grad)
    tile = 2 * half
    for step in range(hidden // tile):
        cols = pl.ds(step * tile, tile)
        value = dot(normed[...], up_weight[:, cols]) + up_bias[:, cols]
        square = value * value
        tanh = jnp.tanh(value * (TANH_IN + TANH_IN * TANH_CUBE * square))
        gate = 0.5 + 0.5 * tanh
        activated = (value * gate).astype(BF16)
        slope = gate + (0.5 * value) * (1.0 - tanh * tanh) * (
            TANH_IN + 3.0 * TANH_IN * TANH_CUBE * square
        )
        up_grad = (dot_nt(out_grad[...], down_weight[cols, :]) * slope).astype(BF16)
        branch[...] += dot(activated, down_weight[cols, :])
        normed_grad[...] += dot_nt(up_grad, up_weight[:, cols])
        up_sums[:, cols] = col_sum(up_grad.astype(F32))
        up_part = dot(normed_t[...], up_grad).astype(BF16)
        down_part = dot_tn(activated, out_grad[...]).astype(BF16)
        for sub in range(2):
            slot = (step * 2 + sub) % 4
            side = (step * 2 + sub) // 4
            for owner in range(owners):
                grads[side, owner, slot * up_rows : (slot + 1) * up_rows, :] = up_part[
                    owner * up_rows : (owner + 1) * up_rows, sub * half : (sub + 1) * half
                ]
        for owner in range(owners):
            first = max(owner * down_rows, step * tile)
            last = min((owner + 1) * down_rows, (step + 1) * tile)
            if first < last:
                place = 4 * up_rows + first - owner * down_rows
                for side in range(2):
                    grads[side, owner, place : place + last - first, :] = down_part[
                        first - step * tile : last - step * tile, side * half : (side + 1) * half
                    ]
    sums = [0.0] * 4
    for block_id in range(2):
        span = slice(block_id * rows, (block_id + 1) * rows)
        value = middle[span, :]
        unit, scale = normalize(value)
        inner = normed_grad[span, :]
        scaled = inner * gain[...]
        cot = out_grad[span, :].astype(F32)
        grad = cot + scale * (scaled - row_mean(scaled) - unit * row_mean(scaled * unit))
        middle_grad[span, :] = grad
        low = grad.astype(BF16)
        normed[span, :] = low
        result = jnp.where(
            valid[block_id], value + branch[span, :] + down_bias[...], 0.0
        ).astype(BF16)

        @pl.when(seq == block_id)
        def _():
            out_kept[...] = result

        @pl.when(seq != block_id)
        def _():
            out_away[...] = result

        mixed_grad_kept[span, :] = dot_nt(
            low, out_weight[pl.ds(pl.multiple_of(core * half, 128), half), :]
        ).astype(BF16)
        mixed_grad_away[span, :] = dot_nt(
            low, out_weight[pl.ds(pl.multiple_of((1 - core) * half, 128), half), :]
        ).astype(BF16)
        terms = (inner * unit, inner, low.astype(F32), cot)
        sums = [have + col_sum(term) for have, term in zip(sums, terms)]
    row_sums[...] = jnp.concatenate(sums + [jnp.zeros((4, width), F32)], axis=0)
    out_part = dot_tn(mixed[...], normed[...]).astype(BF16)
    base_row = 4 * up_rows + down_rows
    for owner in range(owners):
        for side in range(2):
            grads[side, owner, base_row : base_row + up_rows, :] = out_part[
                owner * up_rows : (owner + 1) * up_rows, side * half : (side + 1) * half
            ]


def backward_kernel(
    scalars,
    packed,
    log_total,
    mixed_kept,
    mixed_away,
    grad_kept,
    grad_came,
    whole,
    weight,
    inner_kept,
    inner_away,
    heads_grad,
    bias_sums,
    mixed,
    mixed_grad,
    packed_grad,
    inner,
    value_key_sum,
):
    core = scalars[0]
    full = whole.shape[0]
    owners = heads_grad.shape[0]
    own_rows = heads_grad.shape[1] // 3
    gather_rows(core, mixed_kept, mixed_away, mixed)
    gather_rows(core, grad_kept, grad_came, mixed_grad)
    visible = causal_block(BASE)

    def pair(index, carry):
        base = pl.multiple_of(index * 6 * HEAD, 128)
        block = packed[:, pl.ds(base, 6 * HEAD)]
        lanes = pl.ds(pl.multiple_of(index * 2 * HEAD, 128), 2 * HEAD)
        both_grad = mixed_grad[:, lanes]
        overlap = both_grad.astype(F32) * mixed[:, lanes].astype(F32)
        parts = []
        for which in range(2):
            queries, keys, values = head_parts(block, which)
            grad = both_grad[:, HEAD * which : HEAD * (which + 1)]
            delta = jnp.sum(
                overlap[:, HEAD * which : HEAD * (which + 1)], axis=1, keepdims=True
            ).T
            logs = log_total[index][which : which + 1]
            keys_t = keys.T
            blank = jnp.zeros_like(queries)
            grad_ext = jnp.concatenate([blank, grad], axis=1)
            queries_ext = jnp.concatenate([queries, blank], axis=1)
            query_parts = []
            for start in range(0, full, BASE):
                end = start + BASE
                span = slice(start, end)
                weights = jnp.exp(dot_nt(keys[:end], queries[span]) - logs[:, span])
                last = jnp.where(visible, weights[start:], 0.0)
                weights = (
                    last if start == 0 else jnp.concatenate([weights[:start], last], axis=0)
                )
                weight_grad = dot_nt(values[:end], grad[span])
                score_grad = (weights * (weight_grad - delta[:, span])).astype(BF16)
                added = dot(weights.astype(BF16), grad_ext[span]) + dot(
                    score_grad, queries_ext[span]
                )
                if start > 0:
                    value_key_sum[which, :start, :] += added[:start]
                value_key_sum[which, start:end, :] = added[start:]
                query_parts.append(dot(keys_t[:, :end], score_grad) * HEAD**-0.5)
            parts += [jnp.concatenate(query_parts, axis=1).T, value_key_sum[which]]
        packed_grad[:, pl.ds(base, 6 * HEAD)] = jnp.concatenate(parts, axis=1).astype(BF16)
        return carry

    lax.fori_loop(0, HEADS // 4, pair, 0)
    low = packed_grad[...]
    bias_sums[...] = col_sum(low.astype(F32))
    for start in range(0, full, BASE):
        inner[pl.ds(start, BASE), :] = dot(packed_grad[pl.ds(start, BASE), :], weight[...])
    split_rows(core, inner, inner_kept, inner_away)
    part = dot_tn(whole[...], low).astype(BF16)
    third = heads_grad.shape[2]
    for owner in range(owners):
        for group in range(3):
            heads_grad[owner, group * own_rows : (group + 1) * own_rows, :] = part[
                owner * own_rows : (owner + 1) * own_rows, group * third : (group + 1) * third
            ]


def input_kernel(
    scalars, inner_kept, inner_came, embedded, middle_grad, gain, grad_kept, grad_away, sums
):
    core, seq, count = scalars[0], scalars[1], scalars[2]
    total_rows, width = embedded.shape
    rows = total_rows // 2
    found = [0.0] * (2 + PASSES)
    for block_id in range(2):
        span = slice(block_id * rows, (block_id + 1) * rows)
        unit, scale = normalize(embedded[span, :])
        inner = inner_kept[span, :] + inner_came[span, :].astype(F32)
        scaled = inner * gain[...]
        grad = middle_grad[span, :] + scale * (
            scaled - row_mean(scaled) - unit * row_mean(scaled * unit)
        )

        @pl.when(seq == block_id)
        def _():
            grad_kept[...] = grad

        @pl.when(seq != block_id)
        def _():
            grad_away[...] = grad.astype(BF16)

        section = lax.rem(places_of(block_id, core, 2, rows), count)
        terms = [inner * unit, inner]
        for section_id in range(PASSES):
            terms.append(jnp.where(section == section_id, grad, 0.0))
        found = [have + col_sum(term) for have, term in zip(found, terms)]
    sums[...] = jnp.concatenate(found + [jnp.zeros((1, width), F32)], axis=0)


MESH = pl.DeviceIdType.MESH

UP_KIND, DOWN_KIND, SQUARE_KIND, HEADS_KIND = range(4)
Z2, Z1, X, Y = range(4)

(DOWN_0A, DOWN_0B, UP_0A, UP_0B, DOWN_1A, DOWN_1B, UP_1A, UP_1B, DOWN_2A, DOWN_2B, UP_2A, UP_2B,
    SQUARE, HEADS_0, HEADS_1A, HEADS_1B, HEADS_2A, HEADS_2B, VECTORS, OUT) = range(20)
SUMS = {
    DOWN_0A: (DOWN_KIND, 0, 1, (Z1, Z2, Y, X)),
    DOWN_0B: (DOWN_KIND, 0, 2, (Y, Z1, X, Z2)),
    UP_0A: (UP_KIND, 0, 1, (Z1, X, Z2, Y)),
    UP_0B: (UP_KIND, 0, 2, (X, Z1, Z2, Y)),
    DOWN_1A: (DOWN_KIND, 1, 1, (Y, X, Z1, Z2)),
    DOWN_1B: (DOWN_KIND, 1, 2, (X, Z1, Z2, Y)),
    UP_1A: (UP_KIND, 1, 1, (Y, Z1, X, Z2)),
    UP_1B: (UP_KIND, 1, 2, (Z1, X, Z2, Y)),
    DOWN_2A: (DOWN_KIND, 2, 1, (Y, X, Z1, Z2)),
    DOWN_2B: (DOWN_KIND, 2, 2, (X, Z1, Z2, Y)),
    UP_2A: (UP_KIND, 2, 1, (Y, X, Z1, Z2)),
    UP_2B: (UP_KIND, 2, 2, (X, Z1, Z2, Y)),
    SQUARE: (SQUARE_KIND, 0, 0, (Z1, X, Y, Z2)),
    HEADS_0: (HEADS_KIND, 0, 0, (X, Y, Z1, Z2)),
    HEADS_1A: (HEADS_KIND, 1, 1, (X, Z1, Z2, Y)),
    HEADS_1B: (HEADS_KIND, 1, 2, (Y, Z1, Z2, X)),
    HEADS_2A: (HEADS_KIND, 2, 1, (X, Z1, Z2, Y)),
    HEADS_2B: (HEADS_KIND, 2, 2, (X, Z1, Z2, Y)),
}
(AT_HIDDEN_0, AT_DOWN_0, AT_UP_0, AT_BRANCH_0, AT_HIDDEN_1, AT_DOWN_1, AT_UP_1, AT_BRANCH_1,
    AT_HIDDEN_2, AT_DOWN_2, AT_UP_2, AT_BRANCH_2, AT_MIDDLE, AT_SQUARED, AT_HALF_PAIR_0,
    AT_PAIR_0, AT_HEADS_WEIGHT_0, AT_HALF_PAIR_1, AT_PAIR_1, AT_HEADS_WEIGHT_1, AT_HALF_PAIR_2,
    AT_PAIR_2, AT_INNER_0, AT_HEADS_WEIGHT_2, AT_INPUT_0, AT_INNER_1, AT_INPUT_1) = range(27)
PLAN = {
    AT_DOWN_0: (DOWN_0A, DOWN_0B),
    AT_UP_0: (UP_0A, UP_0B),
    AT_BRANCH_0: (DOWN_0A,),
    AT_HIDDEN_1: (DOWN_0B,),
    AT_DOWN_1: (UP_0A, DOWN_1A, DOWN_1B),
    AT_UP_1: (UP_0B, UP_1A, UP_1B),
    AT_BRANCH_1: (DOWN_0A, DOWN_1A),
    AT_HIDDEN_2: (DOWN_0B, DOWN_1B, UP_0A),
    AT_DOWN_2: (UP_1A, UP_0B, DOWN_2A, DOWN_2B),
    AT_UP_2: (UP_1B, UP_2A, UP_2B),
    AT_BRANCH_2: (DOWN_1A, DOWN_0A, DOWN_0B, DOWN_2A),
    AT_MIDDLE: (OUT, DOWN_1B, UP_0B, DOWN_2B, UP_1A),
    AT_SQUARED: (UP_0A, UP_2A, DOWN_0A, SQUARE),
    AT_HALF_PAIR_0: (UP_2B, DOWN_1A, UP_1B, DOWN_0B, DOWN_2A, SQUARE),
    AT_PAIR_0: (DOWN_1B, UP_0B, UP_1A, DOWN_2B, DOWN_0A, DOWN_1A, UP_0A),
    AT_HEADS_WEIGHT_0: (DOWN_0B, UP_2B, HEADS_0),
    AT_HALF_PAIR_1: (UP_1B, DOWN_1B),
    AT_PAIR_1: (DOWN_2A, UP_1A, SQUARE),
    AT_HEADS_WEIGHT_1: (UP_2A, DOWN_2B, UP_0B, DOWN_1A, DOWN_0A, HEADS_1A, HEADS_1B),
    AT_HALF_PAIR_2: (UP_0A, UP_2B, DOWN_0B, UP_0B, DOWN_0A, DOWN_1B, HEADS_0, DOWN_1A, DOWN_2A,
        UP_1B),
    AT_PAIR_2: (UP_1A, HEADS_1B, UP_0A, SQUARE, DOWN_0B, DOWN_1B, DOWN_1A, DOWN_2B),
    AT_INNER_0: (UP_2A, HEADS_0, UP_2B, UP_1B, DOWN_2A),
    AT_HEADS_WEIGHT_2: (UP_1A, HEADS_1B, HEADS_2A, HEADS_2B),
    AT_INPUT_0: (SQUARE, UP_1B, HEADS_1A),
    AT_INNER_1: (UP_2A, DOWN_2B, UP_1A, UP_2B, HEADS_0, DOWN_2A),
    AT_INPUT_1: (HEADS_1B, VECTORS),
}
ENDING = (DOWN_2B, UP_2B, SQUARE, DOWN_2A, HEADS_2A, HEADS_1A, HEADS_2B, UP_2A, HEADS_1B, HEADS_0,
    VECTORS, HEADS_2A, HEADS_1A, HEADS_2B, SQUARE, UP_2A, HEADS_2A, HEADS_1B, HEADS_0, HEADS_2B,
    SQUARE, UP_2A, HEADS_1B, HEADS_1A, HEADS_0, VECTORS, HEADS_2A, HEADS_2B, HEADS_1A, HEADS_2A,
    HEADS_2B)

SENDS, RECEIVES, FETCHES = 37, 127, 17


def add_low(left, right):
    return (left.astype(F32) + right.astype(F32)).astype(BF16)


def main_kernel(
    passes,
    first_gain,
    first_shift,
    query_bias,
    value_bias,
    out_bias,
    second_gain,
    second_shift,
    up_bias,
    down_bias,
    table,
    tokens_in,
    cot_in,
    weight_hbm,
    out_weight_hbm,
    up_weight_hbm,
    down_weight_hbm,
    out_hbm,
    tokens_kept_hbm,
    tokens_came_hbm,
    up_hbm,
    down_hbm,
    square_hbm,
    heads_hbm,
    vectors_out,
    landed,
    embedded,
    out_weight,
    up_weight,
    down_weight,
    whole,
    packed,
    mixed,
    mixed_rows,
    log_total,
    middle_grad,
    mixed_grad,
    mixed_grad_away,
    up_parts,
    up_core,
    up_land,
    down_parts,
    down_core,
    down_land,
    square_parts,
    square_core,
    square_land,
    heads_parts,
    heads_land,
    up_final,
    down_final,
    square_final,
    heads_final,
    vectors,
    vector_owners,
    vector_total,
    vector_heads,
    send_sems,
    recv_sems,
    local_sems,
):
    dp, head = lax.axis_index("dp"), lax.axis_index("head")
    core, seq = head % 2, head // 2
    bit0, bit1, bit2 = dp % 2, (dp // 2) % 2, dp // 4
    far_core, far_seq = 1 - core, 1 - seq
    far0, far1, far2 = 1 - bit0, 1 - bit1, 1 - bit2
    to_core = {"head": head + far_core - core}
    to_seq = {"head": head + 2 * (far_seq - seq)}
    to0 = {"dp": dp + far0 - bit0}
    to1 = {"dp": dp + 2 * (far1 - bit1)}
    to2 = {"dp": dp + 4 * (far2 - bit2)}
    head_peers = [lax.rem(head + step, 4) for step in range(1, 4)]
    dp_peers = [lax.rem(dp + step, 8) for step in range(1, 8)]
    own_half = pl.multiple_of(core * 384, 128)
    far_half = pl.multiple_of(far_core * 384, 128)
    own_starts = [pl.multiple_of((block * 2 + core) * 320, 64) for block in range(2)]
    far_starts = [pl.multiple_of((block * 2 + far_core) * 320, 64) for block in range(2)]
    late_blocks = [far_seq, seq]
    late_own = [pl.multiple_of((block * 2 + core) * 320, 64) for block in late_blocks]
    late_far = [pl.multiple_of((block * 2 + far_core) * 320, 64) for block in late_blocks]
    late_spans = [pl.multiple_of(block * 320, 64) for block in late_blocks]
    owner_base = core * 4
    out_slots = [1 - seq, seq]
    own_weight = pl.multiple_of(core * 1152, 128)
    own_lanes = [pl.multiple_of(core * 384 + index * 128, 128) for index in range(3)]
    count = passes[seq]
    length = count * BASE
    own_second = pl.multiple_of((far_seq * 2 + core) * 320 + 160, 32)
    flat_starts = [pl.multiple_of(block * 320, 64) for block in (seq, far_seq)]
    front_own = [pl.multiple_of((block * 2 + core) * 320, 64) for block in (seq, far_seq)]
    front_far = [pl.multiple_of((block * 2 + far_core) * 320, 64) for block in (seq, far_seq)]
    rows, total_rows, width, half, full, tile = 320, 640, 768, 384, 1280, 1024

    sent = []
    used = [0, 0, 0]

    def view(place):
        if isinstance(place, tuple):
            return place[0].at[place[1:]]
        return place

    groups = {}

    def place_of(kind, group):
        if group is None:
            used[kind] += 1
            return used[kind] - 1
        if (kind, group) not in groups:
            groups[kind, group] = used[kind]
            used[kind] += 1
        return groups[kind, group]

    class Sent:
        def __init__(self, source, target, device, out_group, in_group):
            self.out_place = place_of(0, out_group) if out_group != "" else 0
            self.in_place = place_of(1, in_group) if in_group != "" else 0
            self.parts = (source, target, device)
            self.left = False

        def make(self):
            source, target, device = self.parts
            return pltpu.make_async_remote_copy(
                src_ref=view(source),
                dst_ref=view(target),
                send_sem=send_sems.at[self.out_place],
                recv_sem=recv_sems.at[self.in_place],
                device_id=device,
                device_id_type=MESH,
            )

        def wait_recv(self):
            self.make().wait_recv()

        def wait_send(self):
            if not self.left:
                self.make().wait_send()
            self.left = True

    class Fetched:
        def __init__(self, source, target, group):
            self.parts = (source, target, place_of(2, group))

        def make(self):
            source, target, place = self.parts
            return pltpu.make_async_copy(view(source), view(target), local_sems.at[place])

        def wait(self):
            self.make().wait()

    def send(source, target, device, out_group=None, in_group=None):
        copy = Sent(source, target, device, out_group, in_group)
        copy.make().start()
        if out_group is None:
            sent.append(copy)
        return copy

    def wait_out(group, place):
        Sent(place, place, to_core, group, "").wait_send()

    def wait_in(group, place):
        Sent(place, place, to_core, "", group).wait_recv()

    def fetch(source, target, group=None):
        copy = Fetched(source, target, group)
        copy.make().start()
        return copy

    def wait_fetched(group, place):
        Fetched(place, place, group).wait()

    every = slice(None)

    barrier = pltpu.get_barrier_semaphore()
    for peer in head_peers:
        pl.semaphore_signal(barrier, inc=1, device_id={"head": peer}, device_id_type=MESH)
    for peer in dp_peers:
        pl.semaphore_signal(barrier, inc=1, device_id={"dp": peer}, device_id_type=MESH)

    def first_step(name, parts, at, cored, tail):
        if cored is None:
            return at
        slot = (at[0] % 2,) if at else ()
        rest = (every,) * 4 + tail
        copy = send((parts,) + at + (far_core,) + rest, (cored,) + slot + rest, to_core, name)
        yield
        copy.wait_recv()
        place = at + (core,)
        parts[place + rest] = add_low(parts[place + rest], cored[slot + rest])
        return place

    axes = (
        (bit2, far2, to2),
        (bit1, far1, to1),
        (bit0, far0, to0),
        (seq, far_seq, to_seq),
    )

    def chain(name, kind, order, parts, at, cored, land, final, tail=()):
        lead = yield from first_step(name, parts, at, cored, tail)
        place = [every] * 4
        for step, axis in enumerate(order):
            own, far, device = axes[axis]
            remaining = (every,) * (3 - step) if step < 3 else (every if axis == Y else 0,)
            target = (land[step],) + at + remaining + tail
            source = list(place)
            if axis != Y or step < 3:
                source[axis], place[axis] = far, own
            copy = send((parts,) + lead + tuple(source) + tail, target, device, name)
            yield
            copy.wait_recv()
            found = add_low(parts[lead + tuple(place) + tail], target[0][target[1:]])
            if step < 3:
                parts[lead + tuple(place) + tail] = found
            elif axis == Y:
                final[at + (core, every) + tail] = found
            else:
                final[at + (core, seq) + tail] = found
        if order[3] != Y:
            place = (final,) + at + (core, seq) + tail
            copy = send(place, place, to_seq, name)
            yield
            copy.wait_recv()
        place = (final,) + at + (core, every) + tail
        copy = send(place, place, to_core, (kind,))
        yield
        copy.wait_recv()

    def vector_sum(parts, by_owner, total, by_head, result):
        for peer in dp_peers:
            send((parts, peer), (by_owner, dp), {"dp": peer}, "owners", "owners")
        by_owner[dp] = parts[dp]
        yield
        wait_in("owners", (by_owner, slice(0, 7)))
        found = by_owner[0]
        for place in range(1, 8):
            found = found + by_owner[place]
        total[...] = found
        for peer in head_peers:
            send(total, (by_head, head), {"head": peer}, "heads_sum", "heads_sum")
        by_head[head] = found
        yield
        wait_in("heads_sum", (by_head, slice(0, 3)))
        result[...] = by_head[0] + by_head[1] + by_head[2] + by_head[3]

    class Chain:
        def __init__(self, name, steps, group=None):
            self.name, self.steps, self.group = name, steps, group
            self.taken, self.done = 0, False

        def step(self):
            with jax.named_scope(f"sum{self.name}_{self.taken}"):
                self.taken += 1
                if next(self.steps, self) is self:
                    self.done = True
                    if self.group:
                        kind, final, result, _ = self.group
                        left[kind] -= 1
                        if left[kind] == 0:
                            writes.append(fetch(final, result))

    chains, left, writes = {}, {}, []
    arrays = (
        (up_parts, up_core, up_land, up_final, up_hbm),
        (down_parts, down_core, down_land, down_final, down_hbm),
        (square_parts, square_core, square_land, square_final, square_hbm),
        (heads_parts, None, heads_land, heads_final, heads_hbm),
    )
    for name, (kind, part, side, order) in SUMS.items():
        at = () if kind == SQUARE_KIND else (part,)
        parts, cored, land, final, result = arrays[kind]
        tail = ()
        if side > 0:
            if kind == DOWN_KIND:
                tail = (slice(0, 32) if side == 1 else slice(32, 64),)
            else:
                tail = (every, slice(0, 256) if side == 1 else slice(256, parts.shape[-1]))
        steps = chain(name, kind, order, parts, at, cored, land, final, tail)
        whole_of = (parts,) + at + (every,) * (4 if cored is None else 5) + tail
        chains[name] = Chain(name, steps, (kind, final, result, whole_of))
        left[kind] = left.get(kind, 0) + 1
    chains[VECTORS] = Chain(
        VECTORS, vector_sum(vectors, vector_owners, vector_total, vector_heads, vectors_out)
    )

    def tick(point):
        for name in PLAN.get(point, ()):
            if name == OUT:
                out_sent.append(send((landed, 0), (out_hbm, seq), to_seq))
            else:
                chains[name].step()

    chunk = 32
    chunk_places = lax.broadcasted_iota(jnp.int32, (chunk, 1), 0)
    cot_sent, out_sent = [], []
    out_fetch = fetch(out_weight_hbm, out_weight)

    def fold(term):
        return jnp.sum(term.reshape(-1, 8, width), axis=0)

    def load(step):
        slot = step % 2
        for group in range(8):
            cols = pl.ds(group * half + step * 128, 128)
            into = pl.ds(group * 128, 128)
            fetch((up_weight_hbm, every, cols), (up_weight, slot, every, into), (step,))
            fetch((down_weight_hbm, cols), (down_weight, slot, into), (3 + step,))

    def front_phase(weight, tokens_own, bias):
        weight_fetch = fetch((weight_hbm, pl.ds(own_weight, 1152)), weight)
        own_fetch = fetch((tokens_in, seq), tokens_own)
        with jax.named_scope("barrier"):
            pl.semaphore_wait(barrier, 10)
        pieces = (slice(0, rows // 2), slice(rows // 2, rows))

        def send_piece(piece):
            return send((tokens_in, far_seq, piece), (landed, 0, piece), to_seq)

        came = [send_piece(pieces[0])]
        gain, shift = first_gain[...].reshape(1, width), first_shift[...].reshape(1, width)
        blank = jnp.zeros((1, HEAD), F32)
        for side in range(2):
            parts = []
            for place in range(side * 6 * HEAD, (side + 1) * 6 * HEAD, HEAD):
                parts.append(query_bias[place : place + HEAD].reshape(1, HEAD))
                parts.append(blank)
                parts.append(value_bias[place : place + HEAD].reshape(1, HEAD))
            bias[side] = jnp.concatenate(parts, axis=1)

        def local_chunk(order, step):
            return pl.ds(pl.multiple_of(flat_starts[order] + step * chunk, 32), chunk)

        def embed_passes(order):
            block = (seq, far_seq)[order]
            for step in range(rows // chunk):
                place = (block * 2 + core) * rows + step * chunk + chunk_places
                section = lax.rem(place, count)
                added = jnp.zeros((chunk, width), F32)
                for section_id in range(PASSES):
                    added = jnp.where(
                        section == section_id, table[section_id : section_id + 1, :], added
                    )
                embedded[local_chunk(order, step), :] = added

        def embed(source, order, piece):
            for step in range(piece.start // chunk, piece.stop // chunk):
                place = local_chunk(order, step)
                hidden = source[step * chunk : (step + 1) * chunk, :].astype(F32) + embedded[place, :]
                embedded[place, :] = hidden
                unit, _ = normalize(hidden)
                whole[pl.ds(pl.multiple_of(front_own[order] + step * chunk, 32), chunk), :] = (
                    unit * gain + shift
                ).astype(BF16)
            start = front_own[order] if piece.start == 0 else own_second
            place = (whole, pl.ds(start, piece.stop - piece.start))
            return send(place, place, to_core)

        def project(start, piece):
            span = pl.ds(
                pl.multiple_of(start + piece.start, 32), piece.stop - piece.start
            )
            packed[span, :] = (dot_nt(whole[span, :], weight[...]) + bias[core]).astype(BF16)

        with jax.named_scope("embed"):
            embed_passes(0)
            own_fetch.wait()
            copy = embed(tokens_own, 0, slice(0, rows))
            embed_passes(1)
        weight_fetch.wait()
        with jax.named_scope("packed"):
            project(front_own[0], slice(0, rows))
            came[0].wait_send()
            came.append(send_piece(pieces[1]))
            copy.wait_recv()
            project(front_far[0], slice(0, rows))
        load(0)
        load(1)
        for place, piece in enumerate(pieces):
            with jax.named_scope("tokens_in"):
                came[place].wait_recv()
                if place == 1:
                    came[1].wait_send()
                    cot_sent.append(send((cot_in, far_seq), (landed, 1), to_seq))
            with jax.named_scope("embed"):
                copy = embed(landed.at[0], 1, piece)
            with jax.named_scope("packed"):
                project(front_own[1], piece)
                copy.wait_recv()
                project(front_far[1], piece)

        visible = causal_block(BASE)
        queues, results, logs = {}, {}, {}

        def prepare(index):
            block = packed[:, index * 384 : (index + 1) * 384]
            for which in range(2):
                queries, keys, values = head_parts(block, which)
                values_ext = jnp.concatenate([values.T, jnp.ones((16, full), BF16)], axis=0)
                queues[index, which] = (queries, keys, values_ext)
                results[index, which], logs[index, which] = [], []

        def scores_of(place, start):
            queries, keys, _ = queues[place]
            scores = dot_nt(keys[: start + BASE], queries[start : start + BASE])
            last = jnp.where(visible, scores[start:], NEG_FILL)
            return last if start == 0 else jnp.concatenate([scores[:start], last], axis=0)

        def raise_of(scores):
            top = jnp.max(scores, axis=0, keepdims=True)
            return jnp.exp(scores - top).astype(BF16), top

        def gather_of(place, start, raised, top):
            grown = dot(queues[place][2][:, : start + BASE], raised)
            total = grown[HEAD : HEAD + 1]
            results[place].append(grown[:HEAD] / total)
            logs[place].append(top + jnp.log(total))
            index, which = place
            if start + BASE < full:
                return
            log_total[index, which : which + 1, :] = jnp.concatenate(logs[place], axis=1)
            if which == 0:
                return
            lanes = slice(index * 128, (index + 1) * 128)
            mixed[:, lanes] = jnp.concatenate(
                [jnp.concatenate(results[index, each], axis=1) for each in range(2)], axis=0
            ).T.astype(BF16)
            lanes_out = pl.ds(own_lanes[index], 128)
            for block in range(2):
                send(
                    (mixed, pl.ds(far_starts[block], rows), lanes),
                    (mixed_rows, slice(block * rows, (block + 1) * rows), lanes_out),
                    to_core,
                    "mixed",
                    "mixed",
                )

        with jax.named_scope("attend"):
            first = second = None
            for place in [(index, which) for index in range(3) for which in range(2)]:
                for start in range(0, full, BASE):
                    if place[1] == 0 and start == 0:
                        prepare(place[0])
                    scores = scores_of(place, start)
                    raised = raise_of(first[2]) if first else None
                    if second:
                        gather_of(*second)
                    second = first[:2] + raised if first else None
                    first = (place, start, scores)
            raised = raise_of(first[2])
            gather_of(*second)
            gather_of(*(first[:2] + raised))

    pl.run_scoped(
        front_phase,
        pltpu.VMEM((1152, width), BF16),
        pltpu.VMEM((rows, width), BF16),
        pltpu.VMEM((2, 1, 1152), F32),
    )

    def feed_phase(
        middle, normed, normed_t, out_grad, branch,
        active, up_grads,
    ):
        cot_fetch = fetch((cot_in, seq), (out_grad, pl.ds(flat_starts[0], rows)))

        gain, shift = second_gain[...].reshape(1, width), second_shift[...].reshape(1, width)
        out_fetch.wait()
        out_bias_row = out_bias[...].reshape(1, width)
        with jax.named_scope("project"):
            for block in range(2):
                span = slice(block * rows, (block + 1) * rows)
                own = mixed[pl.ds(own_starts[block], rows), :]
                mixed_rows[span, pl.ds(own_half, half)] = own
                middle[span, :] = (
                    embedded[span, :]
                    + dot(own, out_weight[pl.ds(own_half, half), :])
                    + out_bias_row
                )
        with jax.named_scope("mixed"):
            wait_in("mixed", (mixed_rows, every, slice(0, half)))
        with jax.named_scope("project"):
            for block in range(2):
                span = slice(block * rows, (block + 1) * rows)
                middle[span, :] += dot(
                    mixed_rows[span, pl.ds(far_half, half)], out_weight[pl.ds(far_half, half), :]
                )
                for step in range(rows // chunk):
                    first = block * rows + step * chunk
                    part = slice(first, first + chunk)
                    unit, _ = normalize(middle[part, :])
                    normed[part, :] = (unit * gain + shift).astype(BF16)
            normed_t[...] = normed[...].T
            vectors[...] = jnp.zeros_like(vectors)
        with jax.named_scope("out_grad"):
            cot_fetch.wait()
            cot_sent[0].wait_recv()
            for block in range(2):
                for step in range(rows // chunk):
                    part = slice(block * rows + step * chunk, block * rows + (step + 1) * chunk)
                    inside = slice(step * chunk, (step + 1) * chunk)
                    cot = jnp.where(
                        seq == block,
                        out_grad[part, :].astype(F32),
                        landed[1, inside, :].astype(F32),
                    )
                    place = (block * 2 + core) * rows + step * chunk + chunk_places
                    out_grad[part, :] = jnp.where(place < length, cot, 0.0).astype(BF16)
        for step in range(3):
            slot = step % 2
            wait_fetched((step,), (up_weight, slot))
            wait_fetched((3 + step,), (down_weight, slot))
            with jax.named_scope("hidden"):
                def block_of(place):
                    return slice(place * 256, (place + 1) * 256)

                def value_of(place):
                    bias = jnp.concatenate(
                        [
                            up_bias[
                                group * half + step * 128 : group * half + (step + 1) * 128
                            ].reshape(1, 128)
                            for group in (2 * place, 2 * place + 1)
                        ],
                        axis=1,
                    )
                    return dot(normed[...], up_weight[slot, :, block_of(place)]) + bias

                value = value_of(0)
                for place in range(4):
                    later = value_of(place + 1) if place < 3 else None
                    square_of = value * value
                    tanh = jnp.tanh(value * (TANH_IN + TANH_IN * TANH_CUBE * square_of))
                    gate = 0.5 + 0.5 * tanh
                    active[:, block_of(place)] = (value * gate).astype(BF16)
                    slope = gate * (
                        1.0
                        + (1.0 - gate)
                        * (value * (2.0 * TANH_IN + 6.0 * TANH_IN * TANH_CUBE * square_of))
                    )
                    up_grads[:, block_of(place)] = (
                        dot_nt(out_grad[...], down_weight[slot, block_of(place), :]) * slope
                    ).astype(BF16)
                    value = later
            tick(AT_HIDDEN_0 + 4 * step)

            with jax.named_scope("down_weight"):
                for quarter in range(4):
                    part = dot_tn(active[:, block_of(quarter)], out_grad[...])
                    for side in range(2):
                        down_parts[step, side, quarter // 2, quarter % 2] = (
                            part[:, side * half : (side + 1) * half]
                            .astype(BF16)
                            .reshape(2, 2, 64, half)
                        )
            tick(AT_DOWN_0 + 4 * step)
            with jax.named_scope("up_weight"):
                for side in range(2):
                    for upper in range(2):
                        up_parts[step, side, upper] = (
                            dot(
                                normed_t[upper * half : (upper + 1) * half, :],
                                up_grads[:, side * 512 : (side + 1) * 512],
                            )
                            .astype(BF16)
                            .reshape(2, 2, 2, 48, 512)
                        )
            tick(AT_UP_0 + 4 * step)
            with jax.named_scope("branch"):
                for place in range(3):
                    cols = block_of(place)
                    grown = dot(active[...], down_weight[slot, :, cols])
                    returned = dot_nt(up_grads[...], up_weight[slot, cols, :])
                    if step > 0:
                        grown, returned = grown + branch[:, cols], returned + middle_grad[:, cols]
                    branch[:, cols], middle_grad[:, cols] = grown, returned
                sums = col_sum(up_grads[...].astype(F32))
                for group in range(8):
                    vectors[group, 4 + step : 5 + step, :] = sums[:, group * 128 : (group + 1) * 128]
            if step == 0:
                load(2)
            tick(AT_BRANCH_0 + 4 * step)
        down_bias_row = down_bias[...].reshape(1, width)
        sums = [jnp.zeros((8, width), F32)] * 4
        with jax.named_scope("middle_grad"):
            for block in range(2):
                span = slice(block * rows, (block + 1) * rows)
                for step in range(rows // chunk):
                    first = block * rows + step * chunk
                    part = slice(first, first + chunk)
                    value = middle[part, :]
                    unit, scale = normalize(value)
                    inner = middle_grad[part, :]
                    scaled = inner * gain
                    cot = out_grad[part, :].astype(F32)
                    grad = cot + scale * (
                        scaled - row_mean(scaled) - unit * row_mean(scaled * unit)
                    )
                    middle_grad[part, :] = grad
                    low = grad.astype(BF16)
                    normed[part, :] = low
                    place = (block * 2 + core) * rows + step * chunk + chunk_places
                    landed[out_slots[block], step * chunk : (step + 1) * chunk, :] = jnp.where(
                        place < length, value + branch[part, :] + down_bias_row, 0.0
                    ).astype(BF16)
                    terms = (inner * unit, inner, low.astype(F32), cot)
                    sums = [have + fold(term) for have, term in zip(sums, terms)]
                mixed_grad_away[span, :] = dot_nt(
                    normed[span, :], out_weight[pl.ds(far_half, half), :]
                ).astype(BF16)
                send(
                    (mixed_grad_away, span),
                    (mixed_grad, pl.ds(own_starts[block], rows)),
                    to_core,
                    "mixed_grad",
                    "mixed_grad",
                )
        tick(AT_MIDDLE)
        with jax.named_scope("output_weight"):
            for block in range(2):
                span = slice(block * rows, (block + 1) * rows)
                mixed_grad[pl.ds(own_starts[block], rows), :] = dot_nt(
                    normed[span, :], out_weight[pl.ds(own_half, half), :]
                ).astype(BF16)
            for line, found in enumerate(sums):
                found = col_sum(found)
                for group in range(8):
                    vectors[group, line : line + 1, :96] = found[:, group * 96 : (group + 1) * 96]
            for upper in range(2):
                part = dot_tn(mixed_rows[:, upper * half : (upper + 1) * half], normed[...])
                for side in range(2):
                    square_parts[side, upper] = (
                        part[:, side * half : (side + 1) * half]
                        .astype(BF16)
                        .reshape(2, 2, 2, 48, half)
                    )
        tick(AT_SQUARED)

    pl.run_scoped(
        feed_phase,
        pltpu.VMEM((total_rows, width), F32),
        pltpu.VMEM((total_rows, width), BF16),
        pltpu.VMEM((width, total_rows), BF16),
        pltpu.VMEM((total_rows, width), BF16),
        pltpu.VMEM((total_rows, width), F32),
        pltpu.VMEM((total_rows, tile), BF16),
        pltpu.VMEM((total_rows, tile), BF16),
    )
    out_kept = fetch((landed, 1), (out_hbm, seq))

    def back_phase(
        weight, packed_grad, inner_kept, inner_away, value_key_sum, tokens_away
    ):
        weight_fetch = fetch((weight_hbm, pl.ds(own_weight, 1152)), weight)
        visible = causal_block(BASE)

        def prepare_heads(index):
            block = packed[:, index * 384 : (index + 1) * 384]
            found = []
            for which in range(2):
                queries, keys, values = head_parts(block, which)
                blank = jnp.zeros_like(queries)
                queries_ext = jnp.concatenate([queries, blank], axis=1)
                found.append((queries, keys, values, keys.T, queries_ext))
            return found

        def prepare_grads(index, heads):
            both_grad = mixed_grad[:, index * 128 : (index + 1) * 128]
            overlap = both_grad.astype(F32) * mixed[:, index * 128 : (index + 1) * 128].astype(F32)
            given = []
            for which in range(2):
                queries, keys, values, keys_t, queries_ext = heads[which]
                grad = both_grad[:, HEAD * which : HEAD * (which + 1)]
                delta = jnp.sum(
                    overlap[:, HEAD * which : HEAD * (which + 1)], axis=1, keepdims=True
                ).T
                logs = log_total[index][which : which + 1]
                grad_ext = jnp.concatenate([jnp.zeros_like(grad), grad], axis=1)
                given.append(
                    (queries, keys, values, grad, delta, logs, keys_t, grad_ext, queries_ext)
                )
            return given

        def attend(index, given):
            query_parts = ([], [])
            coming = None

            def begin(which, start):
                queries, keys, values, grad = given[which][:4]
                end = start + BASE
                return (
                    dot_nt(keys[:end], queries[start:end]),
                    dot_nt(values[:end], grad[start:end]),
                )

            def finish(which, start, scores, weight_grad):
                delta, logs, keys_t, grad_ext, queries_ext = given[which][4:]
                end = start + BASE
                span = slice(start, end)
                weights = jnp.exp(scores - logs[:, span])
                last = jnp.where(visible, weights[start:], 0.0)
                weights = (
                    last if start == 0 else jnp.concatenate([weights[:start], last], axis=0)
                )
                score_grad = (weights * (weight_grad - delta[:, span])).astype(BF16)
                added = dot(weights.astype(BF16), grad_ext[span]) + dot(
                    score_grad, queries_ext[span]
                )
                if start > 0:
                    value_key_sum[which, :start, :] += added[:start]
                value_key_sum[which, start:end, :] = added[start:]
                query_parts[which].append(dot(keys_t[:, :end], score_grad) * HEAD**-0.5)

            waiting = None
            for which in range(2):
                for start in range(0, full, BASE):
                    with jax.named_scope("attend"):
                        begun = begin(which, start)
                        if waiting:
                            finish(*waiting)
                        waiting = (which, start) + begun
                    if which == 1 and start == 2 * BASE and index < 2:
                        coming = prepare_grads(index + 1, prepare_heads(index + 1))
                    if which == 1 and start == 0:
                        tick((AT_HALF_PAIR_0, AT_HALF_PAIR_1, AT_HALF_PAIR_2)[index])
            with jax.named_scope("attend"):
                finish(*waiting)
                parts = []
                for which in range(2):
                    parts += [jnp.concatenate(query_parts[which], axis=1).T, value_key_sum[which]]
                low = jnp.concatenate(parts, axis=1).astype(BF16)
                packed_grad[:, index * 384 : (index + 1) * 384] = low
                sums = col_sum(low.astype(F32))
            for which in range(2):
                for line in range(2):
                    first = 192 * which + 128 * line
                    piece = sums[:, first : first + 64]
                    place = (index * 2 + which) * 64
                    while place < (index * 2 + which + 1) * 64:
                        group = place // 96
                        stop = min((group + 1) * 96, (index * 2 + which + 1) * 64)
                        offset = place - (index * 2 + which) * 64
                        vectors[
                            owner_base + group,
                            15 + line : 16 + line,
                            place - group * 96 : stop - group * 96,
                        ] = piece[:, offset : offset + stop - place]
                        place = stop
            tick((AT_PAIR_0, AT_PAIR_1, AT_PAIR_2)[index])
            return coming

        def heads_weight(index):
            with jax.named_scope("heads_weight"):
                heads_parts[index] = (
                    dot_tn(whole[...], packed_grad[:, index * 384 : (index + 1) * 384])
                    .astype(BF16)
                    .reshape(2, 2, 2, 2, 48, half)
                )
            tick((AT_HEADS_WEIGHT_0, AT_HEADS_WEIGHT_1, AT_HEADS_WEIGHT_2)[index])

        with jax.named_scope("prepare"):
            first_heads = prepare_heads(0)
        with jax.named_scope("mixed_grad"):
            wait_in("mixed_grad", mixed_grad_away)
        with jax.named_scope("prepare"):
            given = prepare_grads(0, first_heads)
        for index in range(3):
            given = attend(index, given)
            if index < 2:
                heads_weight(index)
        weight_fetch.wait()
        gain = first_gain[...].reshape(1, width)
        found = [jnp.zeros((8, width), F32)] * (2 + PASSES)
        copies, tokens_sent = [], []

        def inner_of(order):
            with jax.named_scope("inner"):
                inner_away[order] = dot(
                    packed_grad[pl.ds(late_far[order], rows), :], weight[...]
                ).astype(BF16)
                copies.append(send(
                    (inner_away, order),
                    (mixed_rows, slice(order * rows, (order + 1) * rows)),
                    to_core,
                ))
                inner_kept[order] = dot(packed_grad[pl.ds(late_own[order], rows), :], weight[...])
            tick((AT_INNER_0, AT_INNER_1)[order])

        def input_of(order):
            with jax.named_scope("inner_came"):
                copies[order].wait_recv()
            with jax.named_scope("input"):
                for step in range(rows // chunk):
                    inside = slice(step * chunk, (step + 1) * chunk)
                    part = pl.ds(pl.multiple_of(late_spans[order] + step * chunk, 32), chunk)
                    unit, scale = normalize(embedded[part, :])
                    inner = inner_kept[order, inside, :] + mixed_rows[
                        order * rows + step * chunk : order * rows + (step + 1) * chunk, :
                    ].astype(F32)
                    scaled = inner * gain
                    grad = middle_grad[part, :] + scale * (
                        scaled - row_mean(scaled) - unit * row_mean(scaled * unit)
                    )
                    middle_grad[part, :] = grad
                    found[0] += fold(inner * unit)
                    found[1] += fold(inner)
                    if order == 0:
                        tokens_away[inside, :] = grad.astype(BF16)
                        if step % 5 == 4:
                            piece = slice((step - 4) * chunk, (step + 1) * chunk)
                            tokens_sent.append(
                                send((tokens_away, piece), (tokens_came_hbm, piece), to_seq)
                            )

        def sections_of(order):
            with jax.named_scope("sections"):
                for step in range(rows // chunk):
                    part = pl.ds(pl.multiple_of(late_spans[order] + step * chunk, 32), chunk)
                    grad = middle_grad[part, :]
                    place = (late_blocks[order] * 2 + core) * rows + step * chunk + chunk_places
                    section = lax.rem(place, count)
                    for section_id in range(PASSES):
                        found[2 + section_id] += fold(jnp.where(section == section_id, grad, 0.0))

        inner_of(0)
        heads_weight(2)
        input_of(0)
        tick(AT_INPUT_0)
        inner_of(1)
        sections_of(0)
        input_of(1)
        tokens_kept = fetch((middle_grad, pl.ds(late_spans[1], rows)), tokens_kept_hbm)
        sections_of(1)
        for line, value in enumerate(found):
            value = col_sum(value)
            for group in range(8):
                vectors[group, 8 + line : 9 + line, :96] = value[:, group * 96 : (group + 1) * 96]
        tick(AT_INPUT_1)
        for name in ENDING:
            chains[name].step()
        for each in chains.values():
            while not each.done:
                each.step()
        with jax.named_scope("ends"):
            for copy in tokens_sent:
                copy.wait_recv()
            out_sent[0].wait_recv()
            tokens_kept.wait()
            out_kept.wait()
            for copy in sent:
                copy.wait_send()
            wait_out("mixed", (mixed_rows, every, slice(0, half)))
            wait_out("mixed_grad", mixed_grad_away)
            wait_out("owners", (vector_owners, slice(0, 7)))
            wait_out("heads_sum", (vector_heads, slice(0, 3)))
            finals = {}
            for name, each in chains.items():
                if each.group:
                    finals[each.group[0]] = each.group[1]
                    wait_out(name, each.group[3])
            for kind, final in finals.items():
                lead = (core,) if kind == SQUARE_KIND else (every, core)
                wait_out((kind,), (final,) + lead)
            for copy in writes:
                copy.wait()

    pl.run_scoped(
        back_phase,
        pltpu.VMEM((1152, width), BF16),
        pltpu.VMEM((full, 1152), BF16),
        pltpu.VMEM((2, rows, width), F32),
        pltpu.VMEM((2, rows, width), BF16),
        pltpu.VMEM((2, full, 2 * HEAD), F32),
        pltpu.VMEM((rows, width), BF16),
    )


def swap(value, axis, bit):
    count = lax.axis_size(axis)
    return lax.ppermute(value, axis, [(place, place ^ bit) for place in range(count)])


def call(kernel, out_shapes, args, scratch=(), flops=0, moved=0):
    specs = [pl.BlockSpec(memory_space=pltpu.SMEM)] + [
        pl.BlockSpec(memory_space=pltpu.VMEM) for _ in args[1:]
    ]
    return pl.pallas_call(
        kernel,
        out_shape=tuple(jax.ShapeDtypeStruct(*item) for item in out_shapes),
        in_specs=specs,
        scratch_shapes=[pltpu.VMEM(*item) for item in scratch],
        compiler_params=pltpu.CompilerParams(vmem_limit_bytes=VMEM_LIMIT),
        cost_estimate=pl.CostEstimate(flops=flops, bytes_accessed=moved, transcendentals=0),
    )(*args)


def finish_kernel(
    tokens_kept, tokens_came, out, up_final, down_final, square_final, heads_final, vectors,
    out_result, tokens_result, first_gain, first_shift, heads, query_bias, value_bias, square,
    out_bias, second_gain, second_shift, up, up_bias, down, down_bias, table,
    came_low, up_low, down_low, square_low, heads_low, out_low, kept_wide,
    came_wide, up_wide, down_wide, square_wide, heads_wide, sems,
):
    seq = lax.axis_index("head") // 2
    pairs = [
        (up_final, up_low),
        (down_final, down_low),
        (tokens_came, came_low),
        (heads_final, heads_low),
        (square_final, square_low),
        (out, out_low),
        (tokens_kept, kept_wide),
        (out_low, out_result),
        (kept_wide, tokens_result.at[seq]),
        (up_wide, up),
        (down_wide, down),
        (came_wide, tokens_result.at[1 - seq]),
        (heads_wide, heads),
        (square_wide, square),
    ]
    copies = [
        pltpu.make_async_copy(source, target, sems.at[place])
        for place, (source, target) in enumerate(pairs)
    ]
    for copy in copies[:7]:
        copy.start()
    copies[0].wait()
    for side in range(2):
        for step in range(3):
            for group in range(4):
                first = (side * 4 + group) * 384 + step * 128
                for part in range(2):
                    up_wide[part * 48 : (part + 1) * 48, first : first + 128] = up_low[
                        step, side, part, :, group * 128 : (group + 1) * 128
                    ].astype(F32)
    copies[9].start()
    copies[1].wait()
    for side in range(2):
        for step in range(3):
            for part in range(2):
                first = step * 128 + part * 64
                down_wide[first : first + 64, side * 384 : (side + 1) * 384] = down_low[
                    step, side, part
                ].astype(F32)
    copies[10].start()
    copies[2].wait()
    came_wide[...] = came_low[...].astype(F32)
    copies[11].start()
    copies[3].wait()
    for side in range(2):
        for part in range(2):
            for index in range(3):
                for which in range(2):
                    heads_wide[
                        side * 6 + index * 2 + which, part * 48 : (part + 1) * 48, :
                    ] = heads_low[
                        index, side, part, :, which * 192 : (which + 1) * 192
                    ].astype(F32)
    copies[12].start()
    copies[4].wait()
    for side in range(2):
        for part in range(2):
            square_wide[part * 48 : (part + 1) * 48, side * 384 : (side + 1) * 384] = square_low[
                side, part
            ].astype(F32)
    copies[13].start()
    for place in (5, 6):
        copies[place].wait()
        copies[place + 2].start()
    second_gain[...] = vectors[0, :96]
    second_shift[...] = vectors[1, :96]
    out_bias[...] = vectors[2, :96]
    down_bias[...] = vectors[3, :96]
    up_bias[...] = jnp.concatenate(
        [vectors[4:5, :], vectors[5:6, :], vectors[6:7, :]], axis=1
    ).reshape(384)
    first_gain[...] = vectors[8, :96]
    first_shift[...] = vectors[9, :96]
    table[...] = vectors[10:15, :96]
    query_bias[...] = vectors[15, :96]
    value_bias[...] = vectors[16, :96]
    for copy in copies[7:]:
        copy.wait()


def fused_layer(
    tokens, passes, first_gain, first_shift, heads_weight, query_bias, value_bias, output_weight,
    output_bias, second_gain, second_shift, up_weight, up_bias, down_weight, down_bias,
    pass_embed, cotangent,
):
    rows, width, half, full = 320, 768, 384, 1280
    weight_t = heads_weight.transpose(1, 2, 0).reshape(3 * width, width)

    def lands(lead, count, wide):
        return (
            pltpu.VMEM(lead + (2, 2, 2, count, wide), BF16),
            pltpu.VMEM(lead + (2, 2, count, wide), BF16),
            pltpu.VMEM(lead + (2, count, wide), BF16),
            pltpu.VMEM(lead + (2, count, wide), BF16),
        )

    def sums(lines):
        return (
            pltpu.VMEM((8, lines, 128), F32),
            pltpu.VMEM((8, lines, 128), F32),
            pltpu.VMEM((lines, 128), F32),
            pltpu.VMEM((4, lines, 128), F32),
        )

    scratch = (
        pltpu.VMEM((2, rows, width), BF16),
        pltpu.VMEM((2 * rows, width), F32),
        pltpu.VMEM((width, width), BF16),
        pltpu.VMEM((2, width, 1024), BF16),
        pltpu.VMEM((2, 1024, width), BF16),
        pltpu.VMEM((full, width), BF16),
        pltpu.VMEM((full, 3 * half), BF16),
        pltpu.VMEM((full, half), BF16),
        pltpu.VMEM((2 * rows, width), BF16),
        pltpu.VMEM((3, 2, full), F32),
        pltpu.VMEM((2 * rows, width), F32),
        pltpu.VMEM((full, half), BF16),
        pltpu.VMEM((2 * rows, half), BF16),
        pltpu.VMEM((3, 2, 2, 2, 2, 2, 48, 512), BF16),
        pltpu.VMEM((2, 2, 2, 2, 2, 48, 512), BF16),
        lands((3,), 48, 512),
        pltpu.VMEM((3, 2, 2, 2, 2, 2, 64, half), BF16),
        pltpu.VMEM((2, 2, 2, 2, 2, 64, half), BF16),
        lands((3,), 64, half),
        pltpu.VMEM((2, 2, 2, 2, 2, 48, half), BF16),
        pltpu.VMEM((2, 2, 2, 2, 48, half), BF16),
        lands((), 48, half),
        pltpu.VMEM((3, 2, 2, 2, 2, 48, half), BF16),
        lands((3,), 48, half),
        pltpu.VMEM((3, 2, 2, 48, 512), BF16),
        pltpu.VMEM((3, 2, 2, 64, half), BF16),
        pltpu.VMEM((2, 2, 48, half), BF16),
        pltpu.VMEM((3, 2, 2, 48, half), BF16),
        *sums(24),
        pltpu.SemaphoreType.DMA((SENDS,)),
        pltpu.SemaphoreType.DMA((RECEIVES,)),
        pltpu.SemaphoreType.DMA((FETCHES,)),
    )
    any_space = pl.BlockSpec(memory_space=pl.ANY)
    vmem = pl.BlockSpec(memory_space=pltpu.VMEM)

    def shapes(*items):
        return tuple(jax.ShapeDtypeStruct(*item) for item in items)

    found = pl.pallas_call(
        main_kernel,
        out_shape=shapes(
            ((2, rows, width), BF16),
            ((rows, width), F32),
            ((rows, width), BF16),
            ((3, 2, 2, 48, 512), BF16),
            ((3, 2, 2, 64, half), BF16),
            ((2, 2, 48, half), BF16),
            ((3, 2, 2, 48, half), BF16),
            ((24, 128), F32),
        ),
        in_specs=[pl.BlockSpec(memory_space=pltpu.SMEM)] + [vmem] * 10 + [any_space] * 6,
        out_specs=(any_space,) * 7 + (vmem,),
        scratch_shapes=scratch,
        compiler_params=pltpu.CompilerParams(
            vmem_limit_bytes=64 * 2**20, collective_id=0, has_side_effects=True
        ),
    )(
        passes, first_gain, first_shift, query_bias, value_bias, output_bias, second_gain,
        second_shift, up_bias, down_bias, pass_embed, tokens, cotangent, weight_t, output_weight,
        up_weight, down_weight,
    )
    out, tokens_kept, tokens_came, up, down, square, heads, vectors = found
    wide = (any_space, any_space, vmem, vmem, any_space, vmem, vmem, any_space)
    results = pl.pallas_call(
        finish_kernel,
        out_shape=shapes(
            ((2, rows, width), BF16),
            ((2, rows, width), F32),
            ((96,), F32),
            ((96,), F32),
            ((HEADS, 96, 192), F32),
            ((96,), F32),
            ((96,), F32),
            ((96, width), F32),
            ((96,), F32),
            ((96,), F32),
            ((96,), F32),
            ((96, 3072), F32),
            ((384,), F32),
            ((384, width), F32),
            ((96,), F32),
            ((PASSES, 96), F32),
        ),
        in_specs=[any_space] * 7 + [vmem],
        out_specs=wide + (vmem, vmem, vmem, any_space, vmem, any_space, vmem, vmem),
        scratch_shapes=[
            pltpu.VMEM((rows, width), BF16),
            pltpu.VMEM((3, 2, 2, 48, 512), BF16),
            pltpu.VMEM((3, 2, 2, 64, half), BF16),
            pltpu.VMEM((2, 2, 48, half), BF16),
            pltpu.VMEM((3, 2, 2, 48, half), BF16),
            pltpu.VMEM((2, rows, width), BF16),
            pltpu.VMEM((rows, width), F32),
            pltpu.VMEM((rows, width), F32),
            pltpu.VMEM((96, 3072), F32),
            pltpu.VMEM((384, width), F32),
            pltpu.VMEM((96, width), F32),
            pltpu.VMEM((HEADS, 96, 192), F32),
            pltpu.SemaphoreType.DMA((14,)),
        ],
        compiler_params=pltpu.CompilerParams(vmem_limit_bytes=VMEM_LIMIT),
    )(tokens_kept, tokens_came, out, up, down, square, heads, vectors)
    return results[:4] + (results[4].transpose(1, 0, 2),) + results[5:]


def both(left, right):
    return (left.astype(F32) + right.astype(F32)).astype(BF16)


def halve(value, axis, bit):
    mine = (lax.axis_index(axis) // bit) % 2
    pairs = value.reshape((value.shape[0] // 2, 2) + value.shape[1:])
    kept = lax.dynamic_index_in_dim(pairs, mine, 1, keepdims=False)
    away = lax.dynamic_index_in_dim(pairs, 1 - mine, 1, keepdims=False)
    return both(kept, swap(away, axis, bit))


def over_owners(value):
    bit = 1
    while bit < lax.axis_size("dp"):
        value = halve(value, "dp", bit)
        bit *= 2
    return value[0]


def total_share(value):
    count = value.shape[1] // 2
    seq = lax.axis_index("head") // 2
    first = over_owners(value[:, :count])
    first = both(first, swap(first, "head", 2))
    second = jnp.swapaxes(value[:, count:].reshape(value.shape[0], 2, -1, value.shape[2]), 0, 1)
    kept = lax.dynamic_index_in_dim(second, seq, 0, keepdims=False)
    away = lax.dynamic_index_in_dim(second, 1 - seq, 0, keepdims=False)
    second = over_owners(both(kept, swap(away, "head", 2)))
    other = swap(second, "head", 2)
    low_part = jnp.where(seq == 0, second, other)
    high_part = jnp.where(seq == 0, other, second)
    return jnp.concatenate([first, low_part, high_part], axis=0)


def on_device(
    tokens,
    passes,
    first_gain,
    first_shift,
    heads_weight,
    query_bias,
    value_bias,
    output_weight,
    output_bias,
    second_gain,
    second_shift,
    upward_weight,
    upward_bias,
    downward_weight,
    downward_bias,
    pass_embed,
    cotangent,
):
    owners = lax.axis_size("dp")
    _, rows, width = tokens.shape
    hidden = upward_weight.shape[1]
    half = width // 2
    full = 4 * rows
    if owners == 8 and (rows, width, hidden) == (320, 768, 3072):
        return fused_layer(
            tokens, passes, first_gain, first_shift, heads_weight, query_bias, value_bias,
            output_weight, output_bias, second_gain, second_shift, upward_weight, upward_bias,
            downward_weight, downward_bias, pass_embed, cotangent,
        )
    place = lax.axis_index("head")
    core, seq = place % 2, place // 2
    count = lax.dynamic_index_in_dim(passes, seq, 0, keepdims=False)
    scalars = jnp.stack([core, seq, count]).astype(jnp.int32)

    def pick(array, index, axis=0):
        return lax.dynamic_index_in_dim(array, index, axis, keepdims=False)

    tokens_came = swap(pick(tokens, 1 - seq), "head", 2)
    cot_came = swap(pick(cotangent, 1 - seq), "head", 2)
    row = lambda vector: vector.reshape(1, -1)
    weight_t = heads_weight.transpose(1, 2, 0).reshape(2, 3 * half, width)
    weight_own = pick(weight_t, core)
    bias_table = jnp.concatenate(
        [
            query_bias.reshape(HEADS, HEAD),
            jnp.zeros((HEADS, HEAD), F32),
            value_bias.reshape(HEADS, HEAD),
        ],
        axis=1,
    ).reshape(2, 1, 3 * half)
    bias_own = pick(bias_table, core)

    embedded, normed = call(
        embed_kernel,
        [((2 * rows, width), F32), ((2 * rows, width), BF16)],
        (
            scalars,
            pick(tokens, seq),
            tokens_came,
            pass_embed,
            row(first_gain),
            row(first_shift),
        ),
        moved=10 * 2**20,
    )
    normed_came = swap(normed, "head", 1)
    whole, packed, mixed, mixed_kept, mixed_away, log_total = call(
        forward_kernel,
        [
            ((full, width), BF16),
            ((full, 3 * half), BF16),
            ((full, half), BF16),
            ((2 * rows, half), BF16),
            ((2 * rows, half), BF16),
            ((HEADS // 4, 2, full), F32),
        ],
        (scalars, normed, normed_came, weight_own, bias_own),
        moved=70 * 2**20,
    )
    mixed_came = swap(mixed_away, "head", 1)
    up_rows, down_rows = width // owners, hidden // owners
    out_kept, out_away, middle_grad, mg_kept, mg_away, grads, row_sums, up_sums = call(
        feed_kernel,
        [
            ((rows, width), BF16),
            ((rows, width), BF16),
            ((2 * rows, width), F32),
            ((2 * rows, half), BF16),
            ((2 * rows, half), BF16),
            ((2, owners, 5 * up_rows + down_rows, half), BF16),
            ((8, width), F32),
            ((1, hidden), F32),
        ],
        (
            scalars,
            mixed_kept,
            mixed_came,
            embedded,
            pick(cotangent, seq),
            cot_came,
            output_weight,
            row(output_bias),
            row(second_gain),
            row(second_shift),
            upward_weight,
            row(upward_bias),
            downward_weight,
            row(downward_bias),
        ),
        scratch=[
            ((2 * rows, width), BF16),
            ((2 * rows, width), F32),
            ((2 * rows, width), BF16),
            ((width, 2 * rows), BF16),
            ((2 * rows, width), BF16),
            ((2 * rows, width), F32),
            ((2 * rows, width), F32),
        ],
        moved=120 * 2**20,
    )
    mg_came = swap(mg_away, "head", 1)
    out_came = swap(out_away, "head", 2)
    share = both(pick(grads, core), swap(pick(grads, 1 - core), "head", 1))
    inner_kept, inner_away, heads_grad, bias_sums = call(
        backward_kernel,
        [
            ((2 * rows, width), F32),
            ((2 * rows, width), BF16),
            ((owners, 3 * up_rows, half), BF16),
            ((1, 3 * half), F32),
        ],
        (
            scalars,
            packed,
            log_total,
            mixed_kept,
            mixed_away,
            mg_kept,
            mg_came,
            whole,
            weight_own,
        ),
        scratch=[
            ((full, half), BF16),
            ((full, half), BF16),
            ((full, 3 * half), BF16),
            ((full, width), F32),
            ((2, full, 2 * HEAD), F32),
        ],
        moved=100 * 2**20,
    )
    inner_came = swap(inner_away, "head", 1)
    grad_kept, grad_away, sums = call(
        input_kernel,
        [((rows, width), F32), ((rows, width), BF16), ((8, width), F32)],
        (scalars, inner_kept, inner_came, embedded, middle_grad, row(first_gain)),
        moved=10 * 2**20,
    )
    grad_came = swap(grad_away, "head", 2).astype(F32)

    def place_rows(kept, came):
        return jnp.stack([jnp.where(seq == 0, kept, came), jnp.where(seq == 0, came, kept)])

    bias_parts = jnp.where(
        (jnp.arange(2) == core)[:, None], bias_sums, 0.0
    ).reshape(HEADS, 3, HEAD)
    vectors = jnp.concatenate(
        [
            sums[:7],
            row_sums[:4],
            bias_parts[:, 0].reshape(1, width),
            bias_parts[:, 2].reshape(1, width),
            up_sums.reshape(-1, width // owners, owners).reshape(-1, width),
        ],
        axis=0,
    )
    vectors = lax.psum(vectors, ("dp", "head"))
    owner = lax.axis_index("dp")
    mine = lax.dynamic_slice_in_dim(vectors[:13], owner * up_rows, up_rows, 1)
    up_mine = lax.dynamic_slice_in_dim(vectors[13:].reshape(-1), owner * down_rows, down_rows, 0)

    share = total_share(share)
    share = jnp.stack([share, swap(share, "head", 1)])
    heads_share = total_share(heads_grad)
    heads_share = jnp.stack([heads_share, swap(heads_share, "head", 1)])
    share = jnp.where(core == 0, share, share[::-1]).astype(F32)
    heads_share = jnp.where(core == 0, heads_share, heads_share[::-1]).astype(F32)
    up_share = share[:, : 4 * up_rows].reshape(8, up_rows, half)
    up_share = up_share.transpose(1, 0, 2).reshape(up_rows, hidden)
    down_share = share[:, 4 * up_rows : 4 * up_rows + down_rows]
    down_share = down_share.transpose(1, 0, 2).reshape(down_rows, width)
    out_share = share[:, 4 * up_rows + down_rows :].transpose(1, 0, 2).reshape(up_rows, width)
    heads_share = heads_share.reshape(6, up_rows, half).transpose(1, 0, 2)
    heads_share = heads_share.reshape(up_rows, HEADS, 3 * HEAD)
    return (
        place_rows(out_kept, out_came),
        place_rows(grad_kept, grad_came),
        mine[0],
        mine[1],
        heads_share,
        mine[11],
        mine[12],
        out_share,
        mine[9],
        mine[7],
        mine[8],
        up_share,
        up_mine,
        down_share,
        mine[10],
        mine[2:7],
    )


def solution(mesh):
    rows_spec = P("dp", "head", None)
    in_specs = (rows_spec, P("dp")) + (P(),) * 14 + (rows_spec,)
    out_specs = (
        rows_spec,
        rows_spec,
        P("dp"),
        P("dp"),
        P("dp", None, None),
        P("dp"),
        P("dp"),
        P("dp", None),
        P("dp"),
        P("dp"),
        P("dp"),
        P("dp", None),
        P("dp"),
        P("dp", None),
        P("dp"),
        P(None, "dp"),
    )
    return jax.shard_map(
        on_device, mesh=mesh, in_specs=in_specs, out_specs=out_specs, check_vma=False
    )
```
